128 devices in a mesh: reader: 8 (over x_hi, y), blk: 16 (over z, x_lo, core).
Axes of the slice: x: 4 (x_hi: 2, x_lo: 2; x = x_hi * 2 + x_lo), y: 4, z: 4, core: 2. Of those that a mesh axis runs over, the one named last changes fastest.
Arguments:
- features: bfloat16 [16384, 512], P(('reader', 'blk')), may hold values from -40 to 40
- cotangent: bfloat16 [16384, 512], P(('reader', 'blk')), may hold values from -6 to 6
- w_query: bfloat16 [512, 512], replicated, may hold values from -0.25 to 0.25
- w_key: bfloat16 [512, 512], replicated, may hold values from -0.25 to 0.25
- w_value: bfloat16 [512, 512], replicated, may hold values from -0.25 to 0.25
- tile_coords: int32 [8, 16, 32, 3], P('reader', 'blk'), may hold values from 0 to 239, as said below
- tile_count: int32 [8, 16], P('reader', 'blk'), may hold values from 4 to 32, as said below
- mask_table: int32 [240, 128, 4], replicated, may hold values from -2147483648 to 2147483647, as said below
Outputs:
- attn_out: bfloat16 [16384, 512], P(('reader', 'blk'))
- grad_features: bfloat16 [16384, 512], P(('reader', 'blk'))
The draws below stay inside these ranges and needn't reach their ends.
Inputs may be any that keep to these rules, and one draw needn't show every extreme that they name: `tile_coords`: for every r and b the 32 slots name distinct (qb, kb) pairs with qb < 16, kb < 8, p < 240; the first 1 slots are the tiles in which the nodes of segment r * 16 + b meet themselves. `tile_count`: some pair (r, b) uses all 32 slots, and some pair uses the fewest. `mask_table`: each word packs 32 edge bits as a signed int32; each bit is set with probability 1/32.
All inputs are finite; a program needn't handle non-finite values.
Results may differ from the reference program's by a relative error of at most 0.01265.
The reference program's roundings to bfloat16 on the way count: a program that leaves them out, or rounds other values in their place, can miss the bound.
Values may be sent and summed in bfloat16 or wider, within the bound.
A program may use at most 128 MiB of HBM per device.

```python
import jax
import jax.numpy as jnp
from jax import lax

D = 512
HEADS = 8
BLOCK = 128
PATTERNS = 240
NODE_DEV = 128
NODES = 16384
SEG_BLOCKS = 1
QBLK = 16
KBLK = 8
CAP = 32
N_READER = 8
N_BLK = 16


def draw_features(key, part):
    key_base = jax.random.fold_in(key, 0)
    base = jax.random.normal(key_base, (NODES, D), jnp.float32)
    return jnp.clip(base, -40.0, 40.0).astype(jnp.bfloat16)


def draw_tile_coords(key, part):
    key_order, key_pattern = jax.random.split(key)
    pair_count = QBLK * KBLK
    device_keys = jax.random.split(key_order, N_READER * N_BLK)
    pair_ranks = jax.vmap(lambda one: jax.random.permutation(one, pair_count))(device_keys)
    pair_ranks = pair_ranks.reshape(N_READER, N_BLK, pair_count).astype(jnp.int32)
    pair_ids = jnp.arange(pair_count, dtype=jnp.int32)[None, None, :]
    query_blk = pair_ids // KBLK
    key_blk = pair_ids % KBLK
    reader_ids = jnp.arange(N_READER, dtype=jnp.int32)[:, None, None]
    blk_ids = jnp.arange(N_BLK, dtype=jnp.int32)[None, :, None]
    on_diag = (query_blk // SEG_BLOCKS == blk_ids) & (key_blk // SEG_BLOCKS == reader_ids) & (query_blk % SEG_BLOCKS == key_blk % SEG_BLOCKS)
    ordered = jnp.argsort(pair_ranks - pair_count * on_diag.astype(jnp.int32), axis=-1)[..., :CAP].astype(jnp.int32)
    patterns = jax.random.randint(key_pattern, (N_READER, N_BLK, CAP), 0, PATTERNS, dtype=jnp.int32)
    return jnp.stack([ordered // KBLK, ordered % KBLK, patterns], axis=-1).astype(jnp.int32)


def draw_tile_count(key, part):
    key_draw, key_place = jax.random.split(key)
    floor_count = max(SEG_BLOCKS, CAP // 8)
    drawn = jax.random.randint(key_draw, (N_READER * N_BLK,), floor_count, CAP // 2 + 1, dtype=jnp.int32)
    counts = jnp.maximum(floor_count, drawn)
    order_ids = jax.random.permutation(key_place, N_READER * N_BLK)
    counts = counts.at[order_ids[0]].set(CAP).at[order_ids[1]].set(floor_count)
    return counts.reshape(N_READER, N_BLK).astype(jnp.int32)


def draw_mask_table(key, part):
    word_keys = jax.random.split(key, 5)
    shape = (PATTERNS, BLOCK, BLOCK // 32)
    words = jax.random.randint(word_keys[0], shape, -2147483648, 2147483647, dtype=jnp.int32)
    for index in range(1, 5):
        words = words & jax.random.randint(word_keys[index], shape, -2147483648, 2147483647, dtype=jnp.int32)
    return words


def steps_of(key, shape, pieces, low, largest):
    loudness = 1.0
    for axis_at, shards_of in pieces:
        draws = jax.random.uniform(jax.random.fold_in(jax.random.fold_in(key, 6), axis_at), (shards_of,), jnp.float32, low / len(pieces), largest / len(pieces))
        loudness = loudness * jnp.repeat(jnp.exp(draws), shape[axis_at] // shards_of).reshape((-1,) + (1,) * (len(shape) - 1 - axis_at))
    return loudness


def scatter_about(key, shape, scale, limit, pieces=(), kind=jnp.bfloat16):
    entries = scale * jax.random.normal(key, shape, jnp.float32)
    if pieces:
        entries = entries * steps_of(key, shape, pieces, -0.22, 0.18)
    return jnp.clip(entries, -limit, limit).astype(kind)


def setup_inputs(seed: int = 0) -> dict:
    keys = jax.random.split(jax.random.key(seed), 9)
    return {
        "features": draw_features(jax.random.fold_in(keys[8], 71), 0),
        "cotangent": scatter_about(keys[1], (NODES, D), 1.0, 6.0, ((0, 128),)),
        "w_query": scatter_about(keys[2], (D, D), D ** -0.5, 0.25),
        "w_key": scatter_about(keys[3], (D, D), D ** -0.5, 0.25),
        "w_value": scatter_about(keys[4], (D, D), D ** -0.5, 0.25),
        "tile_coords": draw_tile_coords(jax.random.fold_in(keys[8], 71), 0),
        "tile_count": draw_tile_count(jax.random.fold_in(keys[8], 71), 0),
        "mask_table": draw_mask_table(jax.random.fold_in(keys[8], 71), 0),
    }


NEG_FILL = -1.0e30


def unpack(mask_words):
    shifts = jnp.arange(32, dtype=jnp.int32)
    mask_bits = jnp.right_shift(mask_words[..., None], shifts) & 1
    return mask_bits.reshape(mask_words.shape[:-1] + (mask_words.shape[-1] * 32,)) > 0


def project(rows, weight):
    return jnp.dot(rows, weight, preferred_element_type=jnp.float32).astype(jnp.bfloat16)


def key_layout(node_rows):
    moved = node_rows.reshape(N_READER, N_BLK, NODE_DEV, D).transpose(1, 0, 2, 3)
    return moved.reshape(N_BLK * KBLK, BLOCK, HEADS, D // HEADS)


def node_layout(key_tiles):
    moved = key_tiles.reshape(N_BLK, N_READER, NODE_DEV, D).transpose(1, 0, 2, 3)
    return moved.reshape(NODES, D)


def rounded_low(values_in):
    return lax.optimization_barrier(values_in.astype(jnp.bfloat16)).astype(jnp.float32)


def reference(features, cotangent, w_query, w_key, w_value, tile_coords, tile_count, mask_table):
    head_dim = D // HEADS
    scale = float(head_dim) ** -0.5
    tile_batch = 32
    query_tiles = project(features, w_query).reshape(N_READER * QBLK, BLOCK, HEADS, head_dim).astype(jnp.float32)
    key_tiles = key_layout(project(features, w_key)).astype(jnp.float32)
    value_tiles = key_layout(project(features, w_value)).astype(jnp.float32)
    grad_tiles = cotangent.reshape(N_READER * QBLK, BLOCK, HEADS, head_dim).astype(jnp.float32)
    reader_ids = jnp.arange(N_READER, dtype=jnp.int32)[:, None, None]
    blk_ids = jnp.arange(N_BLK, dtype=jnp.int32)[None, :, None]
    slot_ids = jnp.arange(CAP, dtype=jnp.int32)[None, None, :]
    query_blk = tile_coords[..., 0].astype(jnp.int32)
    key_blk = tile_coords[..., 1].astype(jnp.int32)
    usable = slot_ids < tile_count[:, :, None]
    on_diag = (query_blk // SEG_BLOCKS == blk_ids) & (key_blk // SEG_BLOCKS == reader_ids) & (query_blk % SEG_BLOCKS == key_blk % SEG_BLOCKS)
    global_query = (reader_ids * QBLK + query_blk).reshape(-1, tile_batch)
    global_key = (blk_ids * KBLK + key_blk).reshape(-1, tile_batch)
    items = (global_query, global_key, tile_coords[..., 2].astype(jnp.int32).reshape(-1, tile_batch),
             usable.reshape(-1, tile_batch), on_diag.reshape(-1, tile_batch))
    diagonal_cells = jnp.eye(BLOCK, dtype=bool)

    def tile_scores(item):
        g_query, g_key, patterns, usable_now, diag_now = item
        allowed = (unpack(mask_table[patterns]) | (diag_now[:, None, None] & diagonal_cells)) & usable_now[:, None, None]
        scores = jnp.einsum("gqhd,gkhd->ghqk", query_tiles[g_query], key_tiles[g_key]) * scale
        return allowed[:, None], scores

    def max_step(row_max, item):
        allowed, scores = tile_scores(item)
        tile_max = jnp.max(jnp.where(allowed, scores, NEG_FILL), axis=-1)
        return row_max.at[item[0]].max(tile_max), None

    start_max = jnp.full((N_READER * QBLK, HEADS, BLOCK), NEG_FILL, jnp.float32)
    row_max = lax.scan(max_step, start_max, items)[0]

    def sum_step(state_now, item):
        totals, weighted = state_now
        allowed, scores = tile_scores(item)
        expo = jnp.exp(jnp.where(allowed, scores - row_max[item[0]][..., None], NEG_FILL))
        totals = totals.at[item[0]].add(jnp.sum(expo, axis=-1))
        weighted = weighted.at[item[0]].add(jnp.einsum("ghqk,gkhd->gqhd", rounded_low(expo), value_tiles[item[1]]))
        return (totals, weighted), None

    start_sums = (jnp.zeros((N_READER * QBLK, HEADS, BLOCK), jnp.float32),
                  jnp.zeros((N_READER * QBLK, BLOCK, HEADS, head_dim), jnp.float32))
    totals, weighted = lax.scan(sum_step, start_sums, items)[0]
    outputs = weighted / totals.transpose(0, 2, 1)[..., None]
    attn_out = outputs.reshape(NODES, D).astype(jnp.bfloat16)
    delta = jnp.sum(grad_tiles * outputs, axis=-1).transpose(0, 2, 1)

    def grad_step(state_now, item):
        grad_query, grad_key, grad_value = state_now
        allowed, scores = tile_scores(item)
        probs = jnp.exp(jnp.where(allowed, scores - row_max[item[0]][..., None], NEG_FILL)) / totals[item[0]][..., None]
        d_rows = grad_tiles[item[0]]
        grad_value = grad_value.at[item[1]].add(jnp.einsum("ghqk,gqhd->gkhd", rounded_low(probs), d_rows))
        d_probs = jnp.einsum("gqhd,gkhd->ghqk", d_rows, value_tiles[item[1]])
        d_scores = rounded_low(probs * (d_probs - delta[item[0]][..., None]) * scale)
        grad_query = grad_query.at[item[0]].add(jnp.einsum("ghqk,gkhd->gqhd", d_scores, key_tiles[item[1]]))
        grad_key = grad_key.at[item[1]].add(jnp.einsum("ghqk,gqhd->gkhd", d_scores, query_tiles[item[0]]))
        return (grad_query, grad_key, grad_value), None

    start_grads = (jnp.zeros((N_READER * QBLK, BLOCK, HEADS, head_dim), jnp.float32),
                   jnp.zeros((N_BLK * KBLK, BLOCK, HEADS, head_dim), jnp.float32),
                   jnp.zeros((N_BLK * KBLK, BLOCK, HEADS, head_dim), jnp.float32))
    grad_query, grad_key, grad_value = lax.scan(grad_step, start_grads, items)[0]
    query_low = grad_query.reshape(NODES, D).astype(jnp.bfloat16)
    key_low = node_layout(grad_key).astype(jnp.bfloat16)
    value_low = node_layout(grad_value).astype(jnp.bfloat16)
    grad_total = jnp.dot(query_low, w_query.T, preferred_element_type=jnp.float32)
    grad_total = grad_total + jnp.dot(key_low, w_key.T, preferred_element_type=jnp.float32)
    grad_total = grad_total + jnp.dot(value_low, w_value.T, preferred_element_type=jnp.float32)
    return attn_out, grad_total.astype(jnp.bfloat16)
```

```python
import functools

import jax
import jax.numpy as jnp
from jax import lax
from jax.experimental import pallas as pl
from jax.experimental.pallas import tpu as pltpu
from jax.sharding import PartitionSpec as P

HEADS = 8
HEAD_DIM = 64
D = 512
BLOCK = 128
SCALE = 0.125
FLOOR = -1e20
NEG_FILL = -1e30
MESH = pl.DeviceIdType.MESH
F32 = jnp.float32
BF16 = jnp.bfloat16
VMEM = pltpu.VMEM


def dot(a, b):
    return jnp.dot(a, b, preferred_element_type=F32)


def dot_nt(a, b):
    return lax.dot_general(a, b, (((1,), (1,)), ((), ())), preferred_element_type=F32)


def greet(devices):
    barrier = pltpu.get_barrier_semaphore()
    for device in devices:
        pl.semaphore_signal(barrier, inc=1, device_id=device, device_id_type=MESH)
    pl.semaphore_wait(barrier, len(devices))


def gather_kernel(
    nb, nr, x_ref, g_ref, wq_ref, wk_ref, wv_ref,
    qg_ref, k_ref, v_ref, kt_ref, vt_ref,
    own, xs, psend, precv, rsend, rrecv, ssend, srecv, lsem,
):
    reader, blk = lax.axis_index("reader"), lax.axis_index("blk")
    sib = blk + 1 - 2 * lax.rem(blk, 2)
    half = nb // 2
    peer = lambda d: lax.rem(blk + 2 * d, nb)
    source = lambda d: lax.rem(blk + nb - 2 * d, nb)
    rpeer = lambda d: lax.rem(reader + d, nr)
    rsource = lambda d: lax.rem(reader + nr - d, nr)

    greet(
        [(reader, peer(d)) for d in range(1, half)]
        + [(rpeer(d), blk) for d in range(1, nr)]
        + [(reader, sib)]
    )

    def feature_copy(d):
        return pltpu.make_async_remote_copy(
            src_ref=x_ref, dst_ref=xs.at[d], send_sem=rsend.at[d], recv_sem=rrecv.at[d],
            device_id=(rpeer(d), blk), device_id_type=MESH,
        )

    def peer_copy(d):
        return pltpu.make_async_remote_copy(
            src_ref=own, dst_ref=qg_ref.at[blk], send_sem=psend.at[d], recv_sem=precv.at[d],
            device_id=(reader, peer(d)), device_id_type=MESH,
        )

    def arrival(d):
        return pltpu.make_async_remote_copy(
            src_ref=own, dst_ref=qg_ref.at[source(d)], send_sem=psend.at[d], recv_sem=precv.at[d],
            device_id=(reader, peer(d)), device_id_type=MESH,
        )

    def relay(d, src=None):
        at = source(d)
        return pltpu.make_async_remote_copy(
            src_ref=qg_ref.at[at] if src is None else src, dst_ref=qg_ref.at[at],
            send_sem=ssend.at[d], recv_sem=srecv.at[d],
            device_id=(reader, sib), device_id_type=MESH,
        )

    def relay_arrival(d):
        at = lax.rem(sib + nb - 2 * d, nb)
        return pltpu.make_async_remote_copy(
            src_ref=own, dst_ref=qg_ref.at[at],
            send_sem=ssend.at[d], recv_sem=srecv.at[d],
            device_id=(reader, sib), device_id_type=MESH,
        )

    for d in range(1, nr):
        feature_copy(d).start()
    own[D:] = g_ref[...].astype(F32).T.astype(BF16)
    q = dot(x_ref[...], wq_ref[...]).astype(BF16).astype(F32) * SCALE
    own[:D] = q.T.astype(BF16)
    for d in range(1, half):
        peer_copy(d).start()
    relay(0, own).start()
    keep = pltpu.make_async_copy(own, qg_ref.at[blk], lsem)
    keep.start()

    def project(at, rows):
        k = dot(rows, wk_ref[...])
        k_ref[at] = k.astype(BF16)
        kt_ref[at] = k.T.astype(BF16)
        v = dot(rows, wv_ref[...])
        v_ref[at] = v.astype(BF16)
        vt_ref[at] = v.T.astype(BF16)

    project(reader, x_ref[...])

    def reader_step(d, carry):
        feature_copy(d).wait_recv()
        project(rsource(d), xs[d])
        return carry

    lax.fori_loop(1, nr, reader_step, 0)

    def relay_step(d, carry):
        arrival(d).wait_recv()
        relay(d).start()
        return carry

    lax.fori_loop(1, half, relay_step, 0)

    def relay_done(d, carry):
        relay_arrival(d).wait_recv()
        relay(d).wait_send()
        return carry

    lax.fori_loop(1, half, relay_done, 0)
    relay_arrival(0).wait_recv()
    relay(0, own).wait_send()
    keep.wait()
    for d in range(1, nr):
        feature_copy(d).wait_send()
    for d in range(1, half):
        peer_copy(d).wait_send()


def gather(features, cotangent, w_query, w_key, w_value):
    nb, nr = lax.axis_size("blk"), lax.axis_size("reader")
    rows = pl.BlockSpec(memory_space=VMEM)
    sems = [pltpu.SemaphoreType.DMA((n,)) for n in (nb // 2, nb // 2, nr, nr, nb // 2, nb // 2)]
    return pl.pallas_call(
        functools.partial(gather_kernel, nb, nr),
        out_shape=[
            jax.ShapeDtypeStruct((nb, 2 * D, BLOCK), BF16),
            jax.ShapeDtypeStruct((nr, BLOCK, D), BF16),
            jax.ShapeDtypeStruct((nr, BLOCK, D), BF16),
            jax.ShapeDtypeStruct((nr, D, BLOCK), BF16),
            jax.ShapeDtypeStruct((nr, D, BLOCK), BF16),
        ],
        in_specs=[rows] * 5,
        out_specs=[pl.BlockSpec(memory_space=pl.ANY)] + [rows] * 4,
        scratch_shapes=[
            VMEM((2 * D, BLOCK), BF16),
            VMEM((nr, BLOCK, D), BF16),
            *sems,
            pltpu.SemaphoreType.DMA,
        ],
        compiler_params=pltpu.CompilerParams(
            collective_id=0, has_side_effects=True, vmem_limit_bytes=48 * 2**20
        ),
        name="gather",
    )(features, cotangent, w_query, w_key, w_value)


def tile_bias(words, first):
    spread = jnp.concatenate(
        [jnp.broadcast_to(words[w : w + 1], (32, BLOCK)) for w in range(BLOCK // 32)], axis=0
    )
    key = lax.broadcasted_iota(jnp.int32, (BLOCK, BLOCK), 0)
    query = lax.broadcasted_iota(jnp.int32, (BLOCK, BLOCK), 1)
    bits = lax.shift_right_logical(spread, key & 31) & 1
    own = jnp.where(key == query, first, 0)
    return jnp.where((bits | own) > 0, 0.0, NEG_FILL).astype(F32)


def pair_product(left, right):
    zero = jnp.zeros((HEAD_DIM, BLOCK), right.dtype)
    top = jnp.concatenate([right[:HEAD_DIM], zero], axis=1)
    bottom = jnp.concatenate([zero, right[HEAD_DIM:]], axis=1)
    return dot(left, jnp.concatenate([top, bottom], axis=0))


def stats_kernel(count_ref, coords_ref, qg_ref, k_ref, v_ref, mask_ref, out_ref):
    nb = out_ref.shape[0]
    row = lax.broadcasted_iota(jnp.int32, (nb, 3 * HEADS, BLOCK), 1)
    out_ref[...] = jnp.where(row < HEADS, FLOOR, 0.0).astype(F32)

    def tile(t, carry):
        qb, kb, p = (coords_ref[0, 0, t, c] for c in range(3))
        bias = tile_bias(mask_ref[p], jnp.where(t == 0, 1, 0))
        for pair in range(HEADS // 2):
            at = pair * 2 * HEAD_DIM
            s2 = pair_product(k_ref[kb, :, at : at + 128], qg_ref[qb, at : at + 128])
            d2 = pair_product(v_ref[kb, :, at : at + 128], qg_ref[qb, D + at : D + at + 128])
            for half in range(2):
                h = pair * 2 + half
                s = s2[:, half * BLOCK : (half + 1) * BLOCK] + bias
                m_old = out_ref[qb, h : h + 1]
                m = jnp.maximum(m_old, jnp.max(s, axis=0, keepdims=True))
                e = jnp.exp(s - m)
                drop = jnp.exp(m_old - m)
                out_ref[qb, h : h + 1] = m
                l_at, d_at = HEADS + h, 2 * HEADS + h
                out_ref[qb, l_at : l_at + 1] = out_ref[qb, l_at : l_at + 1] * drop + jnp.sum(
                    e, axis=0, keepdims=True
                )
                out_ref[qb, d_at : d_at + 1] = out_ref[qb, d_at : d_at + 1] * drop + jnp.sum(
                    e * d2[:, half * BLOCK : (half + 1) * BLOCK], axis=0, keepdims=True
                )
        return carry

    lax.fori_loop(0, count_ref[0, 0], tile, 0)


def stats(count, coords, qg, keys, values, masks):
    nb = qg.shape[0]
    smem, vmem = pl.BlockSpec(memory_space=pltpu.SMEM), pl.BlockSpec(memory_space=VMEM)
    return pl.pallas_call(
        stats_kernel,
        out_shape=jax.ShapeDtypeStruct((nb, 3 * HEADS, BLOCK), F32),
        in_specs=[smem, smem, vmem, vmem, vmem, vmem],
        out_specs=vmem,
        compiler_params=pltpu.CompilerParams(vmem_limit_bytes=48 * 2**20),
        name="stats",
    )(count, coords, qg, keys, values, masks)


def merge_kernel(nb, st_ref, out_ref, land, fin, send, recv, fsend, frecv):
    reader, blk = lax.axis_index("reader"), lax.axis_index("blk")
    peer = lambda d: lax.rem(blk + d, nb)
    source = lambda d: lax.rem(blk + nb - d, nb)
    greet([(reader, peer(d)) for d in range(1, nb)])

    def part(d):
        return pltpu.make_async_remote_copy(
            src_ref=st_ref.at[peer(d)], dst_ref=land.at[d], send_sem=send.at[d], recv_sem=recv.at[d],
            device_id=(reader, peer(d)), device_id_type=MESH,
        )

    def whole(d):
        return pltpu.make_async_remote_copy(
            src_ref=fin.at[0], dst_ref=fin.at[d], send_sem=fsend.at[d], recv_sem=frecv.at[d],
            device_id=(reader, peer(d)), device_id_type=MESH,
        )

    for d in range(1, nb):
        part(d).start()
    land[0] = st_ref[blk]
    for d in range(1, nb):
        part(d).wait()
    m = land[0, :HEADS]
    for d in range(1, nb):
        m = jnp.maximum(m, land[d, :HEADS])
    total = jnp.zeros_like(m)
    dots = jnp.zeros_like(m)
    for d in range(nb):
        weight = jnp.exp(land[d, :HEADS] - m)
        total += land[d, HEADS : 2 * HEADS] * weight
        dots += land[d, 2 * HEADS :] * weight
    fin[0, :HEADS] = m + jnp.log(total)
    fin[0, HEADS:] = dots / total
    for d in range(1, nb):
        whole(d).start()
    out_ref[blk] = fin[0]
    for d in range(1, nb):
        whole(d).wait()
        out_ref[source(d)] = fin[d]


def merge(partial):
    nb = partial.shape[0]
    vmem = pl.BlockSpec(memory_space=VMEM)
    return pl.pallas_call(
        functools.partial(merge_kernel, nb),
        out_shape=jax.ShapeDtypeStruct((nb, 2 * HEADS, BLOCK), F32),
        in_specs=[vmem],
        out_specs=vmem,
        scratch_shapes=[
            VMEM((nb, 3 * HEADS, BLOCK), F32),
            VMEM((nb, 2 * HEADS, BLOCK), F32),
            *[pltpu.SemaphoreType.DMA((nb,))] * 4,
        ],
        compiler_params=pltpu.CompilerParams(collective_id=1, has_side_effects=True),
        name="merge",
    )(partial)


def grad_kernel(
    count_ref, coords_ref, qg_ref, k_ref, v_ref, kt_ref, vt_ref, mask_ref, fin_ref, wk_ref, wv_ref,
    out_ref, kv_ref, acc, kacc, vacc,
):
    nb, nr = out_ref.shape[0], kv_ref.shape[0]

    def clear(at, carry):
        acc[at] = jnp.zeros(acc.shape[1:], F32)
        return carry

    def clear_keys(at, carry):
        kacc[at] = jnp.zeros(kacc.shape[1:], F32)
        vacc[at] = jnp.zeros(vacc.shape[1:], F32)
        return carry

    lax.fori_loop(0, nb, clear, 0)
    lax.fori_loop(0, nr, clear_keys, 0)

    def tile(t, carry):
        qb, kb, p = (coords_ref[0, 0, t, c] for c in range(3))
        bias = tile_bias(mask_ref[p], jnp.where(t == 0, 1, 0))
        for pair in range(HEADS // 2):
            at = pair * 2 * HEAD_DIM
            s2 = pair_product(k_ref[kb, :, at : at + 128], qg_ref[qb, at : at + 128])
            d2 = pair_product(v_ref[kb, :, at : at + 128], qg_ref[qb, D + at : D + at + 128])
            for half in range(2):
                h = pair * 2 + half
                lanes = slice(half * BLOCK, (half + 1) * BLOCK)
                head = slice(h * HEAD_DIM, (h + 1) * HEAD_DIM)
                ghead = slice(D + h * HEAD_DIM, D + (h + 1) * HEAD_DIM)
                prob = jnp.exp(s2[:, lanes] + bias - fin_ref[qb, h : h + 1])
                low = prob.astype(BF16)
                ds = (prob * (d2[:, lanes] - fin_ref[qb, HEADS + h : HEADS + h + 1])).astype(BF16)
                acc[qb, head] += dot(vt_ref[kb, head], low)
                acc[qb, ghead] += dot(kt_ref[kb, head], ds)
                kacc[kb, head] += dot_nt(qg_ref[qb, head], ds)
                vacc[kb, head] += dot_nt(qg_ref[qb, ghead], low)
        return carry

    lax.fori_loop(0, count_ref[0, 0], tile, 0)

    def finish(at, carry):
        out_ref[at] = acc[at].astype(BF16)
        return carry

    def finish_keys(at, carry):
        low = dot(wk_ref[...], kacc[at].astype(BF16)) + dot(wv_ref[...], vacc[at].astype(BF16))
        kv_ref[at] = low.astype(BF16)
        return carry

    lax.fori_loop(0, nb, finish, 0)
    lax.fori_loop(0, nr, finish_keys, 0)


def grads(count, coords, qg, keys, values, keys_t, values_t, masks, fin, w_key, w_value):
    nb, nr = qg.shape[0], keys.shape[0]
    smem, vmem = pl.BlockSpec(memory_space=pltpu.SMEM), pl.BlockSpec(memory_space=VMEM)
    return pl.pallas_call(
        grad_kernel,
        out_shape=[
            jax.ShapeDtypeStruct((nb, 2 * D, BLOCK), BF16),
            jax.ShapeDtypeStruct((nr, D, BLOCK), BF16),
        ],
        in_specs=[smem, smem] + [vmem] * 9,
        out_specs=[vmem, vmem],
        scratch_shapes=[
            VMEM((nb, 2 * D, BLOCK), F32),
            VMEM((nr, D, BLOCK), F32),
            VMEM((nr, D, BLOCK), F32),
        ],
        compiler_params=pltpu.CompilerParams(vmem_limit_bytes=56 * 2**20),
        name="grads",
    )(count, coords, qg, keys, values, keys_t, values_t, masks, fin, w_key, w_value)


def reduce_kernel(
    nb, nr, p_ref, kv_ref, wq_ref, attn_ref, grad_ref,
    sland, sums, land, rland, ssend, srecv, psend, precv, rsend, rrecv,
):
    reader, blk = lax.axis_index("reader"), lax.axis_index("blk")
    core = lax.rem(blk, 2)
    sib = blk + 1 - 2 * core
    half = nb // 2
    peer = lambda d: lax.rem(blk + 2 * d, nb)
    rpeer = lambda d: lax.rem(reader + d, nr)

    greet(
        [(reader, peer(d)) for d in range(1, half)]
        + [(rpeer(d), blk) for d in range(1, nr)]
        + [(reader, sib)]
    )

    def to_sibling(d):
        at = lax.rem(sib + 2 * d, nb)
        return pltpu.make_async_remote_copy(
            src_ref=p_ref.at[at], dst_ref=sland.at[d], send_sem=ssend.at[d], recv_sem=srecv.at[d],
            device_id=(reader, sib), device_id_type=MESH,
        )

    def to_reader(d):
        return pltpu.make_async_remote_copy(
            src_ref=kv_ref.at[rpeer(d)], dst_ref=rland.at[d], send_sem=rsend.at[d], recv_sem=rrecv.at[d],
            device_id=(rpeer(d), blk), device_id_type=MESH,
        )

    def to_peer(d):
        return pltpu.make_async_remote_copy(
            src_ref=sums.at[d], dst_ref=land.at[d], send_sem=psend.at[d], recv_sem=precv.at[d],
            device_id=(reader, peer(d)), device_id_type=MESH,
        )

    for d in range(1, half):
        to_sibling(d).start()
    to_sibling(0).start()
    for d in range(1, nr):
        to_reader(d).start()

    def pass_on(d, carry):
        to_sibling(d).wait_recv()
        both = p_ref[peer(d)].astype(F32) + sland[d].astype(F32)
        sums[d] = both.astype(BF16)
        to_peer(d).start()
        return carry

    lax.fori_loop(1, half, pass_on, 0)
    to_sibling(0).wait_recv()
    total = p_ref[blk].astype(F32) + sland[0].astype(F32)
    nodes = kv_ref[reader].astype(F32)
    for d in range(1, nr):
        to_reader(d).wait()
        nodes += rland[d].astype(F32)
    for d in range(1, half):
        to_peer(d).wait()
        total += land[d].astype(F32)
    attn_ref[...] = total[:D].T.astype(BF16)
    nodes += dot(wq_ref[...], (total[D:] * SCALE).astype(BF16))
    grad_ref[...] = nodes.T.astype(BF16)
    for d in range(half):
        to_sibling(d).wait_send()


def reduce(parts, key_parts, w_query):
    nb, nr = parts.shape[0], key_parts.shape[0]
    vmem = pl.BlockSpec(memory_space=VMEM)
    half = nb // 2
    return pl.pallas_call(
        functools.partial(reduce_kernel, nb, nr),
        out_shape=[jax.ShapeDtypeStruct((BLOCK, D), BF16)] * 2,
        in_specs=[vmem] * 3,
        out_specs=[vmem] * 2,
        scratch_shapes=[
            VMEM((half, 2 * D, BLOCK), BF16),
            VMEM((half, 2 * D, BLOCK), BF16),
            VMEM((half, 2 * D, BLOCK), BF16),
            VMEM((nr, D, BLOCK), BF16),
            *[pltpu.SemaphoreType.DMA((n,)) for n in (half, half, half, half, nr, nr)],
        ],
        compiler_params=pltpu.CompilerParams(
            collective_id=2, has_side_effects=True, vmem_limit_bytes=48 * 2**20
        ),
        name="reduce",
    )(parts, key_parts, w_query)


def local(features, cotangent, w_query, w_key, w_value, tile_coords, tile_count, mask_table):
    masks = mask_table.transpose(0, 2, 1)
    qg, keys, values, keys_t, values_t = gather(features, cotangent, w_query, w_key, w_value)
    partial = stats(tile_count, tile_coords, qg, keys, values, masks)
    fin = merge(partial)
    parts, key_parts = grads(
        tile_count, tile_coords, qg, keys, values, keys_t, values_t, masks, fin, w_key, w_value
    )
    return tuple(reduce(parts, key_parts, w_query))


def solution(mesh):
    return jax.shard_map(
        local,
        mesh=mesh,
        in_specs=(
            P(("reader", "blk"), None),
            P(("reader", "blk"), None),
            P(),
            P(),
            P(),
            P("reader", "blk", None, None),
            P("reader", "blk"),
            P(),
        ),
        out_specs=(P(("reader", "blk"), None), P(("reader", "blk"), None)),
        check_vma=False,
    )
```

```python
import functools

import jax
import jax.numpy as jnp
from jax import lax
from jax.experimental import pallas as pl
from jax.experimental.pallas import tpu as pltpu
from jax.sharding import PartitionSpec as P

HEADS = 8
HEAD_DIM = 64
D = 512
BLOCK = 128
SCALE = 0.125
FLOOR = -1e20
NEG_FILL = -1e30
MESH = pl.DeviceIdType.MESH
F32 = jnp.float32
BF16 = jnp.bfloat16
VMEM = pltpu.VMEM


def dot(a, b):
    return jnp.dot(a, b, preferred_element_type=F32)


def dot_nt(a, b):
    return lax.dot_general(a, b, (((1,), (1,)), ((), ())), preferred_element_type=F32)


def greet(devices):
    barrier = pltpu.get_barrier_semaphore()
    for device in devices:
        pl.semaphore_signal(barrier, inc=1, device_id=device, device_id_type=MESH)
    pl.semaphore_wait(barrier, len(devices))


def remote(src, dst, send, recv, device):
    return pltpu.make_async_remote_copy(
        src_ref=src, dst_ref=dst, send_sem=send, recv_sem=recv, device_id=device, device_id_type=MESH
    )


class Links:
    def __init__(self, send, recv, self_device):
        self.send, self.recv, self.anyone, self.started = send, recv, self_device, {}

    def start(self, i, src, dst, device):
        copy = remote(src, dst, self.send.at[i], self.recv.at[i], device)
        self.started[i] = copy
        copy.start()

    def arrive(self, i, dst):
        remote(dst, dst, self.send.at[i], self.recv.at[i], self.anyone).wait_recv()

    def finish(self):
        for copy in self.started.values():
            copy.wait_send()


def place():
    reader, blk = lax.axis_index("reader"), lax.axis_index("blk")
    return reader, blk, blk // 4, lax.rem(blk // 2, 2), lax.rem(blk, 2), reader // 4, lax.rem(reader, 4)


def neighbours():
    reader, blk, z, x, core, xh, y = place()
    on_blk = lambda z, x, core: (reader, z * 4 + x * 2 + core)
    on_reader = lambda xh, y: (xh * 4 + y, blk)
    return (
        on_blk(lax.rem(z + 1, 4), x, core),
        on_blk(lax.rem(z + 3, 4), x, core),
        on_blk(z, 1 - x, core),
        on_blk(z, x, 1 - core),
        on_reader(xh, lax.rem(y + 1, 4)),
        on_reader(xh, lax.rem(y + 3, 4)),
        on_reader(1 - xh, y),
    )


def gather_kernel(
    x_hbm, g_hbm, wq_hbm, wk_hbm, wv_hbm, mask_hbm,
    qg_ref, qn_ref, k_ref, v_ref, kt_ref, vt_ref, mask_ref, wq_ref, wkt_ref, wvt_ref,
    g_buf, wk_buf, wv_buf, xs, send, recv, local,
):
    reader, blk, z, x, core, xh, y = place()
    zp, zm, xn, sib, yp, ym, xp = neighbours()
    links = Links(send, recv, sib)
    at = lambda dz, side, other=0: (
        lax.rem(z + dz, 4) * 4 + (x if side == 0 else 1 - x) * 2 + (core if other == 0 else 1 - core)
    )
    half = pl.ds(0, D), pl.ds(D, D)
    own = xs.at[y, xh]

    loads = [
        pltpu.make_async_copy(src, dst, local.at[i])
        for i, (src, dst) in enumerate(
            [
                (x_hbm, own), (g_hbm, g_buf), (wq_hbm, wq_ref),
                (wk_hbm, wk_buf), (wv_hbm, wv_buf), (mask_hbm, mask_ref),
            ]
        )
    ]
    for load in loads:
        load.start()
    barrier = pltpu.get_barrier_semaphore()
    for device in (zp, zm, xn, sib, yp, ym, xp):
        pl.semaphore_signal(barrier, inc=1, device_id=device, device_id_type=MESH)

    def natural(b):
        qn_ref[b] = qg_ref[b].T

    loads[1].wait()
    qg_ref[blk, D:] = g_buf[...].astype(F32).T.astype(BF16)
    loads[0].wait()
    loads[2].wait()
    q = dot(xs[y, xh], wq_ref[...]).astype(BF16).astype(F32) * SCALE
    qg_ref[blk, :D] = q.T.astype(BF16)

    pl.semaphore_wait(barrier, 7)
    links.start(0, own, own, xp)
    mine = qg_ref.at[blk]
    links.start(10, mine, mine, zp)
    links.start(11, mine, mine, zm)
    links.start(12, mine, mine, xn)
    links.start(20, mine, mine, sib)

    loads[3].wait()
    loads[4].wait()

    def project(ring, side):
        b = side * 4 + ring
        rows = xs[ring, side]
        k = dot(rows, wk_buf[...])
        k_ref[b] = k.astype(BF16)
        kt_ref[b] = k.T.astype(BF16)
        v = dot(rows, wv_buf[...])
        v_ref[b] = v.astype(BF16)
        vt_ref[b] = v.T.astype(BF16)

    links.arrive(0, xs.at[y, 1 - xh])
    pair = xs.at[y]
    links.start(1, pair, pair, yp)
    links.start(2, pair, pair, ym)
    project(y, xh)
    project(y, 1 - xh)

    def relay(i, block, device):
        links.start(i, qg_ref.at[block], qg_ref.at[block], device)

    b_zm, b_zp, b_xn = at(3, 0), at(1, 0), at(0, 1)
    links.arrive(10, qg_ref.at[b_zm])
    ref = qg_ref.at[b_zm, half[0]]
    links.start(13, ref, ref, zp)
    relay(21, b_zm, sib)
    links.arrive(11, qg_ref.at[b_zp])
    ref = qg_ref.at[b_zp, half[1]]
    links.start(14, ref, ref, zm)
    relay(22, b_zp, sib)
    links.arrive(12, qg_ref.at[b_xn])
    relay(15, b_xn, zp)
    relay(16, b_xn, zm)
    relay(23, b_xn, sib)

    y_m, y_p, y_2 = lax.rem(y + 3, 4), lax.rem(y + 1, 4), lax.rem(y + 2, 4)
    links.arrive(1, xs.at[y_m])
    ref = xs.at[y_m, 0]
    links.start(3, ref, ref, yp)
    links.arrive(2, xs.at[y_p])
    ref = xs.at[y_p, 1]
    links.start(4, ref, ref, ym)
    natural(blk)
    natural(b_zm)
    natural(b_zp)
    project(y_m, 0)

    b_z2 = at(2, 0)
    links.arrive(13, qg_ref.at[b_z2, half[0]])
    links.arrive(14, qg_ref.at[b_z2, half[1]])
    relay(17, b_z2, xn)
    relay(24, b_z2, sib)
    natural(b_xn)
    project(y_m, 1)
    project(y_p, 0)
    project(y_p, 1)
    links.arrive(3, xs.at[y_2, 0])
    links.arrive(4, xs.at[y_2, 1])
    project(y_2, 0)
    project(y_2, 1)
    natural(b_z2)
    wkt_ref[...] = wk_buf[...].T
    wvt_ref[...] = wv_buf[...].T

    others = [at(0, 0, 1), at(3, 0, 1), at(1, 0, 1), at(0, 1, 1), at(2, 0, 1)]
    for i in range(4):
        links.arrive(20 + i, qg_ref.at[others[i]])
        natural(others[i])
    b_zmx, b_zpx, b_z2x = at(3, 1), at(1, 1), at(2, 1)
    links.arrive(15, qg_ref.at[b_zmx])
    relay(25, b_zmx, sib)
    links.arrive(16, qg_ref.at[b_zpx])
    relay(26, b_zpx, sib)
    natural(b_zmx)
    natural(b_zpx)
    links.arrive(24, qg_ref.at[others[4]])
    natural(others[4])
    links.arrive(17, qg_ref.at[b_z2x])
    relay(27, b_z2x, sib)
    natural(b_z2x)
    for i, block in enumerate([at(3, 1, 1), at(1, 1, 1), at(2, 1, 1)]):
        links.arrive(25 + i, qg_ref.at[block])
        natural(block)
    loads[5].wait()
    links.finish()


def gather(features, cotangent, w_query, w_key, w_value, masks):
    nb, nr = lax.axis_size("blk"), lax.axis_size("reader")
    hbm, vmem = pl.BlockSpec(memory_space=pltpu.HBM), pl.BlockSpec(memory_space=VMEM)
    return pl.pallas_call(
        gather_kernel,
        out_shape=[
            VMEM((nb, 2 * D, BLOCK), BF16),
            VMEM((nb, BLOCK, 2 * D), BF16),
            VMEM((nr, BLOCK, D), BF16),
            VMEM((nr, BLOCK, D), BF16),
            VMEM((nr, D, BLOCK), BF16),
            VMEM((nr, D, BLOCK), BF16),
            VMEM(masks.shape, jnp.int32),
            VMEM((D, D), BF16),
            VMEM((D, D), BF16),
            VMEM((D, D), BF16),
        ],
        in_specs=[hbm] * 6,
        out_specs=[vmem] * 10,
        scratch_shapes=[
            VMEM((BLOCK, D), BF16),
            VMEM((D, D), BF16),
            VMEM((D, D), BF16),
            VMEM((4, 2, BLOCK, D), BF16),
            pltpu.SemaphoreType.DMA((28,)),
            pltpu.SemaphoreType.DMA((28,)),
            pltpu.SemaphoreType.DMA((6,)),
        ],
        compiler_params=pltpu.CompilerParams(
            collective_id=0, has_side_effects=True, vmem_limit_bytes=16 * 2**20
        ),
        name="gather",
    )(*(pltpu.with_memory_space_constraint(a, pltpu.HBM) for a in (features, cotangent, w_query, w_key, w_value, masks)))


def tile_bias(words, first):
    spread = jnp.concatenate(
        [jnp.broadcast_to(words[w : w + 1], (32, BLOCK)) for w in range(BLOCK // 32)], axis=0
    )
    key = lax.broadcasted_iota(jnp.int32, (BLOCK, BLOCK), 0)
    query = lax.broadcasted_iota(jnp.int32, (BLOCK, BLOCK), 1)
    bits = lax.shift_right_logical(spread, key & 31) & 1
    own = jnp.where(key == query, first, 0)
    return jnp.where((bits | own) > 0, 0.0, NEG_FILL).astype(F32)


def pair_product(left, right):
    zero = jnp.zeros((HEAD_DIM, BLOCK), right.dtype)
    top = jnp.concatenate([right[:HEAD_DIM], zero], axis=1)
    bottom = jnp.concatenate([zero, right[HEAD_DIM:]], axis=1)
    return dot(left, jnp.concatenate([top, bottom], axis=0))


def stats_kernel(count_ref, coords_ref, qg_ref, k_ref, v_ref, mask_ref, out_ref):
    nb = out_ref.shape[0]
    row = lax.broadcasted_iota(jnp.int32, (nb, 3 * HEADS, BLOCK), 1)
    out_ref[...] = jnp.where(row < HEADS, FLOOR, 0.0).astype(F32)

    def tile(t, carry):
        qb, kb, p = (coords_ref[0, c, 0, t] for c in range(3))
        bias = tile_bias(mask_ref[p], jnp.where(t == 0, 1, 0))
        for pair in range(HEADS // 2):
            at = pair * 2 * HEAD_DIM
            s2 = pair_product(k_ref[kb, :, at : at + 128], qg_ref[qb, at : at + 128])
            d2 = pair_product(v_ref[kb, :, at : at + 128], qg_ref[qb, D + at : D + at + 128])
            for half in range(2):
                h = pair * 2 + half
                s = s2[:, half * BLOCK : (half + 1) * BLOCK] + bias
                m_old = out_ref[qb, h : h + 1]
                m = jnp.maximum(m_old, jnp.max(s, axis=0, keepdims=True))
                e = jnp.exp(s - m)
                drop = jnp.exp(m_old - m)
                out_ref[qb, h : h + 1] = m
                l_at, d_at = HEADS + h, 2 * HEADS + h
                out_ref[qb, l_at : l_at + 1] = out_ref[qb, l_at : l_at + 1] * drop + jnp.sum(
                    e, axis=0, keepdims=True
                )
                out_ref[qb, d_at : d_at + 1] = out_ref[qb, d_at : d_at + 1] * drop + jnp.sum(
                    e * d2[:, half * BLOCK : (half + 1) * BLOCK], axis=0, keepdims=True
                )
        return carry

    lax.fori_loop(0, count_ref[0, 0], tile, 0)


def stats(count, coords, qg, keys, values, masks):
    nb = qg.shape[0]
    smem, vmem = pl.BlockSpec(memory_space=pltpu.SMEM), pl.BlockSpec(memory_space=VMEM)
    return pl.pallas_call(
        stats_kernel,
        out_shape=VMEM((nb, 3 * HEADS, BLOCK), F32),
        in_specs=[smem, smem, vmem, vmem, vmem, vmem],
        out_specs=vmem,
        compiler_params=pltpu.CompilerParams(vmem_limit_bytes=8 * 2**20),
        name="stats",
    )(count, coords, qg, keys, values, masks)


def merge_kernel(nb, st_ref, out_ref, land, fin, send, recv, fsend, frecv):
    reader, blk = lax.axis_index("reader"), lax.axis_index("blk")
    peer = lambda d: lax.rem(blk + d, nb)
    source = lambda d: lax.rem(blk + nb - d, nb)
    greet([(reader, peer(d)) for d in range(1, nb)])

    def part(d):
        return pltpu.make_async_remote_copy(
            src_ref=st_ref.at[peer(d)], dst_ref=land.at[d], send_sem=send.at[d], recv_sem=recv.at[d],
            device_id=(reader, peer(d)), device_id_type=MESH,
        )

    def whole(d):
        return pltpu.make_async_remote_copy(
            src_ref=fin.at[0], dst_ref=fin.at[d], send_sem=fsend.at[d], recv_sem=frecv.at[d],
            device_id=(reader, peer(d)), device_id_type=MESH,
        )

    for d in range(1, nb):
        part(d).start()
    land[0] = st_ref[blk]
    for d in range(1, nb):
        part(d).wait()
    m = land[0, :HEADS]
    for d in range(1, nb):
        m = jnp.maximum(m, land[d, :HEADS])
    total = jnp.zeros_like(m)
    dots = jnp.zeros_like(m)
    for d in range(nb):
        weight = jnp.exp(land[d, :HEADS] - m)
        total += land[d, HEADS : 2 * HEADS] * weight
        dots += land[d, 2 * HEADS :] * weight
    fin[0, :HEADS] = m + jnp.log(total)
    fin[0, HEADS:] = dots / total
    for d in range(1, nb):
        whole(d).start()
    out_ref[blk] = fin[0]
    for d in range(1, nb):
        whole(d).wait()
        out_ref[source(d)] = fin[d]


def merge(partial):
    nb = partial.shape[0]
    vmem = pl.BlockSpec(memory_space=VMEM)
    return pl.pallas_call(
        functools.partial(merge_kernel, nb),
        out_shape=VMEM((nb, 2 * HEADS, BLOCK), F32),
        in_specs=[vmem],
        out_specs=vmem,
        scratch_shapes=[
            VMEM((nb, 3 * HEADS, BLOCK), F32),
            VMEM((nb, 2 * HEADS, BLOCK), F32),
            *[pltpu.SemaphoreType.DMA((nb,))] * 4,
        ],
        compiler_params=pltpu.CompilerParams(
            collective_id=1, has_side_effects=True, vmem_limit_bytes=4 * 2**20
        ),
        name="merge",
    )(partial)


def lane_split(block):
    lane = lax.broadcasted_iota(jnp.int32, block.shape, 1)
    zero = jnp.zeros_like(block)
    return jnp.concatenate(
        [jnp.where(lane < HEAD_DIM, block, zero), jnp.where(lane >= HEAD_DIM, block, zero)], axis=0
    )


def grad_kernel(
    count_ref, coords_ref, qg_ref, qn_ref, k_ref, v_ref, kt_ref, vt_ref, mask_ref, fin_ref, wkt_ref, wvt_ref,
    acc, kv_ref, kacc, vacc, probs, dscores,
):
    nb, nr = acc.shape[0], kacc.shape[0]

    def clear(at, carry):
        acc[at] = jnp.zeros(acc.shape[1:], F32)
        return carry

    def clear_keys(at, carry):
        kacc[at] = jnp.zeros(kacc.shape[1:], F32)
        vacc[at] = jnp.zeros(vacc.shape[1:], F32)
        return carry

    lax.fori_loop(0, nb, clear, 0)
    lax.fori_loop(0, nr, clear_keys, 0)

    def scores(t):
        qb, kb, p = (coords_ref[0, c, 0, t] for c in range(3))
        bias = tile_bias(mask_ref[p], jnp.where(t == 0, 1, 0))
        for pair in range(HEADS // 2):
            at = pair * 2 * HEAD_DIM
            s2 = pair_product(k_ref[kb, :, at : at + 128], qg_ref[qb, at : at + 128])
            d2 = pair_product(v_ref[kb, :, at : at + 128], qg_ref[qb, D + at : D + at + 128])
            for half in range(2):
                h = pair * 2 + half
                lanes = slice(half * BLOCK, (half + 1) * BLOCK)
                prob = jnp.exp(s2[:, lanes] + bias - fin_ref[qb, h : h + 1])
                probs[h] = prob.astype(BF16)
                delta = fin_ref[qb, HEADS + h : HEADS + h + 1]
                dscores[h] = (prob * (d2[:, lanes] - delta)).astype(BF16)

    def products(t):
        qb, kb = coords_ref[0, 0, 0, t], coords_ref[0, 1, 0, t]
        for pair in range(HEADS // 2):
            for h in (2 * pair, 2 * pair + 1):
                head = slice(h * HEAD_DIM, (h + 1) * HEAD_DIM)
                ghead = slice(D + h * HEAD_DIM, D + (h + 1) * HEAD_DIM)
                acc[qb, head] += dot(vt_ref[kb, head], probs[h])
                acc[qb, ghead] += dot(kt_ref[kb, head], dscores[h])
            two = slice(pair * 128, pair * 128 + 128)
            gtwo = slice(D + pair * 128, D + pair * 128 + 128)
            low = jnp.concatenate([probs[2 * pair], probs[2 * pair + 1]], axis=1)
            ds = jnp.concatenate([dscores[2 * pair], dscores[2 * pair + 1]], axis=1)
            kacc[kb, :, two] += dot(ds, lane_split(qn_ref[qb, :, two]))
            vacc[kb, :, two] += dot(low, lane_split(qn_ref[qb, :, gtwo]))

    def step(t, carry):
        products(t - 1)
        scores(t)
        return carry

    count = count_ref[0, 0]
    scores(0)
    lax.fori_loop(1, count, step, 0)
    products(count - 1)

    for ring in range(4):
        for side in range(2):
            at = side * 4 + ring
            total = dot(kacc[at].astype(BF16), wkt_ref[...]) + dot(vacc[at].astype(BF16), wvt_ref[...])
            kv_ref[ring, side] = total.astype(BF16)


def grads(count, coords, qg, qn, keys, values, keys_t, values_t, masks, fin, wkt, wvt):
    nb, nr = qg.shape[0], keys.shape[0]
    smem, vmem = pl.BlockSpec(memory_space=pltpu.SMEM), pl.BlockSpec(memory_space=VMEM)
    return pl.pallas_call(
        grad_kernel,
        out_shape=[VMEM((nb, 2 * D, BLOCK), F32), VMEM((4, 2, BLOCK, D), BF16)],
        in_specs=[smem, smem] + [vmem] * 10,
        out_specs=[vmem, vmem],
        scratch_shapes=[
            VMEM((nr, BLOCK, D), F32),
            VMEM((nr, BLOCK, D), F32),
            VMEM((HEADS, BLOCK, BLOCK), BF16),
            VMEM((HEADS, BLOCK, BLOCK), BF16),
        ],
        compiler_params=pltpu.CompilerParams(vmem_limit_bytes=16 * 2**20),
        name="grads",
    )(count, coords, qg, qn, keys, values, keys_t, values_t, masks, fin, wkt, wvt)


def reduce_kernel(
    p_ref, kv_ref, wq_ref, attn_ref, grad_ref,
    to_sib, from_sib, sums, land, halves, kland, khalves, ksum, send, recv,
):
    reader, blk, z, x, core, xh, y = place()
    zp, zm, xn, sib, yp, ym, xp = neighbours()
    links = Links(send, recv, sib)
    at = lambda dz, side, other=0: (
        lax.rem(z + dz, 4) * 4 + (x if side == 0 else 1 - x) * 2 + (core if other == 0 else 1 - core)
    )
    order = [(2, 1), (1, 1), (3, 1), (2, 0), (0, 1), (1, 0), (3, 0), (0, 0)]
    barrier = pltpu.get_barrier_semaphore()
    for device in (zp, zm, xn, sib, yp, ym, xp):
        pl.semaphore_signal(barrier, inc=1, device_id=device, device_id_type=MESH)
    for i in range(2):
        to_sib[i] = p_ref[at(*order[i], 1)].astype(BF16)
    pl.semaphore_wait(barrier, 7)

    y_m, y_p, y_2 = lax.rem(y + 3, 4), lax.rem(y + 1, 4), lax.rem(y + 2, 4)
    links.start(0, kv_ref.at[y_2, 0], khalves.at[0], yp)
    links.start(1, kv_ref.at[y_2, 1], khalves.at[1], ym)
    for i in range(8):
        if i >= 2:
            to_sib[i] = p_ref[at(*order[i], 1)].astype(BF16)
        links.start(20 + i, to_sib.at[i], from_sib.at[i], sib)

    def both(i):
        links.arrive(20 + i, from_sib.at[i])
        return p_ref[at(*order[i])] + from_sib[i].astype(F32)

    sums[0] = both(0).astype(BF16)
    links.start(10, sums.at[0], land.at[0], xn)
    sums[1] = both(1).astype(BF16)
    links.start(11, sums.at[1], land.at[1], zp)
    sums[2] = both(2).astype(BF16)
    links.start(12, sums.at[2], land.at[2], zm)

    links.arrive(0, khalves.at[0])
    ksum[0, 0] = (kv_ref[y_p, 0].astype(F32) + khalves[0].astype(F32)).astype(BF16)
    ksum[0, 1] = kv_ref[y_p, 1]
    links.start(2, ksum.at[0], kland.at[0], yp)
    links.arrive(1, khalves.at[1])
    ksum[1, 0] = kv_ref[y_m, 0]
    ksum[1, 1] = (kv_ref[y_m, 1].astype(F32) + khalves[1].astype(F32)).astype(BF16)
    links.start(3, ksum.at[1], kland.at[1], ym)

    far = both(3)
    links.arrive(10, land.at[0])
    sums[3] = (far + land[0].astype(F32)).astype(BF16)
    links.start(13, sums.at[3, pl.ds(0, D)], halves.at[0], zp)
    links.start(14, sums.at[3, pl.ds(D, D)], halves.at[1], zm)
    across = both(4)
    links.arrive(11, land.at[1])
    links.arrive(12, land.at[2])
    sums[4] = (across + land[1].astype(F32) + land[2].astype(F32)).astype(BF16)
    links.start(15, sums.at[4], land.at[3], xn)

    up = both(5)
    links.arrive(13, halves.at[0])
    sums[5, :D] = (up[:D] + halves[0].astype(F32)).astype(BF16)
    sums[5, D:] = up[D:].astype(BF16)
    links.start(16, sums.at[5], land.at[4], zp)
    down = both(6)
    links.arrive(14, halves.at[1])
    sums[6, :D] = down[:D].astype(BF16)
    sums[6, D:] = (down[D:] + halves[1].astype(F32)).astype(BF16)
    links.start(17, sums.at[6], land.at[5], zm)

    links.arrive(2, kland.at[0])
    links.arrive(3, kland.at[1])
    ksum[2, 0] = (
        kv_ref[y, 1 - xh].astype(F32) + kland[0, 1 - xh].astype(F32) + kland[1, 1 - xh].astype(F32)
    ).astype(BF16)
    links.start(4, ksum.at[2, 0], ksum.at[2, 1], xp)
    nodes = kv_ref[y, xh].astype(F32) + kland[0, xh].astype(F32) + kland[1, xh].astype(F32)

    total = both(7)
    links.arrive(15, land.at[3])
    total += land[3].astype(F32)
    links.arrive(4, ksum.at[2, 1])
    nodes += ksum[2, 1].astype(F32)
    links.arrive(16, land.at[4])
    links.arrive(17, land.at[5])
    total += land[4].astype(F32) + land[5].astype(F32)
    attn_ref[...] = total[:D].T.astype(BF16)
    nodes += dot(wq_ref[...], (total[D:] * SCALE).astype(BF16)).T
    grad_ref[...] = nodes.astype(BF16)
    links.finish()


def reduce(parts, key_parts, w_query):
    vmem = pl.BlockSpec(memory_space=VMEM)
    block = (2 * D, BLOCK)
    return pl.pallas_call(
        reduce_kernel,
        out_shape=[jax.ShapeDtypeStruct((BLOCK, D), BF16)] * 2,
        in_specs=[vmem] * 3,
        out_specs=[vmem] * 2,
        scratch_shapes=[
            VMEM((8, *block), BF16),
            VMEM((8, *block), BF16),
            VMEM((7, *block), BF16),
            VMEM((6, *block), BF16),
            VMEM((2, D, BLOCK), BF16),
            VMEM((2, 2, BLOCK, D), BF16),
            VMEM((2, BLOCK, D), BF16),
            VMEM((3, 2, BLOCK, D), BF16),
            pltpu.SemaphoreType.DMA((28,)),
            pltpu.SemaphoreType.DMA((28,)),
        ],
        compiler_params=pltpu.CompilerParams(
            collective_id=2, has_side_effects=True, vmem_limit_bytes=24 * 2**20
        ),
        name="reduce",
    )(parts, key_parts, w_query)


def local(features, cotangent, w_query, w_key, w_value, tile_coords, tile_count, mask_table):
    masks = mask_table.transpose(0, 2, 1)
    coords = tile_coords.transpose(0, 3, 1, 2)
    qg, qn, keys, values, keys_t, values_t, masks, wq, wkt, wvt = gather(
        features, cotangent, w_query, w_key, w_value, masks
    )
    partial = stats(tile_count, coords, qg, keys, values, masks)
    fin = merge(partial)
    parts, key_parts = grads(
        tile_count, coords, qg, qn, keys, values, keys_t, values_t, masks, fin, wkt, wvt
    )
    return tuple(reduce(parts, key_parts, wq))


def solution(mesh):
    return jax.shard_map(
        local,
        mesh=mesh,
        in_specs=(
            P(("reader", "blk"), None),
            P(("reader", "blk"), None),
            P(),
            P(),
            P(),
            P("reader", "blk", None, None),
            P("reader", "blk"),
            P(),
        ),
        out_specs=(P(("reader", "blk"), None), P(("reader", "blk"), None)),
        check_vma=False,
    )
```

```python
import functools

import jax
import jax.numpy as jnp
from jax import lax
from jax.experimental import pallas as pl
from jax.experimental.pallas import tpu as pltpu
from jax.sharding import PartitionSpec as P

HEADS = 8
HEAD_DIM = 64
D = 512
BLOCK = 128
SCALE = 0.125
FLOOR = -1e20
NEG_FILL = -1e30
MESH = pl.DeviceIdType.MESH
F32 = jnp.float32
BF16 = jnp.bfloat16
VMEM = pltpu.VMEM


def dot(a, b):
    return jnp.dot(a, b, preferred_element_type=F32)


def remote(src, dst, send, recv, device):
    return pltpu.make_async_remote_copy(
        src_ref=src, dst_ref=dst, send_sem=send, recv_sem=recv, device_id=device, device_id_type=MESH
    )


class Links:
    def __init__(self, send, recv, self_device):
        self.send, self.recv, self.anyone, self.started = send, recv, self_device, {}

    def start(self, i, src, dst, device):
        copy = remote(src, dst, self.send.at[i], self.recv.at[i], device)
        self.started[i] = copy
        copy.start()

    def arrive(self, i, dst):
        remote(dst, dst, self.send.at[i], self.recv.at[i], self.anyone).wait_recv()

    def finish(self):
        for copy in self.started.values():
            copy.wait_send()


def place():
    reader, blk = lax.axis_index("reader"), lax.axis_index("blk")
    return reader, blk, blk // 4, lax.rem(blk // 2, 2), lax.rem(blk, 2), reader // 4, lax.rem(reader, 4)


def neighbours():
    reader, blk, z, x, core, xh, y = place()
    on_blk = lambda z, x, core: (reader, z * 4 + x * 2 + core)
    on_reader = lambda xh, y: (xh * 4 + y, blk)
    return (
        on_blk(lax.rem(z + 1, 4), x, core),
        on_blk(lax.rem(z + 3, 4), x, core),
        on_blk(z, 1 - x, core),
        on_blk(z, x, 1 - core),
        on_reader(xh, lax.rem(y + 1, 4)),
        on_reader(xh, lax.rem(y + 3, 4)),
        on_reader(1 - xh, y),
    )


def blocks():
    _, _, z, x, core, _, _ = place()
    return lambda dz, side, other=0: (
        lax.rem(z + dz, 4) * 4 + (x if side == 0 else 1 - x) * 2 + (core if other == 0 else 1 - core)
    )


def gather_kernel(
    x_hbm, g_hbm, wq_hbm, wk_hbm, wv_hbm, mask_hbm,
    qt_ref, gt_ref, qn_ref, gn_ref, k_ref, v_ref, kt_ref, vt_ref, mask_ref, wq_ref, wkt_ref, wvt_ref,
    wk_buf, wv_buf, xb, xs, send, recv, local,
):
    reader, blk, z, x, core, xh, y = place()
    zp, zm, xn, sib, yp, ym, xp = neighbours()
    links = Links(send, recv, sib)
    at = blocks()

    barrier = pltpu.get_barrier_semaphore()
    for device in (zp, zm, xn, sib, yp, ym, xp):
        pl.semaphore_signal(barrier, inc=1, device_id=device, device_id_type=MESH)
    loads = [
        pltpu.make_async_copy(src, dst, local.at[i])
        for i, (src, dst) in enumerate(
            [
                (x_hbm, xs.at[y, xh]), (x_hbm, xb.at[blk]), (g_hbm, gn_ref.at[blk]), (wk_hbm, wk_buf),
                (wv_hbm, wv_buf), (wq_hbm, wq_ref), (mask_hbm, mask_ref),
            ]
        )
    ]
    for load in loads:
        load.start()
    pl.semaphore_wait(barrier, 7)

    links.start(10, x_hbm, xb.at[blk], zp)
    links.start(12, x_hbm, xb.at[blk], zm)
    links.start(14, x_hbm, xb.at[blk], xn)
    links.start(1, x_hbm, xs.at[y, xh], yp)
    links.start(2, x_hbm, xs.at[y, xh], ym)
    links.start(0, x_hbm, xs.at[y, xh], xp)
    links.start(11, g_hbm, gn_ref.at[blk], zp)
    links.start(13, g_hbm, gn_ref.at[blk], zm)
    links.start(15, g_hbm, gn_ref.at[blk], xn)
    links.start(30, x_hbm, xb.at[blk], sib)
    links.start(31, g_hbm, gn_ref.at[blk], sib)

    def arrive_x(i, b):
        links.arrive(i, xb.at[b])

    def arrive_g(i, b):
        links.arrive(i, gn_ref.at[b])

    def pass_x(i, b, device):
        links.start(i, xb.at[b], xb.at[b], device)

    def pass_g(i, b, device):
        links.start(i, gn_ref.at[b], gn_ref.at[b], device)

    def arrive_s(i, ring, side):
        links.arrive(i, xs.at[ring, side])

    def pass_s(i, ring, side, device):
        links.start(i, xs.at[ring, side], xs.at[ring, side], device)

    def prepare(b):
        q = (dot(xb[b], wq_ref[...]).astype(BF16).astype(F32) * SCALE).astype(BF16)
        qn_ref[b] = q
        qt_ref[b] = q.T
        gt_ref[b] = gn_ref[b].T

    def project(ring, side):
        b = side * 4 + ring
        rows = xs[ring, side]
        k = dot(rows, wk_buf[...]).astype(BF16)
        k_ref[b] = k
        kt_ref[b] = k.T
        v = dot(rows, wv_buf[...]).astype(BF16)
        v_ref[b] = v
        vt_ref[b] = v.T

    b_zm, b_zp, b_xn, b_z2 = at(3, 0), at(1, 0), at(0, 1), at(2, 0)
    b_zmx, b_zpx, b_z2x = at(3, 1), at(1, 1), at(2, 1)
    y_m, y_p, y_2 = lax.rem(y + 3, 4), lax.rem(y + 1, 4), lax.rem(y + 2, 4)

    for i in range(6):
        loads[i].wait()
    project(y, xh)
    prepare(blk)

    arrive_x(10, b_zm)
    pass_x(18, b_zm, zp)
    arrive_x(14, b_xn)
    pass_x(20, b_xn, zp)
    pass_x(22, b_xn, zm)
    arrive_x(12, b_zp)
    arrive_s(1, y_m, xh)
    pass_s(5, y_m, xh, yp)
    pass_x(32, b_zm, sib)
    pass_x(34, b_zp, sib)
    pass_x(36, b_xn, sib)
    arrive_s(2, y_p, xh)
    project(y_m, xh)

    arrive_g(13, b_zp)
    pass_g(19, b_zp, zm)
    arrive_g(15, b_xn)
    pass_g(21, b_xn, zp)
    pass_g(23, b_xn, zm)
    arrive_s(0, y, 1 - xh)
    pass_s(3, y, 1 - xh, yp)
    pass_s(4, y, 1 - xh, ym)
    arrive_g(11, b_zm)
    pass_g(33, b_zm, sib)
    pass_g(35, b_zp, sib)
    pass_g(37, b_xn, sib)
    project(y_p, xh)
    project(y, 1 - xh)

    arrive_x(18, b_z2)
    pass_x(24, b_z2, xn)
    pass_x(38, b_z2, sib)
    prepare(b_zm)
    prepare(b_zp)
    arrive_s(4, y_p, 1 - xh)
    pass_s(6, y_p, 1 - xh, ym)
    arrive_g(19, b_z2)
    pass_g(25, b_z2, xn)
    pass_g(39, b_z2, sib)
    prepare(b_xn)
    project(y_p, 1 - xh)
    arrive_s(3, y_m, 1 - xh)
    project(y_m, 1 - xh)
    arrive_s(5, y_2, xh)
    project(y_2, xh)
    wkt_ref[...] = wk_buf[...].T
    wvt_ref[...] = wv_buf[...].T

    o_own, o_zm, o_zp, o_xn, o_z2 = at(0, 0, 1), at(3, 0, 1), at(1, 0, 1), at(0, 1, 1), at(2, 0, 1)
    for i, b in ((30, o_own), (32, o_zm), (34, o_zp), (36, o_xn)):
        arrive_x(i, b)
        arrive_g(i + 1, b)
        prepare(b)
    arrive_x(20, b_zmx)
    pass_x(40, b_zmx, sib)
    arrive_x(22, b_zpx)
    pass_x(42, b_zpx, sib)
    arrive_s(6, y_2, 1 - xh)
    project(y_2, 1 - xh)
    prepare(b_z2)
    arrive_g(23, b_zpx)
    pass_g(43, b_zpx, sib)
    arrive_g(21, b_zmx)
    pass_g(41, b_zmx, sib)
    arrive_x(24, b_z2x)
    pass_x(44, b_z2x, sib)
    arrive_x(38, o_z2)
    arrive_g(39, o_z2)
    prepare(o_z2)
    prepare(b_zmx)
    prepare(b_zpx)
    arrive_g(25, b_z2x)
    pass_g(45, b_z2x, sib)
    prepare(b_z2x)
    for i, b in ((40, at(3, 1, 1)), (42, at(1, 1, 1)), (44, at(2, 1, 1))):
        arrive_x(i, b)
        arrive_g(i + 1, b)
        prepare(b)
    loads[6].wait()
    links.finish()


def gather(features, cotangent, w_query, w_key, w_value, masks):
    nb, nr = lax.axis_size("blk"), lax.axis_size("reader")
    hbm, vmem = pl.BlockSpec(memory_space=pltpu.HBM), pl.BlockSpec(memory_space=VMEM)
    operands = (features, cotangent, w_query, w_key, w_value, masks)
    return pl.pallas_call(
        gather_kernel,
        out_shape=[
            VMEM((nb, D, BLOCK), BF16),
            VMEM((nb, D, BLOCK), BF16),
            VMEM((nb, BLOCK, D), BF16),
            VMEM((nb, BLOCK, D), BF16),
            VMEM((nr, BLOCK, D), BF16),
            VMEM((nr, BLOCK, D), BF16),
            VMEM((nr, D, BLOCK), BF16),
            VMEM((nr, D, BLOCK), BF16),
            VMEM(masks.shape, jnp.int32),
            VMEM((D, D), BF16),
            VMEM((D, D), BF16),
            VMEM((D, D), BF16),
        ],
        in_specs=[hbm] * 6,
        out_specs=[vmem] * 12,
        scratch_shapes=[
            VMEM((D, D), BF16),
            VMEM((D, D), BF16),
            VMEM((nb, BLOCK, D), BF16),
            VMEM((4, 2, BLOCK, D), BF16),
            pltpu.SemaphoreType.DMA((46,)),
            pltpu.SemaphoreType.DMA((46,)),
            pltpu.SemaphoreType.DMA((7,)),
        ],
        compiler_params=pltpu.CompilerParams(
            collective_id=0, has_side_effects=True, vmem_limit_bytes=16 * 2**20
        ),
        name="gather",
    )(*(pltpu.with_memory_space_constraint(a, pltpu.HBM) for a in operands))


def tile_bias(words, t, count):
    spread = jnp.concatenate(
        [jnp.broadcast_to(words[w : w + 1], (32, BLOCK)) for w in range(BLOCK // 32)], axis=0
    )
    key = lax.broadcasted_iota(jnp.int32, (BLOCK, BLOCK), 0)
    query = lax.broadcasted_iota(jnp.int32, (BLOCK, BLOCK), 1)
    own = jnp.where(key == query, jnp.where(t == 0, 1, 0), 0)
    bits = (lax.shift_right_logical(spread, key & 31) | own) & jnp.where(t < count, 1, 0)
    return jnp.where(bits > 0, 0.0, NEG_FILL).astype(F32)


def pair_product(left, right):
    zero = jnp.zeros((HEAD_DIM, BLOCK), right.dtype)
    top = jnp.concatenate([right[:HEAD_DIM], zero], axis=1)
    bottom = jnp.concatenate([zero, right[HEAD_DIM:]], axis=1)
    return dot(left, jnp.concatenate([top, bottom], axis=0))


UNROLL = 4


def stats_kernel(count_ref, coords_ref, qt_ref, gt_ref, k_ref, v_ref, mask_ref, out_ref, run):
    nb = out_ref.shape[0]
    row = lax.broadcasted_iota(jnp.int32, run.shape, 1)
    run[...] = jnp.where(row < HEADS, FLOOR, 0.0).astype(F32)
    count = count_ref[0, 0]

    def tile(t):
        qb, kb, p = (coords_ref[0, c, 0, t] for c in range(3))
        bias = tile_bias(mask_ref[p], t, count)
        peaks, totals, dots = [], [], []
        for pair in range(HEADS // 2):
            two = slice(pair * 128, pair * 128 + 128)
            s2 = pair_product(k_ref[kb, :, two], qt_ref[qb, two])
            d2 = pair_product(v_ref[kb, :, two], gt_ref[qb, two])
            for half in range(2):
                lanes = slice(half * BLOCK, (half + 1) * BLOCK)
                s = s2[:, lanes] + bias
                peak = jnp.max(s, axis=0, keepdims=True)
                e = jnp.exp(s - peak)
                peaks.append(peak)
                totals.append(jnp.sum(e, axis=0, keepdims=True))
                dots.append(jnp.sum(e * d2[:, lanes], axis=0, keepdims=True))
        return qb, *(jnp.concatenate(rows, axis=0) for rows in (peaks, totals, dots))

    def add(qb, peak, total, dots):
        before = run[qb, :HEADS]
        m = jnp.maximum(before, peak)
        old, new = jnp.exp(before - m), jnp.exp(peak - m)
        run[qb, :HEADS] = m
        run[qb, HEADS : 2 * HEADS] = run[qb, HEADS : 2 * HEADS] * old + total * new
        run[qb, 2 * HEADS :] = run[qb, 2 * HEADS :] * old + dots * new

    def step(g, carry):
        for found in [tile(g * UNROLL + u) for u in range(UNROLL)]:
            add(*found)
        return carry

    lax.fori_loop(0, (count + UNROLL - 1) // UNROLL, step, 0)
    for b in range(nb):
        total = jnp.maximum(run[b, HEADS : 2 * HEADS], 1e-30)
        out_ref[b, :HEADS] = run[b, :HEADS] + jnp.log(total)
        out_ref[b, HEADS:] = run[b, 2 * HEADS :] / total


def stats(count, coords, qt, gt, keys, values, masks):
    nb = qt.shape[0]
    smem, vmem = pl.BlockSpec(memory_space=pltpu.SMEM), pl.BlockSpec(memory_space=VMEM)
    return pl.pallas_call(
        stats_kernel,
        out_shape=VMEM((nb, 2 * HEADS, BLOCK), F32),
        in_specs=[smem, smem] + [vmem] * 5,
        out_specs=vmem,
        scratch_shapes=[VMEM((nb, 3 * HEADS, BLOCK), F32)],
        compiler_params=pltpu.CompilerParams(vmem_limit_bytes=8 * 2**20),
        name="stats",
    )(count, coords, qt, gt, keys, values, masks)


def merge_kernel(nb, st_ref, out_ref, acc, kacc, vacc, land, fin, send, recv, fsend, frecv):
    reader, blk = lax.axis_index("reader"), lax.axis_index("blk")
    peer = lambda d: lax.rem(blk + d, nb)
    source = lambda d: lax.rem(blk + nb - d, nb)
    barrier = pltpu.get_barrier_semaphore()
    for d in range(1, nb):
        pl.semaphore_signal(barrier, inc=1, device_id=(reader, peer(d)), device_id_type=MESH)

    def clear(ref):
        def one(b, carry):
            ref[b] = jnp.zeros(ref.shape[1:], F32)
            return carry

        lax.fori_loop(0, ref.shape[0], one, 0)

    def part(d):
        return remote(st_ref.at[peer(d)], land.at[d], send.at[d], recv.at[d], (reader, peer(d)))

    def whole(d):
        return remote(fin.at[0], fin.at[d], fsend.at[d], frecv.at[d], (reader, peer(d)))

    clear(kacc)
    pl.semaphore_wait(barrier, nb - 1)
    for d in range(1, nb):
        part(d).start()
    land[0] = st_ref[blk]
    clear(vacc)
    for d in range(1, nb):
        part(d).wait()
    m = land[0, :HEADS]
    for d in range(1, nb):
        m = jnp.maximum(m, land[d, :HEADS])
    total = jnp.zeros_like(m)
    dots = jnp.zeros_like(m)
    for d in range(nb):
        weight = jnp.exp(land[d, :HEADS] - m)
        total += weight
        dots += land[d, HEADS:] * weight
    fin[0, :HEADS] = m + jnp.log(total)
    fin[0, HEADS:] = dots / total
    for d in range(1, nb):
        whole(d).start()
    out_ref[blk] = fin[0]
    clear(acc)
    for d in range(1, nb):
        whole(d).wait()
        out_ref[source(d)] = fin[d]


def merge(partial, nr):
    nb = partial.shape[0]
    vmem = pl.BlockSpec(memory_space=VMEM)
    return pl.pallas_call(
        functools.partial(merge_kernel, nb),
        out_shape=[
            VMEM(partial.shape, F32),
            VMEM((nb, 2 * D, BLOCK), F32),
            VMEM((nr, BLOCK, D), F32),
            VMEM((nr, BLOCK, D), F32),
        ],
        in_specs=[vmem],
        out_specs=[vmem] * 4,
        scratch_shapes=[
            VMEM(partial.shape, F32),
            VMEM(partial.shape, F32),
            *[pltpu.SemaphoreType.DMA((nb,))] * 4,
        ],
        compiler_params=pltpu.CompilerParams(
            collective_id=1, has_side_effects=True, vmem_limit_bytes=4 * 2**20
        ),
        name="merge",
    )(partial)


def lane_split(block):
    lane = lax.broadcasted_iota(jnp.int32, block.shape, 1)
    zero = jnp.zeros_like(block)
    return jnp.concatenate(
        [jnp.where(lane < HEAD_DIM, block, zero), jnp.where(lane >= HEAD_DIM, block, zero)], axis=0
    )


def grad_kernel(
    count_ref, coords_ref, qt_ref, gt_ref, qn_ref, gn_ref, k_ref, v_ref, kt_ref, vt_ref, mask_ref, fin_ref, wkt_ref,
    wvt_ref, acc_in, kacc_in, vacc_in, acc, kacc, vacc, kv_ref, probs, dscores,
):
    count = count_ref[0, 0]

    def scores(t, u):
        qb, kb, p = (coords_ref[0, c, 0, t] for c in range(3))
        bias = tile_bias(mask_ref[p], t, count)
        for pair in range(HEADS // 2):
            two = slice(pair * 128, pair * 128 + 128)
            s2 = pair_product(k_ref[kb, :, two], qt_ref[qb, two])
            d2 = pair_product(v_ref[kb, :, two], gt_ref[qb, two])
            for half in range(2):
                h = pair * 2 + half
                lanes = slice(half * BLOCK, (half + 1) * BLOCK)
                prob = jnp.exp(s2[:, lanes] + bias - fin_ref[qb, h : h + 1])
                probs[u, h] = prob.astype(BF16)
                delta = fin_ref[qb, HEADS + h : HEADS + h + 1]
                dscores[u, h] = (prob * (d2[:, lanes] - delta)).astype(BF16)

    def products(t, u):
        qb, kb = coords_ref[0, 0, 0, t], coords_ref[0, 1, 0, t]
        for pair in range(HEADS // 2):
            for h in (2 * pair, 2 * pair + 1):
                head = slice(h * HEAD_DIM, (h + 1) * HEAD_DIM)
                ghead = slice(D + h * HEAD_DIM, D + (h + 1) * HEAD_DIM)
                acc[qb, head] += dot(vt_ref[kb, head], probs[u, h])
                acc[qb, ghead] += dot(kt_ref[kb, head], dscores[u, h])
            two = slice(pair * 128, pair * 128 + 128)
            low = jnp.concatenate([probs[u, 2 * pair], probs[u, 2 * pair + 1]], axis=1)
            ds = jnp.concatenate([dscores[u, 2 * pair], dscores[u, 2 * pair + 1]], axis=1)
            kacc[kb, :, two] += dot(ds, lane_split(qn_ref[qb, :, two]))
            vacc[kb, :, two] += dot(low, lane_split(gn_ref[qb, :, two]))

    def step(g, carry):
        for u in range(UNROLL):
            scores(g * UNROLL + u, u)
        for u in range(UNROLL):
            products(g * UNROLL + u, u)
        return carry

    lax.fori_loop(0, (count + UNROLL - 1) // UNROLL, step, 0)
    for side in range(2):
        rows = pl.ds(side * 4, 4)
        keys = kacc[rows].reshape(4 * BLOCK, D).astype(BF16)
        values = vacc[rows].reshape(4 * BLOCK, D).astype(BF16)
        total = dot(keys, wkt_ref[...]) + dot(values, wvt_ref[...])
        kv_ref[:, side] = total.reshape(4, BLOCK, D).astype(BF16)


def grads(count, coords, arrays, acc, kacc, vacc):
    smem, vmem = pl.BlockSpec(memory_space=pltpu.SMEM), pl.BlockSpec(memory_space=VMEM)
    first = 2 + len(arrays)
    out = pl.pallas_call(
        grad_kernel,
        out_shape=[
            VMEM(acc.shape, F32),
            VMEM(kacc.shape, F32),
            VMEM(vacc.shape, F32),
            VMEM((4, 2, BLOCK, D), BF16),
        ],
        in_specs=[smem, smem] + [vmem] * (len(arrays) + 3),
        out_specs=[vmem] * 4,
        scratch_shapes=[VMEM((UNROLL, HEADS, BLOCK, BLOCK), BF16)] * 2,
        input_output_aliases={first: 0, first + 1: 1, first + 2: 2},
        compiler_params=pltpu.CompilerParams(vmem_limit_bytes=12 * 2**20),
        name="grads",
    )(count, coords, *arrays, acc, kacc, vacc)
    return out[0], out[3]


def reduce_kernel(
    p_ref, kv_ref, wq_ref, attn_ref, grad_ref,
    to_sib, from_sib, sums, land, kland, ksum, send, recv,
):
    reader, blk, z, x, core, xh, y = place()
    zp, zm, xn, sib, yp, ym, xp = neighbours()
    links = Links(send, recv, sib)
    at = blocks()
    y_m, y_p, y_2 = lax.rem(y + 3, 4), lax.rem(y + 1, 4), lax.rem(y + 2, 4)
    order = [(2, 1), (1, 1), (3, 1), (2, 0), (0, 1), (1, 0), (3, 0), (0, 0)]
    part = lambda c: pl.ds(c * D, D)
    parts = [(i, c) for i in range(8) for c in range(2)]
    parts = [(0, 0), (1, 0), (2, 0), (0, 1), (1, 1), (2, 1)] + parts[6:]

    barrier = pltpu.get_barrier_semaphore()
    for device in (zp, zm, xn, sib, yp, ym, xp):
        pl.semaphore_signal(barrier, inc=1, device_id=device, device_id_type=MESH)
    for i, c in parts[:6]:
        to_sib[i, c] = p_ref[at(*order[i], 1), part(c)].astype(BF16)
    pl.semaphore_wait(barrier, 7)
    for i, c in parts[:6]:
        links.start(40 + 2 * i + c, to_sib.at[i, c], from_sib.at[i, c], sib)
    links.start(0, kv_ref.at[y_2, 0], kland.at[0, 0], yp)
    links.start(1, kv_ref.at[y_2, 1], kland.at[0, 1], ym)
    links.start(2, kv_ref.at[y_p, 1], kland.at[1, 1], yp)
    links.start(3, kv_ref.at[y_m, 0], kland.at[2, 0], ym)
    for i, c in parts[6:]:
        to_sib[i, c] = p_ref[at(*order[i], 1), part(c)].astype(BF16)
        links.start(40 + 2 * i + c, to_sib.at[i, c], from_sib.at[i, c], sib)

    def both(i, c):
        links.arrive(40 + 2 * i + c, from_sib.at[i, c])
        return p_ref[at(*order[i]), part(c)] + from_sib[i, c].astype(F32)

    def put(channel, i, c, value, slot, device):
        sums[i, c] = value.astype(BF16)
        links.start(channel, sums.at[i, c], land.at[slot, c], device)

    def landed(channel, slot, c):
        links.arrive(channel, land.at[slot, c])
        return land[slot, c].astype(F32)

    for c in range(2):
        put(10 + c, 0, c, both(0, c), 0, xn)
        put(12 + c, 1, c, both(1, c), 1, zp)
        put(14 + c, 2, c, both(2, c), 2, zm)
    far = [both(3, c) for c in range(2)]
    put(16, 3, 0, far[0] + landed(10, 0, 0), 6, zp)

    links.arrive(0, kland.at[0, 0])
    ksum[0] = (kv_ref[y_p, 0].astype(F32) + kland[0, 0].astype(F32)).astype(BF16)
    links.start(4, ksum.at[0], kland.at[1, 0], yp)
    links.arrive(1, kland.at[0, 1])
    ksum[1] = (kv_ref[y_m, 1].astype(F32) + kland[0, 1].astype(F32)).astype(BF16)
    links.start(5, ksum.at[1], kland.at[2, 1], ym)

    put(18, 4, 0, both(4, 0) + landed(12, 1, 0) + landed(14, 2, 0), 3, xn)
    put(17, 3, 1, far[1] + landed(11, 0, 1), 6, zm)
    put(21, 5, 1, both(5, 1), 4, zp)
    put(22, 6, 0, both(6, 0), 5, zm)
    put(19, 4, 1, both(4, 1) + landed(13, 1, 1) + landed(15, 2, 1), 3, xn)

    up, down = both(5, 0), both(6, 1)
    put(20, 5, 0, up + landed(16, 6, 0), 4, zp)
    put(23, 6, 1, down + landed(17, 6, 1), 5, zm)

    links.arrive(4, kland.at[1, 0])
    links.arrive(2, kland.at[1, 1])
    links.arrive(3, kland.at[2, 0])
    links.arrive(5, kland.at[2, 1])
    ksum[2] = (
        kv_ref[y, 1 - xh].astype(F32) + kland[1, 1 - xh].astype(F32) + kland[2, 1 - xh].astype(F32)
    ).astype(BF16)
    links.start(6, ksum.at[2], ksum.at[3], xp)
    nodes = kv_ref[y, xh].astype(F32) + kland[1, xh].astype(F32) + kland[2, xh].astype(F32)

    outputs = both(7, 0) + landed(18, 3, 0)
    queries = both(7, 1) + landed(19, 3, 1)
    links.arrive(6, ksum.at[3])
    nodes += ksum[3].astype(F32)
    outputs += landed(22, 5, 0)
    queries += landed(21, 4, 1)
    outputs += landed(20, 4, 0)
    attn_ref[...] = outputs.T.astype(BF16)
    queries += landed(23, 5, 1)
    nodes += dot(wq_ref[...], (queries * SCALE).astype(BF16)).T
    grad_ref[...] = nodes.astype(BF16)
    links.finish()


def reduce(parts, key_parts, w_query):
    vmem = pl.BlockSpec(memory_space=VMEM)
    block = (2, D, BLOCK)
    return pl.pallas_call(
        reduce_kernel,
        out_shape=[jax.ShapeDtypeStruct((BLOCK, D), BF16)] * 2,
        in_specs=[vmem] * 3,
        out_specs=[vmem] * 2,
        scratch_shapes=[
            VMEM((8, *block), BF16),
            VMEM((8, *block), BF16),
            VMEM((7, *block), BF16),
            VMEM((7, *block), BF16),
            VMEM((3, 2, BLOCK, D), BF16),
            VMEM((4, BLOCK, D), BF16),
            pltpu.SemaphoreType.DMA((56,)),
            pltpu.SemaphoreType.DMA((56,)),
        ],
        compiler_params=pltpu.CompilerParams(
            collective_id=2, has_side_effects=True, vmem_limit_bytes=24 * 2**20
        ),
        name="reduce",
    )(parts, key_parts, w_query)


def local(features, cotangent, w_query, w_key, w_value, tile_coords, tile_count, mask_table):
    masks = mask_table.transpose(0, 2, 1)
    coords = tile_coords.transpose(0, 3, 1, 2)
    qt, gt, qn, gn, keys, values, keys_t, values_t, masks, wq, wkt, wvt = gather(
        features, cotangent, w_query, w_key, w_value, masks
    )
    partial = stats(tile_count, coords, qt, gt, keys, values, masks)
    fin, acc, kacc, vacc = merge(partial, keys.shape[0])
    arrays = (qt, gt, qn, gn, keys, values, keys_t, values_t, masks, fin, wkt, wvt)
    parts, key_parts = grads(tile_count, coords, arrays, acc, kacc, vacc)
    return tuple(reduce(parts, key_parts, wq))


def solution(mesh):
    return jax.shard_map(
        local,
        mesh=mesh,
        in_specs=(
            P(("reader", "blk"), None),
            P(("reader", "blk"), None),
            P(),
            P(),
            P(),
            P("reader", "blk", None, None),
            P("reader", "blk"),
            P(),
        ),
        out_specs=(P(("reader", "blk"), None), P(("reader", "blk"), None)),
        check_vma=False,
    )
```

```python
import functools

import jax
import jax.numpy as jnp
from jax import lax
from jax.experimental import pallas as pl
from jax.experimental.pallas import tpu as pltpu
from jax.sharding import PartitionSpec as P

HEADS = 8
HEAD_DIM = 64
D = 512
BLOCK = 128
SCALE = 0.125
FLOOR = -1e20
NEG_FILL = -1e30
MESH = pl.DeviceIdType.MESH
F32 = jnp.float32
BF16 = jnp.bfloat16
VMEM = pltpu.VMEM


def dot(a, b):
    return jnp.dot(a, b, preferred_element_type=F32)


def remote(src, dst, send, recv, device):
    return pltpu.make_async_remote_copy(
        src_ref=src, dst_ref=dst, send_sem=send, recv_sem=recv, device_id=device, device_id_type=MESH
    )


class Links:
    def __init__(self, send, recv, self_device):
        self.send, self.recv, self.anyone, self.started = send, recv, self_device, {}

    def start(self, i, src, dst, device):
        copy = remote(src, dst, self.send.at[i], self.recv.at[i], device)
        self.started[i] = copy
        copy.start()

    def arrive(self, i, dst):
        remote(dst, dst, self.send.at[i], self.recv.at[i], self.anyone).wait_recv()

    def finish(self):
        for copy in self.started.values():
            copy.wait_send()


def place():
    reader, blk = lax.axis_index("reader"), lax.axis_index("blk")
    side = lax.rem(blk // 2, 2)
    return (reader // 4) * 2 + side, lax.rem(reader, 4), blk // 4, lax.rem(blk, 2), side


def device(x, y, z, core):
    return (x // 2) * 4 + y, z * 4 + lax.rem(x, 2) * 2 + core


def ahead(i, d):
    return lax.rem(i + d, 4)


def neighbours():
    x, y, z, core, _ = place()
    return (
        device(ahead(x, 1), y, z, core),
        device(ahead(x, 3), y, z, core),
        device(x, ahead(y, 1), z, core),
        device(x, ahead(y, 3), z, core),
        device(x, y, ahead(z, 1), core),
        device(x, y, ahead(z, 3), core),
        device(x, y, z, 1 - core),
    )


def enter():
    barrier = pltpu.get_barrier_semaphore()
    for one in neighbours():
        pl.semaphore_signal(barrier, inc=1, device_id=one, device_id_type=MESH)
    return lambda: pl.semaphore_wait(barrier, 7)


HALF = BLOCK // 2
QUARTER = HALF // 2


class HalfGather:
    def __init__(self, links, base, buf, source, first, second):
        self.links, self.base, self.buf, self.source = links, base, buf, source
        self.me1, self.up1, self.down1 = first
        self.me2, self.up2, self.down2 = second

    def piece(self, d1, d2):
        return self.buf.at[ahead(self.me2, d2), ahead(self.me1, d1)]

    def quarter(self, d1, q):
        return self.buf.at[self.me2, ahead(self.me1, d1), pl.ds(q * QUARTER, QUARTER)]

    def spread(self, d1, src=None):
        ref = self.piece(d1, 0)
        self.links.start(self.base + 4 + d1, ref if src is None else src, ref, self.up2)
        self.links.start(self.base + 8 + d1, ref if src is None else src, ref, self.down2)

    def own(self):
        ref = self.piece(0, 0)
        self.links.start(self.base, self.source, ref, self.up1)
        self.links.start(self.base + 1, self.source, ref, self.down1)
        self.spread(0, self.source)

    def near(self):
        self.links.arrive(self.base, self.piece(3, 0))
        self.links.start(self.base + 2, self.quarter(3, 0), self.quarter(3, 0), self.up1)
        self.spread(3)
        self.links.arrive(self.base + 1, self.piece(1, 0))
        self.links.start(self.base + 3, self.quarter(1, 1), self.quarter(1, 1), self.down1)
        self.spread(1)

    def far(self):
        self.links.arrive(self.base + 2, self.quarter(2, 0))
        self.links.arrive(self.base + 3, self.quarter(2, 1))
        self.spread(2)

    def relay(self, d1):
        up = d1 < 2
        ref = self.piece(d1, 3 if up else 1)
        self.links.arrive(self.base + (4 if up else 8) + d1, ref)
        self.links.start(self.base + 12 + d1, ref, ref, self.up2 if up else self.down2)

    def rest(self, up):
        for d1 in (3, 2) if up else (0, 1):
            self.links.arrive(self.base + (4 if up else 8) + d1, self.piece(d1, 3 if up else 1))

    def last(self):
        for d1 in (0, 3, 1, 2):
            self.links.arrive(self.base + 12 + d1, self.piece(d1, 2))


def gather_kernel(
    x_hbm, g_hbm, wq_hbm, wk_hbm, wv_hbm, mask_hbm, coords_hbm, count_ref,
    qt_ref, gt_ref, qn_ref, gn_ref, k_ref, v_ref, mask_ref, wq_ref, wk_ref, wv_ref, coords_own, coords_out, count_out,
    xb, low, high, count_buf, send, recv, local,
):
    x, y, z, core, side = place()
    xp, xm, yp, ym, zp, zm, sib = neighbours()
    links = Links(send, recv, sib)
    begin = enter()
    count_buf[...] = jnp.full(count_buf.shape, count_ref[0, 0], jnp.int32)
    loads = [
        pltpu.make_async_copy(src, dst, local.at[i])
        for i, (src, dst) in enumerate(
            [
                (x_hbm.at[pl.ds(0, HALF)], low.at[y, x]), (x_hbm.at[pl.ds(HALF, HALF)], high.at[x, y]),
                (wk_hbm, wk_ref), (wv_hbm, wv_ref), (x_hbm, xb.at[z, core]), (g_hbm, gn_ref.at[z, core]),
                (wq_hbm, wq_ref), (mask_hbm, mask_ref), (coords_hbm, coords_own),
            ]
        )
    ]
    for load in loads:
        load.start()
    rings = [
        HalfGather(links, 16, low, x_hbm.at[pl.ds(0, HALF)], (x, xp, xm), (y, yp, ym)),
        HalfGather(links, 32, high, x_hbm.at[pl.ds(HALF, HALF)], (y, yp, ym), (x, xp, xm)),
    ]
    begin()

    for ring in rings:
        ring.own()
    links.start(0, x_hbm, xb.at[z, core], zp)
    links.start(2, x_hbm, xb.at[z, core], zm)
    links.start(1, g_hbm, gn_ref.at[z, core], zp)
    links.start(3, g_hbm, gn_ref.at[z, core], zm)
    links.start(8, x_hbm, xb.at[z, core], sib)
    links.start(9, g_hbm, gn_ref.at[z, core], sib)
    other = device(x + 1 - 2 * side, y, z, core)
    links.start(6, coords_hbm, coords_out, other)
    links.start(7, count_buf, count_out, other)

    def arrive(i, ref, dz, c=core):
        links.arrive(i, ref.at[ahead(z, dz), c])

    def pass_on(i, ref, dz, to):
        block = ref.at[ahead(z, dz), core]
        links.start(i, block, block, to)

    def prepare(dz):
        b = ahead(z, dz)
        rows = xb[b].reshape(2 * BLOCK, D)
        q = (dot(rows, wq_ref[...]).astype(BF16).astype(F32) * SCALE).astype(BF16)
        for c in range(2):
            one = q[c * BLOCK : (c + 1) * BLOCK]
            qn_ref[b, c] = one
            qt_ref[b, c] = one.T
            gt_ref[b, c] = gn_ref[b, c].T

    def project(half, d):
        at = ahead(x if half else y, d)
        rows = (high if half else low)[at].reshape(4 * HALF, D)
        for weight, out in ((wk_ref, k_ref), (wv_ref, v_ref)):
            found = dot(rows, weight[...]).astype(BF16).reshape(4, HALF, D)
            if half:
                out[at, :, HALF:] = found
            else:
                out[:, at, :HALF] = found

    for i in range(7):
        loads[i].wait()
    for ring in rings:
        ring.near()
    for ring in rings:
        ring.relay(0)
    arrive(0, xb, 3)
    pass_on(4, xb, 3, zp)
    for ring in rings:
        ring.far()
    for ring in rings:
        ring.relay(3)
        ring.relay(1)
    pass_on(10, xb, 3, sib)
    arrive(2, xb, 1)
    pass_on(12, xb, 1, sib)
    project(0, 0)
    project(1, 0)

    arrive(3, gn_ref, 1)
    pass_on(5, gn_ref, 1, zm)
    pass_on(13, gn_ref, 1, sib)
    arrive(1, gn_ref, 3)
    pass_on(11, gn_ref, 3, sib)
    for ring in rings:
        ring.relay(2)
    arrive(8, xb, 0, 1 - core)
    arrive(9, gn_ref, 0, 1 - core)
    prepare(0)
    for half, ring in enumerate(rings):
        ring.rest(True)
        project(half, 3)
        ring.rest(False)
        project(half, 1)
    arrive(4, xb, 2)
    pass_on(14, xb, 2, sib)
    for i, dz in ((10, 3), (12, 1)):
        arrive(i, xb, dz, 1 - core)
        arrive(i + 1, gn_ref, dz, 1 - core)
        prepare(dz)
        if i == 10:
            arrive(5, gn_ref, 2)
            pass_on(15, gn_ref, 2, sib)
    for half, ring in enumerate(rings):
        ring.last()
        project(half, 2)
    arrive(14, xb, 2, 1 - core)
    arrive(15, gn_ref, 2, 1 - core)
    prepare(2)
    links.arrive(6, coords_out)
    links.arrive(7, count_out)
    loads[7].wait()
    loads[8].wait()
    links.finish()


def gather(features, cotangent, w_query, w_key, w_value, masks, coords, count):
    hbm, vmem = pl.BlockSpec(memory_space=pltpu.HBM), pl.BlockSpec(memory_space=VMEM)
    operands = (features, cotangent, w_query, w_key, w_value, masks, coords)
    return pl.pallas_call(
        gather_kernel,
        out_shape=[
            VMEM((4, 2, D, BLOCK), BF16),
            VMEM((4, 2, D, BLOCK), BF16),
            VMEM((4, 2, BLOCK, D), BF16),
            VMEM((4, 2, BLOCK, D), BF16),
            VMEM((4, 4, BLOCK, D), BF16),
            VMEM((4, 4, BLOCK, D), BF16),
            VMEM(masks.shape, jnp.int32),
            VMEM((D, D), BF16),
            VMEM((D, D), BF16),
            VMEM((D, D), BF16),
            VMEM(coords.shape, jnp.int32),
            VMEM(coords.shape, jnp.int32),
            VMEM((8, 128), jnp.int32),
        ],
        in_specs=[hbm] * 7 + [pl.BlockSpec(memory_space=pltpu.SMEM)],
        out_specs=[vmem] * 13,
        scratch_shapes=[
            VMEM((4, 2, BLOCK, D), BF16),
            VMEM((4, 4, HALF, D), BF16),
            VMEM((4, 4, HALF, D), BF16),
            VMEM((8, 128), jnp.int32),
            pltpu.SemaphoreType.DMA((48,)),
            pltpu.SemaphoreType.DMA((48,)),
            pltpu.SemaphoreType.DMA((9,)),
        ],
        compiler_params=pltpu.CompilerParams(
            collective_id=0, has_side_effects=True, vmem_limit_bytes=16 * 2**20
        ),
        name="gather",
    )(*(pltpu.with_memory_space_constraint(a, pltpu.HBM) for a in operands), count)


def tile_bias(words, first, used):
    spread = jnp.concatenate(
        [jnp.broadcast_to(words[w : w + 1], (32, BLOCK)) for w in range(BLOCK // 32)], axis=0
    )
    key = lax.broadcasted_iota(jnp.int32, (BLOCK, BLOCK), 0)
    query = lax.broadcasted_iota(jnp.int32, (BLOCK, BLOCK), 1)
    bits = (lax.shift_right_logical(spread, key & 31) | jnp.where(key == query, first, 0)) & used
    return jnp.where(bits > 0, 0.0, NEG_FILL).astype(F32)


def pair_product(left, right):
    zero = jnp.zeros((HEAD_DIM, BLOCK), right.dtype)
    top = jnp.concatenate([right[:HEAD_DIM], zero], axis=1)
    bottom = jnp.concatenate([zero, right[HEAD_DIM:]], axis=1)
    return dot(left, jnp.concatenate([top, bottom], axis=0))


UNROLL = 4
LIST = 2 * 32 + UNROLL


def stats_kernel(
    count_ref, coords_ref, count2_ref, coords2_ref, qt_ref, gt_ref, k_ref, v_ref, mask_ref, out_ref, list_ref, run
):
    nb = run.shape[0]
    row = lax.broadcasted_iota(jnp.int32, run.shape, 1)
    run[...] = jnp.where(row < HEADS, FLOOR, 0.0).astype(F32)
    side = lax.rem(lax.axis_index("blk") // 2, 2)

    def collect(counts, coords, column, found):
        def one(i, found):
            qb, kb, p = (coords[0, c, 0, i] for c in range(3))
            list_ref[0, found] = lax.shift_right_logical(qb, 2) * 2 + (qb & 1)
            list_ref[1, found] = (lax.shift_right_logical(kb, 2) * 2 + column) * 4 + (kb & 3)
            list_ref[2, found] = p
            list_ref[3, found] = jnp.where(i + found + (column != side) == 0, 1, 0)
            list_ref[4, found] = 1
            return found + jnp.where((lax.shift_right_logical(qb, 1) & 1) == side, 1, 0)

        return lax.fori_loop(0, counts[0, 0], one, found)

    count = collect(count_ref, coords_ref, side, 0)
    count = collect(count2_ref, coords2_ref, 1 - side, count)
    for u in range(UNROLL):
        for i in range(5):
            list_ref[i, count + u] = 0
    list_ref[5, 0] = count

    def tile(t):
        qb, kb, p = (list_ref[c, t] for c in range(3))
        bias = tile_bias(mask_ref[p], list_ref[3, t], list_ref[4, t])
        peaks, totals, dots = [], [], []
        for pair in range(HEADS // 2):
            two = slice(pair * 128, pair * 128 + 128)
            s2 = pair_product(k_ref[kb, :, two], qt_ref[qb, two])
            d2 = pair_product(v_ref[kb, :, two], gt_ref[qb, two])
            for half in range(2):
                lanes = slice(half * BLOCK, (half + 1) * BLOCK)
                s = s2[:, lanes] + bias
                peak = jnp.max(s, axis=0, keepdims=True)
                e = jnp.exp(s - peak)
                peaks.append(peak)
                totals.append(jnp.sum(e, axis=0, keepdims=True))
                dots.append(jnp.sum(e * d2[:, lanes], axis=0, keepdims=True))
        return qb, *(jnp.concatenate(rows, axis=0) for rows in (peaks, totals, dots))

    def add(qb, peak, total, dots):
        before = run[qb, :HEADS]
        m = jnp.maximum(before, peak)
        old, new = jnp.exp(before - m), jnp.exp(peak - m)
        run[qb, :HEADS] = m
        run[qb, HEADS : 2 * HEADS] = run[qb, HEADS : 2 * HEADS] * old + total * new
        run[qb, 2 * HEADS :] = run[qb, 2 * HEADS :] * old + dots * new

    def step(g, carry):
        for found in [tile(g * UNROLL + u) for u in range(UNROLL)]:
            add(*found)
        return carry

    lax.fori_loop(0, (count + UNROLL - 1) // UNROLL, step, 0)
    for b in range(nb):
        total = jnp.maximum(run[b, HEADS : 2 * HEADS], 1e-30)
        out_ref[b, :HEADS] = run[b, :HEADS] + jnp.log(total)
        out_ref[b, HEADS:] = run[b, 2 * HEADS :] / total


def stats(count, coords, count2, coords2, qt, gt, keys, values, masks):
    nb = qt.shape[0]
    smem, vmem = pl.BlockSpec(memory_space=pltpu.SMEM), pl.BlockSpec(memory_space=VMEM)
    return pl.pallas_call(
        stats_kernel,
        out_shape=[VMEM((nb, 2 * HEADS, BLOCK), F32), jax.ShapeDtypeStruct((8, LIST), jnp.int32)],
        in_specs=[smem] * 4 + [vmem] * 5,
        out_specs=[vmem, smem],
        scratch_shapes=[VMEM((nb, 3 * HEADS, BLOCK), F32)],
        compiler_params=pltpu.CompilerParams(vmem_limit_bytes=8 * 2**20),
        name="stats",
    )(count, coords, count2, coords2, qt, gt, keys, values, masks)


def merge_kernel(
    st_ref, k_ref, v_ref, wk_ref, wv_ref, out_ref, acc, kacc, vacc, kt_ref, vt_ref, wkt_ref, wvt_ref,
    land, fin, send, recv, fsend, frecv,
):
    x, y, z, core, _ = place()
    nb = st_ref.shape[0]
    me = z * 2 + core
    block = lambda d: lax.rem(me + d, nb)
    peer = lambda d: device(x, y, block(d) // 2, lax.rem(block(d), 2))
    source = lambda d: lax.rem(me + nb - d, nb)
    barrier = pltpu.get_barrier_semaphore()
    for d in range(1, nb):
        pl.semaphore_signal(barrier, inc=1, device_id=peer(d), device_id_type=MESH)

    def part(d):
        return remote(st_ref.at[block(d)], land.at[d], send.at[d], recv.at[d], peer(d))

    def whole(d):
        return remote(fin.at[0], fin.at[d], fsend.at[d], frecv.at[d], peer(d))

    def turn(b, carry):
        kt_ref[b] = k_ref[b].T
        vt_ref[b] = v_ref[b].T
        return carry

    def clear(b, carry):
        kacc[b] = jnp.zeros(kacc.shape[1:], F32)
        vacc[b] = jnp.zeros(vacc.shape[1:], F32)
        return carry

    def clear_queries(b, carry):
        acc[b] = jnp.zeros(acc.shape[1:], F32)
        return carry

    wkt_ref[...] = wk_ref[...].T
    wvt_ref[...] = wv_ref[...].T
    pl.semaphore_wait(barrier, nb - 1)
    for d in range(1, nb):
        part(d).start()
    land[0] = st_ref[me]
    lax.fori_loop(0, 16, turn, 0)
    for d in range(1, nb):
        part(d).wait()
    m = land[0, :HEADS]
    for d in range(1, nb):
        m = jnp.maximum(m, land[d, :HEADS])
    total = jnp.zeros_like(m)
    dots = jnp.zeros_like(m)
    for d in range(nb):
        weight = jnp.exp(land[d, :HEADS] - m)
        total += weight
        dots += land[d, HEADS:] * weight
    fin[0, :HEADS] = m + jnp.log(total)
    fin[0, HEADS:] = dots / total
    for d in range(1, nb):
        whole(d).start()
    out_ref[me] = fin[0]
    lax.fori_loop(0, 16, clear, 0)
    lax.fori_loop(0, nb, clear_queries, 0)
    for d in range(1, nb):
        whole(d).wait()
        out_ref[source(d)] = fin[d]


def merge(partial, keys, values, wk, wv):
    nb, nk = partial.shape[0], keys.shape[0]
    vmem = pl.BlockSpec(memory_space=VMEM)
    return pl.pallas_call(
        merge_kernel,
        out_shape=[
            VMEM(partial.shape, F32),
            VMEM((nb, 2 * D, BLOCK), F32),
            VMEM((nk, BLOCK, D), F32),
            VMEM((nk, BLOCK, D), F32),
            VMEM((nk, D, BLOCK), BF16),
            VMEM((nk, D, BLOCK), BF16),
            VMEM((D, D), BF16),
            VMEM((D, D), BF16),
        ],
        in_specs=[vmem] * 5,
        out_specs=[vmem] * 8,
        scratch_shapes=[
            VMEM(partial.shape, F32),
            VMEM(partial.shape, F32),
            *[pltpu.SemaphoreType.DMA((nb,))] * 4,
        ],
        compiler_params=pltpu.CompilerParams(
            collective_id=1, has_side_effects=True, vmem_limit_bytes=4 * 2**20
        ),
        name="merge",
    )(partial, keys, values, wk, wv)


def lane_split(block):
    lane = lax.broadcasted_iota(jnp.int32, block.shape, 1)
    zero = jnp.zeros_like(block)
    return jnp.concatenate(
        [jnp.where(lane < HEAD_DIM, block, zero), jnp.where(lane >= HEAD_DIM, block, zero)], axis=0
    )


def grad_kernel(
    list_ref, qt_ref, gt_ref, qn_ref, gn_ref, k_ref, v_ref, kt_ref, vt_ref, mask_ref, fin_ref, wkt_ref,
    wvt_ref, acc_in, kacc_in, vacc_in, acc, kacc, vacc, low_ref, high_ref, probs, dscores,
):
    count = list_ref[5, 0]

    def scores(t, u):
        qb, kb, p = (list_ref[c, t] for c in range(3))
        bias = tile_bias(mask_ref[p], list_ref[3, t], list_ref[4, t])
        for pair in range(HEADS // 2):
            two = slice(pair * 128, pair * 128 + 128)
            s2 = pair_product(k_ref[kb, :, two], qt_ref[qb, two])
            d2 = pair_product(v_ref[kb, :, two], gt_ref[qb, two])
            for half in range(2):
                h = pair * 2 + half
                lanes = slice(half * BLOCK, (half + 1) * BLOCK)
                prob = jnp.exp(s2[:, lanes] + bias - fin_ref[qb, h : h + 1])
                probs[u, h] = prob.astype(BF16)
                delta = fin_ref[qb, HEADS + h : HEADS + h + 1]
                dscores[u, h] = (prob * (d2[:, lanes] - delta)).astype(BF16)

    def products(t, u):
        qb, kb = list_ref[0, t], list_ref[1, t]
        for pair in range(HEADS // 2):
            for h in (2 * pair, 2 * pair + 1):
                head = slice(h * HEAD_DIM, (h + 1) * HEAD_DIM)
                ghead = slice(D + h * HEAD_DIM, D + (h + 1) * HEAD_DIM)
                acc[qb, head] += dot(vt_ref[kb, head], probs[u, h])
                acc[qb, ghead] += dot(kt_ref[kb, head], dscores[u, h])
            two = slice(pair * 128, pair * 128 + 128)
            low = jnp.concatenate([probs[u, 2 * pair], probs[u, 2 * pair + 1]], axis=1)
            ds = jnp.concatenate([dscores[u, 2 * pair], dscores[u, 2 * pair + 1]], axis=1)
            kacc[kb, :, two] += dot(ds, lane_split(qn_ref[qb, :, two]))
            vacc[kb, :, two] += dot(low, lane_split(gn_ref[qb, :, two]))

    def step(g, carry):
        for u in range(UNROLL):
            scores(g * UNROLL + u, u)
        for u in range(UNROLL):
            products(g * UNROLL + u, u)
        return carry

    lax.fori_loop(0, (count + UNROLL - 1) // UNROLL, step, 0)
    for x in range(4):
        rows = pl.ds(x * 4, 4)
        keys = kacc[rows].reshape(4 * BLOCK, D).astype(BF16)
        values = vacc[rows].reshape(4 * BLOCK, D).astype(BF16)
        total = (dot(keys, wkt_ref[...]) + dot(values, wvt_ref[...])).reshape(4, BLOCK, D).astype(BF16)
        low_ref[:, x] = total[:, :HALF]
        high_ref[x] = total[:, HALF:]


def grads(tiles, arrays, acc, kacc, vacc):
    smem, vmem = pl.BlockSpec(memory_space=pltpu.SMEM), pl.BlockSpec(memory_space=VMEM)
    first = 1 + len(arrays)
    out = pl.pallas_call(
        grad_kernel,
        out_shape=[
            VMEM(acc.shape, F32),
            VMEM(kacc.shape, F32),
            VMEM(vacc.shape, F32),
            VMEM((4, 4, HALF, D), BF16),
            VMEM((4, 4, HALF, D), BF16),
        ],
        in_specs=[smem] + [vmem] * (len(arrays) + 3),
        out_specs=[vmem] * 5,
        scratch_shapes=[VMEM((UNROLL, HEADS, BLOCK, BLOCK), BF16)] * 2,
        input_output_aliases={first: 0, first + 1: 1, first + 2: 2},
        compiler_params=pltpu.CompilerParams(vmem_limit_bytes=12 * 2**20),
        name="grads",
    )(tiles, *arrays, acc, kacc, vacc)
    return out[0], out[3], out[4]


class HalfReduce:
    def __init__(self, links, base, buf, land, quarters, out, first, second):
        self.links, self.base, self.buf, self.land, self.quarters, self.out = links, base, buf, land, quarters, out
        self.me1, self.up1, self.down1 = first
        self.me2, self.up2, self.down2 = second

    def at(self, d1, d2):
        return ahead(self.me2, d2), ahead(self.me1, d1)

    def send(self, d1, d2, channel, src, to):
        self.links.start(self.base + channel, src, self.land.at[channel], to)

    def landed(self, channel):
        self.links.arrive(self.base + channel, self.land.at[channel])
        return self.land[channel].astype(F32)

    def own(self):
        for d1 in range(4):
            self.send(d1, 2, 12 + d1, self.buf.at[self.at(d1, 2)], self.up2 if d1 < 2 else self.down2)
        for d1 in range(4):
            up = d1 >= 2
            d2, channel = (1, 4 + d1) if up else (3, 8 + d1)
            self.send(d1, d2, channel, self.buf.at[self.at(d1, d2)], self.up2 if up else self.down2)

    def middle(self):
        for d1 in (2, 0, 3, 1):
            up = d1 < 2
            d2, channel = (1, 4 + d1) if up else (3, 8 + d1)
            total = self.buf[self.at(d1, d2)].astype(F32) + self.landed(12 + d1)
            self.out[d1] = total.astype(BF16)
            self.send(d1, d2, channel, self.out.at[d1], self.up2 if up else self.down2)

    def row(self, d1):
        return self.buf[self.at(d1, 0)].astype(F32) + self.landed(4 + d1) + self.landed(8 + d1)

    def cross(self):
        self.out[4] = self.row(2).astype(BF16)
        for q, to in ((0, self.up1), (1, self.down1)):
            rows = pl.ds(q * QUARTER, QUARTER)
            self.links.start(self.base + 2 + q, self.out.at[4, rows], self.quarters.at[rows], to)

    def finals(self):
        up, down = self.row(1), self.row(3)
        self.links.arrive(self.base + 2, self.quarters.at[pl.ds(0, QUARTER)])
        self.out[5, :QUARTER] = (up[:QUARTER] + self.quarters[:QUARTER].astype(F32)).astype(BF16)
        self.out[5, QUARTER:] = up[QUARTER:].astype(BF16)
        self.send(1, 0, 0, self.out.at[5], self.up1)
        self.links.arrive(self.base + 3, self.quarters.at[pl.ds(QUARTER, QUARTER)])
        self.out[6, :QUARTER] = down[:QUARTER].astype(BF16)
        self.out[6, QUARTER:] = (down[QUARTER:] + self.quarters[QUARTER:].astype(F32)).astype(BF16)
        self.send(3, 0, 1, self.out.at[6], self.down1)

    def result(self):
        return self.row(0) + self.landed(0) + self.landed(1)


def reduce_kernel(
    p_ref, low_ref, high_ref, wq_ref, attn_ref, grad_ref,
    to_sib, from_sib, sums, land, kland, quarters, ksums, send, recv,
):
    x, y, z, core, _ = place()
    xp, xm, yp, ym, zp, zm, sib = neighbours()
    links = Links(send, recv, sib)
    begin = enter()
    order = [2, 1, 3, 0]
    part = lambda c: pl.ds(c * D, D)
    parts = [(0, 0), (0, 1), (1, 1), (2, 0), (1, 0), (2, 1), (3, 0), (3, 1)]
    rings = [
        HalfReduce(links, 16, low_ref, kland.at[0], quarters.at[0], ksums.at[0], (x, xp, xm), (y, yp, ym)),
        HalfReduce(links, 32, high_ref, kland.at[1], quarters.at[1], ksums.at[1], (y, yp, ym), (x, xp, xm)),
    ]

    def block(i, c, mine):
        return p_ref[ahead(z, order[i]) * 2 + (core if mine else 1 - core), part(c)]

    for i, c in parts:
        to_sib[i, c] = block(i, c, False).astype(BF16)
    begin()
    for i, c in parts[:4]:
        links.start(8 + 2 * i + c, to_sib.at[i, c], from_sib.at[i, c], sib)
    for ring in rings:
        ring.own()
    for i, c in parts[4:]:
        links.start(8 + 2 * i + c, to_sib.at[i, c], from_sib.at[i, c], sib)

    def both(i, c):
        links.arrive(8 + 2 * i + c, from_sib.at[i, c])
        return block(i, c, True) + from_sib[i, c].astype(F32)

    def put(channel, i, c, value, to):
        sums[i, c] = value.astype(BF16)
        links.start(channel, sums.at[i, c], land.at[channel], to)

    def landed(channel):
        links.arrive(channel, land.at[channel])
        return land[channel].astype(F32)

    put(0, 0, 0, both(0, 0), zp)
    put(1, 0, 1, both(0, 1), zm)
    put(2, 1, 1, both(1, 1), zp)
    put(3, 2, 0, both(2, 0), zm)
    for ring in rings:
        ring.middle()
    up, down = both(1, 0), both(2, 1)
    put(4, 1, 0, up + landed(0), zp)
    put(5, 2, 1, down + landed(1), zm)
    for ring in rings:
        ring.cross()
    for ring in rings:
        ring.finals()
    outputs = both(3, 0) + landed(3) + landed(4)
    attn_ref[...] = outputs.T.astype(BF16)
    queries = both(3, 1) + landed(2) + landed(5)
    nodes = dot(wq_ref[...], (queries * SCALE).astype(BF16)).T
    for half, ring in enumerate(rings):
        rows = slice(half * HALF, (half + 1) * HALF)
        grad_ref[rows] = (nodes[rows] + ring.result()).astype(BF16)
    links.finish()


def reduce(parts, low, high, w_query):
    vmem = pl.BlockSpec(memory_space=VMEM)
    block = (2, D, BLOCK)
    return pl.pallas_call(
        reduce_kernel,
        out_shape=[jax.ShapeDtypeStruct((BLOCK, D), BF16)] * 2,
        in_specs=[vmem] * 4,
        out_specs=[vmem] * 2,
        scratch_shapes=[
            VMEM((4, *block), BF16),
            VMEM((4, *block), BF16),
            VMEM((3, *block), BF16),
            VMEM((6, D, BLOCK), BF16),
            VMEM((2, 16, HALF, D), BF16),
            VMEM((2, HALF, D), BF16),
            VMEM((2, 7, HALF, D), BF16),
            pltpu.SemaphoreType.DMA((48,)),
            pltpu.SemaphoreType.DMA((48,)),
        ],
        compiler_params=pltpu.CompilerParams(
            collective_id=2, has_side_effects=True, vmem_limit_bytes=24 * 2**20
        ),
        name="reduce",
    )(parts, low, high, w_query)


def local(features, cotangent, w_query, w_key, w_value, tile_coords, tile_count, mask_table):
    masks = mask_table.transpose(0, 2, 1)
    coords = tile_coords.transpose(0, 3, 1, 2)
    found = gather(features, cotangent, w_query, w_key, w_value, masks, coords, tile_count)
    qt, gt, qn, gn, keys, values = (a.reshape(-1, *a.shape[2:]) for a in found[:6])
    masks, wq, wk, wv, coords, coords2, count2 = found[6:]
    partial, tiles = stats(tile_count, coords, count2, coords2, qt, gt, keys, values, masks)
    fin, acc, kacc, vacc, keys_t, values_t, wkt, wvt = merge(partial, keys, values, wk, wv)
    arrays = (qt, gt, qn, gn, keys, values, keys_t, values_t, masks, fin, wkt, wvt)
    parts, low, high = grads(tiles, arrays, acc, kacc, vacc)
    return tuple(reduce(parts, low, high, wq))


def solution(mesh):
    return jax.shard_map(
        local,
        mesh=mesh,
        in_specs=(
            P(("reader", "blk"), None),
            P(("reader", "blk"), None),
            P(),
            P(),
            P(),
            P("reader", "blk", None, None),
            P("reader", "blk"),
            P(),
        ),
        out_specs=(P(("reader", "blk"), None), P(("reader", "blk"), None)),
        check_vma=False,
    )
```

```python
import functools

import jax
import jax.numpy as jnp
from jax import lax
from jax.experimental import pallas as pl
from jax.experimental.pallas import tpu as pltpu
from jax.sharding import PartitionSpec as P

HEADS = 8
HEAD_DIM = 64
D = 512
BLOCK = 128
SCALE = 0.125
FLOOR = -1e20
NEG_FILL = -1e30
MESH = pl.DeviceIdType.MESH
F32 = jnp.float32
BF16 = jnp.bfloat16
VMEM = pltpu.VMEM


def dot(a, b):
    return jnp.dot(a, b, preferred_element_type=F32)


def remote(src, dst, send, recv, device):
    return pltpu.make_async_remote_copy(
        src_ref=src, dst_ref=dst, send_sem=send, recv_sem=recv, device_id=device, device_id_type=MESH
    )


class Links:
    def __init__(self, send, recv, self_device):
        self.send, self.recv, self.anyone, self.started = send, recv, self_device, {}

    def start(self, i, src, dst, device):
        copy = remote(src, dst, self.send.at[i], self.recv.at[i], device)
        self.started[i] = copy
        copy.start()

    def arrive(self, i, dst):
        remote(dst, dst, self.send.at[i], self.recv.at[i], self.anyone).wait_recv()

    def finish(self):
        for copy in self.started.values():
            copy.wait_send()


def place():
    reader, blk = lax.axis_index("reader"), lax.axis_index("blk")
    side = lax.rem(blk // 2, 2)
    return (reader // 4) * 2 + side, lax.rem(reader, 4), blk // 4, lax.rem(blk, 2), side


def device(x, y, z, core):
    return (x // 2) * 4 + y, z * 4 + lax.rem(x, 2) * 2 + core


def ahead(i, d):
    return lax.rem(i + d, 4)


def neighbours():
    x, y, z, core, _ = place()
    return (
        device(ahead(x, 1), y, z, core),
        device(ahead(x, 3), y, z, core),
        device(x, ahead(y, 1), z, core),
        device(x, ahead(y, 3), z, core),
        device(x, y, ahead(z, 1), core),
        device(x, y, ahead(z, 3), core),
        device(x, y, z, 1 - core),
    )


def enter():
    barrier = pltpu.get_barrier_semaphore()
    for one in neighbours():
        pl.semaphore_signal(barrier, inc=1, device_id=one, device_id_type=MESH)
    return lambda: pl.semaphore_wait(barrier, 7)


HALF = BLOCK // 2
QUARTER = HALF // 2


class HalfGather:
    def __init__(self, links, base, buf, source, first, second):
        self.links, self.base, self.buf, self.source = links, base, buf, source
        self.me1, self.up1, self.down1 = first
        self.me2, self.up2, self.down2 = second

    def piece(self, d1, d2):
        return self.buf.at[ahead(self.me2, d2), ahead(self.me1, d1)]

    def quarter(self, d1, q):
        return self.buf.at[self.me2, ahead(self.me1, d1), pl.ds(q * QUARTER, QUARTER)]

    def spread(self, d1, src=None):
        ref = self.piece(d1, 0)
        self.links.start(self.base + 4 + d1, ref if src is None else src, ref, self.up2)
        self.links.start(self.base + 8 + d1, ref if src is None else src, ref, self.down2)

    def own(self):
        ref = self.piece(0, 0)
        self.links.start(self.base, self.source, ref, self.up1)
        self.links.start(self.base + 1, self.source, ref, self.down1)
        self.spread(0, self.source)

    def near(self):
        self.links.arrive(self.base, self.piece(3, 0))
        self.links.start(self.base + 2, self.quarter(3, 0), self.quarter(3, 0), self.up1)
        self.spread(3)
        self.links.arrive(self.base + 1, self.piece(1, 0))
        self.links.start(self.base + 3, self.quarter(1, 1), self.quarter(1, 1), self.down1)
        self.spread(1)

    def far(self):
        self.links.arrive(self.base + 2, self.quarter(2, 0))
        self.links.arrive(self.base + 3, self.quarter(2, 1))
        self.spread(2)

    def relay(self, d1):
        up = d1 < 2
        ref = self.piece(d1, 3 if up else 1)
        self.links.arrive(self.base + (4 if up else 8) + d1, ref)
        self.links.start(self.base + 12 + d1, ref, ref, self.up2 if up else self.down2)

    def rest(self, up):
        for d1 in (3, 2) if up else (0, 1):
            self.links.arrive(self.base + (4 if up else 8) + d1, self.piece(d1, 3 if up else 1))

    def last(self):
        for d1 in (0, 3, 1, 2):
            self.links.arrive(self.base + 12 + d1, self.piece(d1, 2))


def gather_kernel(
    x_hbm, g_hbm, wq_hbm, wk_hbm, wv_hbm, mask_hbm, coords_hbm, count_ref,
    qt_ref, gt_ref, qn_ref, gn_ref, k_ref, v_ref, mask_ref, wq_ref, wk_ref, wv_ref, coords_own, coords_out, count_out,
    xb, low, high, count_buf, send, recv, local,
):
    x, y, z, core, side = place()
    xp, xm, yp, ym, zp, zm, sib = neighbours()
    links = Links(send, recv, sib)
    begin = enter()
    count_buf[...] = jnp.full(count_buf.shape, count_ref[0, 0], jnp.int32)
    loads = [
        pltpu.make_async_copy(src, dst, local.at[i])
        for i, (src, dst) in enumerate(
            [
                (x_hbm.at[pl.ds(0, HALF)], low.at[y, x]), (x_hbm.at[pl.ds(HALF, HALF)], high.at[x, y]),
                (x_hbm, xb.at[z, core]), (g_hbm, gn_ref.at[z, core]), (wk_hbm, wk_ref), (wv_hbm, wv_ref),
                (wq_hbm, wq_ref), (mask_hbm, mask_ref), (coords_hbm, coords_own),
            ]
        )
    ]
    for load in loads:
        load.start()
    rings = [
        HalfGather(links, 16, low, low.at[y, x], (x, xp, xm), (y, yp, ym)),
        HalfGather(links, 32, high, high.at[x, y], (y, yp, ym), (x, xp, xm)),
    ]
    for i in range(4):
        loads[i].wait()
    begin()

    for ring in rings:
        ring.own()
    links.start(0, xb.at[z, core], xb.at[z, core], zp)
    links.start(2, xb.at[z, core], xb.at[z, core], zm)
    links.start(1, gn_ref.at[z, core], gn_ref.at[z, core], zp)
    links.start(3, gn_ref.at[z, core], gn_ref.at[z, core], zm)
    links.start(8, xb.at[z, core], xb.at[z, core], sib)
    links.start(9, gn_ref.at[z, core], gn_ref.at[z, core], sib)
    other = device(x + 1 - 2 * side, y, z, core)
    links.start(6, coords_hbm, coords_out, other)
    links.start(7, count_buf, count_out, other)

    def arrive(i, ref, dz, c=core):
        links.arrive(i, ref.at[ahead(z, dz), c])

    def pass_on(i, ref, dz, to):
        block = ref.at[ahead(z, dz), core]
        links.start(i, block, block, to)

    def prepare(dz):
        b = ahead(z, dz)
        rows = xb[b].reshape(2 * BLOCK, D)
        q = (dot(rows, wq_ref[...]).astype(BF16).astype(F32) * SCALE).astype(BF16)
        for c in range(2):
            one = q[c * BLOCK : (c + 1) * BLOCK]
            qn_ref[b, c] = one
            qt_ref[b, c] = one.T
            gt_ref[b, c] = gn_ref[b, c].T

    def project(half, d):
        at = ahead(x if half else y, d)
        rows = (high if half else low)[at].reshape(4 * HALF, D)
        for weight, out in ((wk_ref, k_ref), (wv_ref, v_ref)):
            found = dot(rows, weight[...]).astype(BF16).reshape(4, HALF, D)
            if half:
                out[at, :, HALF:] = found
            else:
                out[:, at, :HALF] = found

    for ring in rings:
        ring.near()
    for ring in rings:
        ring.relay(0)
    arrive(0, xb, 3)
    pass_on(4, xb, 3, zp)
    for ring in rings:
        ring.far()
    for ring in rings:
        ring.relay(3)
        ring.relay(1)
    pass_on(10, xb, 3, sib)
    arrive(2, xb, 1)
    pass_on(12, xb, 1, sib)
    for i in range(4, 7):
        loads[i].wait()
    project(0, 0)
    project(1, 0)

    arrive(3, gn_ref, 1)
    pass_on(5, gn_ref, 1, zm)
    pass_on(13, gn_ref, 1, sib)
    arrive(1, gn_ref, 3)
    pass_on(11, gn_ref, 3, sib)
    for ring in rings:
        ring.relay(2)
    arrive(8, xb, 0, 1 - core)
    arrive(9, gn_ref, 0, 1 - core)
    prepare(0)
    for half, ring in enumerate(rings):
        ring.rest(True)
        project(half, 3)
        ring.rest(False)
        project(half, 1)
    arrive(4, xb, 2)
    pass_on(14, xb, 2, sib)
    for i, dz in ((10, 3), (12, 1)):
        arrive(i, xb, dz, 1 - core)
        arrive(i + 1, gn_ref, dz, 1 - core)
        prepare(dz)
        if i == 10:
            arrive(5, gn_ref, 2)
            pass_on(15, gn_ref, 2, sib)
    for half, ring in enumerate(rings):
        ring.last()
        project(half, 2)
    arrive(14, xb, 2, 1 - core)
    arrive(15, gn_ref, 2, 1 - core)
    prepare(2)
    links.arrive(6, coords_out)
    links.arrive(7, count_out)
    loads[7].wait()
    loads[8].wait()
    links.finish()


def gather(features, cotangent, w_query, w_key, w_value, masks, coords, count):
    hbm, vmem = pl.BlockSpec(memory_space=pltpu.HBM), pl.BlockSpec(memory_space=VMEM)
    operands = (features, cotangent, w_query, w_key, w_value, masks, coords)
    return pl.pallas_call(
        gather_kernel,
        out_shape=[
            VMEM((4, 2, D, BLOCK), BF16),
            VMEM((4, 2, D, BLOCK), BF16),
            VMEM((4, 2, BLOCK, D), BF16),
            VMEM((4, 2, BLOCK, D), BF16),
            VMEM((4, 4, BLOCK, D), BF16),
            VMEM((4, 4, BLOCK, D), BF16),
            VMEM(masks.shape, jnp.int32),
            VMEM((D, D), BF16),
            VMEM((D, D), BF16),
            VMEM((D, D), BF16),
            VMEM(coords.shape, jnp.int32),
            VMEM(coords.shape, jnp.int32),
            VMEM((8, 128), jnp.int32),
        ],
        in_specs=[hbm] * 7 + [pl.BlockSpec(memory_space=pltpu.SMEM)],
        out_specs=[vmem] * 13,
        scratch_shapes=[
            VMEM((4, 2, BLOCK, D), BF16),
            VMEM((4, 4, HALF, D), BF16),
            VMEM((4, 4, HALF, D), BF16),
            VMEM((8, 128), jnp.int32),
            pltpu.SemaphoreType.DMA((48,)),
            pltpu.SemaphoreType.DMA((48,)),
            pltpu.SemaphoreType.DMA((9,)),
        ],
        compiler_params=pltpu.CompilerParams(
            collective_id=0, has_side_effects=True, vmem_limit_bytes=16 * 2**20
        ),
        name="gather",
    )(*(pltpu.with_memory_space_constraint(a, pltpu.HBM) for a in operands), count)


def tile_bias(words, first, used):
    spread = jnp.concatenate(
        [jnp.broadcast_to(words[w : w + 1], (32, BLOCK)) for w in range(BLOCK // 32)], axis=0
    )
    key = lax.broadcasted_iota(jnp.int32, (BLOCK, BLOCK), 0)
    query = lax.broadcasted_iota(jnp.int32, (BLOCK, BLOCK), 1)
    bits = (lax.shift_right_logical(spread, key & 31) | jnp.where(key == query, first, 0)) & used
    return jnp.where(bits > 0, 0.0, NEG_FILL).astype(F32)


def pair_product(left, right):
    zero = jnp.zeros((HEAD_DIM, BLOCK), right.dtype)
    top = jnp.concatenate([right[:HEAD_DIM], zero], axis=1)
    bottom = jnp.concatenate([zero, right[HEAD_DIM:]], axis=1)
    return dot(left, jnp.concatenate([top, bottom], axis=0))


UNROLL = 4
LIST = 2 * 32 + UNROLL
KEPT = 32


def unpacked(word):
    return word & 7, lax.shift_right_logical(word, 3) & 15, lax.shift_right_logical(word, 8), lax.shift_right_logical(word, 7) & 1


def stats_kernel(
    count_ref, coords_ref, count2_ref, coords2_ref, qt_ref, gt_ref, k_ref, v_ref, mask_ref,
    out_ref, list_ref, kept_e, kept_d, peaks_ref, run,
):
    nb = run.shape[0]
    row = lax.broadcasted_iota(jnp.int32, run.shape, 1)
    run[...] = jnp.where(row < HEADS, FLOOR, 0.0).astype(F32)
    side = lax.rem(lax.axis_index("blk") // 2, 2)

    def collect(counts, coords, column, found):
        def one(i, found):
            qb, kb, p = (coords[0, c, 0, i] for c in range(3))
            key = lax.shift_right_logical(kb, 2) * 8 + column * 4 + (kb & 3)
            first = jnp.where(i + found + (column != side) == 0, 128, 0)
            list_ref[found] = lax.shift_right_logical(qb, 2) * 2 + (qb & 1) + key * 8 + first + p * 256
            return found + jnp.where((lax.shift_right_logical(qb, 1) & 1) == side, 1, 0)

        return lax.fori_loop(0, counts[0, 0], one, found)

    count = collect(count_ref, coords_ref, side, 0)
    count = collect(count2_ref, coords2_ref, 1 - side, count)
    for u in range(UNROLL):
        list_ref[count + u] = 0
    list_ref[LIST] = count

    def tile(t):
        qb, kb, p, first = unpacked(list_ref[t])
        bias = tile_bias(mask_ref[p], first, jnp.where(t < count, 1, 0))
        slot = jnp.minimum(t, KEPT)
        peaks, totals, dots = [], [], []
        for pair in range(HEADS // 2):
            two = slice(pair * 128, pair * 128 + 128)
            s2 = pair_product(k_ref[kb, :, two], qt_ref[qb, two])
            d2 = pair_product(v_ref[kb, :, two], gt_ref[qb, two])
            for half in range(2):
                h = 2 * pair + half
                lanes = slice(half * BLOCK, (half + 1) * BLOCK)
                s = s2[:, lanes] + bias
                peak = jnp.max(s, axis=0, keepdims=True)
                e = jnp.exp(s - peak)
                kept_e[slot, h] = e.astype(BF16)
                kept_d[slot, h] = d2[:, lanes].astype(BF16)
                peaks.append(peak)
                totals.append(jnp.sum(e, axis=0, keepdims=True))
                dots.append(jnp.sum(e * d2[:, lanes], axis=0, keepdims=True))
        peak, total, dot_sum = (jnp.concatenate(rows, axis=0) for rows in (peaks, totals, dots))
        peaks_ref[slot] = peak
        return qb, peak, total, dot_sum

    def add(qb, peak, total, dots):
        before = run[qb, :HEADS]
        m = jnp.maximum(before, peak)
        old, new = jnp.exp(before - m), jnp.exp(peak - m)
        run[qb, :HEADS] = m
        run[qb, HEADS : 2 * HEADS] = run[qb, HEADS : 2 * HEADS] * old + total * new
        run[qb, 2 * HEADS :] = run[qb, 2 * HEADS :] * old + dots * new

    def step(g, carry):
        for found in [tile(g * UNROLL + u) for u in range(UNROLL)]:
            add(*found)
        return carry

    lax.fori_loop(0, (count + UNROLL - 1) // UNROLL, step, 0)
    for b in range(nb):
        total = jnp.maximum(run[b, HEADS : 2 * HEADS], 1e-30)
        out_ref[b, :HEADS] = run[b, :HEADS] + jnp.log(total)
        out_ref[b, HEADS:] = run[b, 2 * HEADS :] / total


def stats(count, coords, count2, coords2, qt, gt, keys, values, masks):
    nb = qt.shape[0]
    smem, vmem = pl.BlockSpec(memory_space=pltpu.SMEM), pl.BlockSpec(memory_space=VMEM)
    return pl.pallas_call(
        stats_kernel,
        out_shape=[
            VMEM((nb, 2 * HEADS, BLOCK), F32),
            jax.ShapeDtypeStruct((LIST + 1,), jnp.int32),
            VMEM((KEPT + 1, HEADS, BLOCK, BLOCK), BF16),
            VMEM((KEPT + 1, HEADS, BLOCK, BLOCK), BF16),
            VMEM((KEPT + 1, HEADS, BLOCK), F32),
        ],
        in_specs=[smem] * 4 + [vmem] * 5,
        out_specs=[vmem, smem, vmem, vmem, vmem],
        scratch_shapes=[VMEM((nb, 3 * HEADS, BLOCK), F32)],
        compiler_params=pltpu.CompilerParams(vmem_limit_bytes=4 * 2**20),
        name="stats",
    )(count, coords, count2, coords2, qt, gt, keys, values, masks)


def merge_kernel(
    st_ref, k_ref, v_ref, wk_ref, wv_ref, kept_e, kept_d, out_ref, acc, kacc, vacc, kt_ref, vt_ref, wkt_ref, wvt_ref,
    land, fin, send, recv, fsend, frecv,
):
    x, y, z, core, _ = place()
    nb = st_ref.shape[0]
    me = z * 2 + core
    block = lambda d: lax.rem(me + d, nb)
    peer = lambda d: device(x, y, block(d) // 2, lax.rem(block(d), 2))
    source = lambda d: lax.rem(me + nb - d, nb)
    barrier = pltpu.get_barrier_semaphore()
    for d in range(1, nb):
        pl.semaphore_signal(barrier, inc=1, device_id=peer(d), device_id_type=MESH)

    def part(d):
        return remote(st_ref.at[block(d)], land.at[d], send.at[d], recv.at[d], peer(d))

    def whole(d):
        return remote(fin.at[0], fin.at[d], fsend.at[d], frecv.at[d], peer(d))

    def turn(b, carry):
        kt_ref[b] = k_ref[b].T
        vt_ref[b] = v_ref[b].T
        return carry

    def clear(b, carry):
        kacc[b] = jnp.zeros(kacc.shape[1:], F32)
        vacc[b] = jnp.zeros(vacc.shape[1:], F32)
        return carry

    def clear_queries(b, carry):
        acc[b] = jnp.zeros(acc.shape[1:], F32)
        return carry

    wkt_ref[...] = wk_ref[...].T
    wvt_ref[...] = wv_ref[...].T
    pl.semaphore_wait(barrier, nb - 1)
    for d in range(1, nb):
        part(d).start()
    land[0] = st_ref[me]
    lax.fori_loop(0, 16, turn, 0)
    for d in range(1, nb):
        part(d).wait()
    m = land[0, :HEADS]
    for d in range(1, nb):
        m = jnp.maximum(m, land[d, :HEADS])
    total = jnp.zeros_like(m)
    dots = jnp.zeros_like(m)
    for d in range(nb):
        weight = jnp.exp(land[d, :HEADS] - m)
        total += weight
        dots += land[d, HEADS:] * weight
    fin[0, :HEADS] = m + jnp.log(total)
    fin[0, HEADS:] = dots / total
    for d in range(1, nb):
        whole(d).start()
    out_ref[me] = fin[0]
    lax.fori_loop(0, 16, clear, 0)
    lax.fori_loop(0, nb, clear_queries, 0)
    for d in range(1, nb):
        whole(d).wait()
        out_ref[source(d)] = fin[d]


def merge(partial, keys, values, wk, wv, kept_e, kept_d):
    nb, nk = partial.shape[0], keys.shape[0]
    vmem = pl.BlockSpec(memory_space=VMEM)
    return pl.pallas_call(
        merge_kernel,
        out_shape=[
            VMEM(partial.shape, F32),
            VMEM((nb, 2 * D, BLOCK), F32),
            VMEM((nk, BLOCK, D), F32),
            VMEM((nk, BLOCK, D), F32),
            VMEM((nk, D, BLOCK), BF16),
            VMEM((nk, D, BLOCK), BF16),
            VMEM((D, D), BF16),
            VMEM((D, D), BF16),
        ],
        in_specs=[vmem] * 7,
        out_specs=[vmem] * 8,
        scratch_shapes=[
            VMEM(partial.shape, F32),
            VMEM(partial.shape, F32),
            *[pltpu.SemaphoreType.DMA((nb,))] * 4,
        ],
        compiler_params=pltpu.CompilerParams(
            collective_id=1, has_side_effects=True, vmem_limit_bytes=4 * 2**20
        ),
        name="merge",
    )(partial, keys, values, wk, wv, *(pltpu.with_memory_space_constraint(a, pltpu.VMEM) for a in (kept_e, kept_d)))


def lane_split(block):
    lane = lax.broadcasted_iota(jnp.int32, block.shape, 1)
    zero = jnp.zeros_like(block)
    return jnp.concatenate(
        [jnp.where(lane < HEAD_DIM, block, zero), jnp.where(lane >= HEAD_DIM, block, zero)], axis=0
    )


def grad_kernel(
    list_ref, qt_ref, gt_ref, qn_ref, gn_ref, k_ref, v_ref, kt_ref, vt_ref, mask_ref, fin_ref,
    kept_e, kept_d, peaks_ref, acc_in, kacc_in, vacc_in, acc, kacc, vacc, probs, dscores,
):
    count = list_ref[LIST]

    def scores(t, u):
        qb, kb, p, first = unpacked(list_ref[t])
        bias = tile_bias(mask_ref[p], first, jnp.where(t < count, 1, 0))
        for pair in range(HEADS // 2):
            two = slice(pair * 128, pair * 128 + 128)
            s2 = pair_product(k_ref[kb, :, two], qt_ref[qb, two])
            d2 = pair_product(v_ref[kb, :, two], gt_ref[qb, two])
            for half in range(2):
                h = pair * 2 + half
                lanes = slice(half * BLOCK, (half + 1) * BLOCK)
                prob = jnp.exp(s2[:, lanes] + bias - fin_ref[qb, h : h + 1])
                probs[u, h] = prob.astype(BF16)
                delta = fin_ref[qb, HEADS + h : HEADS + h + 1]
                dscores[u, h] = (prob * (d2[:, lanes] - delta)).astype(BF16)

    def kept_scores(t, u):
        qb = unpacked(list_ref[t])[0]
        factor = jnp.exp(peaks_ref[t] - fin_ref[qb, :HEADS])
        for h in range(HEADS):
            prob = kept_e[t, h].astype(F32) * factor[h : h + 1]
            probs[u, h] = prob.astype(BF16)
            delta = fin_ref[qb, HEADS + h : HEADS + h + 1]
            dscores[u, h] = (prob * (kept_d[t, h].astype(F32) - delta)).astype(BF16)

    def products(t, u):
        qb, kb = unpacked(list_ref[t])[:2]
        for pair in range(HEADS // 2):
            for h in (2 * pair, 2 * pair + 1):
                head = slice(h * HEAD_DIM, (h + 1) * HEAD_DIM)
                ghead = slice(D + h * HEAD_DIM, D + (h + 1) * HEAD_DIM)
                acc[qb, head] += dot(vt_ref[kb, head], probs[u, h])
                acc[qb, ghead] += dot(kt_ref[kb, head], dscores[u, h])
            two = slice(pair * 128, pair * 128 + 128)
            low = jnp.concatenate([probs[u, 2 * pair], probs[u, 2 * pair + 1]], axis=1)
            ds = jnp.concatenate([dscores[u, 2 * pair], dscores[u, 2 * pair + 1]], axis=1)
            kacc[kb, :, two] += dot(ds, lane_split(qn_ref[qb, :, two]))
            vacc[kb, :, two] += dot(low, lane_split(gn_ref[qb, :, two]))

    def step(find, g, carry):
        for u in range(UNROLL):
            find(g * UNROLL + u, u)
        for u in range(UNROLL):
            products(g * UNROLL + u, u)
        return carry

    groups = (count + UNROLL - 1) // UNROLL
    kept = jnp.minimum(groups, KEPT // UNROLL)
    lax.fori_loop(0, kept, functools.partial(step, kept_scores), 0)
    lax.fori_loop(kept, groups, functools.partial(step, scores), 0)


def grads(tiles, arrays, acc, kacc, vacc):
    smem, vmem = pl.BlockSpec(memory_space=pltpu.SMEM), pl.BlockSpec(memory_space=VMEM)
    first = 1 + len(arrays)
    return pl.pallas_call(
        grad_kernel,
        out_shape=[
            VMEM(acc.shape, F32),
            VMEM(kacc.shape, F32),
            VMEM(vacc.shape, F32),
        ],
        in_specs=[smem] + [vmem] * (len(arrays) + 3),
        out_specs=[vmem] * 3,
        scratch_shapes=[VMEM((UNROLL, HEADS, BLOCK, BLOCK), BF16)] * 2,
        input_output_aliases={first: 0, first + 1: 1, first + 2: 2},
        compiler_params=pltpu.CompilerParams(vmem_limit_bytes=5 * 2**20),
        name="grads",
    )(tiles, *arrays, acc, kacc, vacc)


class HalfReduce:
    def __init__(self, links, base, buf, land, quarters, out, first, second):
        self.links, self.base, self.buf, self.land, self.quarters, self.out = links, base, buf, land, quarters, out
        self.me1, self.up1, self.down1 = first
        self.me2, self.up2, self.down2 = second

    def at(self, d1, d2):
        return ahead(self.me2, d2), ahead(self.me1, d1)

    def send(self, d1, d2, channel, src, to):
        self.links.start(self.base + channel, src, self.land.at[channel], to)

    def landed(self, channel):
        self.links.arrive(self.base + channel, self.land.at[channel])
        return self.land[channel].astype(F32)

    def first(self):
        for d1 in range(4):
            self.send(d1, 2, 12 + d1, self.buf.at[self.at(d1, 2)], self.up2 if d1 < 2 else self.down2)

    def second(self):
        for d1 in range(4):
            up = d1 >= 2
            d2, channel = (1, 4 + d1) if up else (3, 8 + d1)
            self.send(d1, d2, channel, self.buf.at[self.at(d1, d2)], self.up2 if up else self.down2)

    def middle(self):
        for d1 in (2, 0, 3, 1):
            up = d1 < 2
            d2, channel = (1, 4 + d1) if up else (3, 8 + d1)
            total = self.buf[self.at(d1, d2)].astype(F32) + self.landed(12 + d1)
            self.out[d1] = total.astype(BF16)
            self.send(d1, d2, channel, self.out.at[d1], self.up2 if up else self.down2)

    def row(self, d1):
        return self.buf[self.at(d1, 0)].astype(F32) + self.landed(4 + d1) + self.landed(8 + d1)

    def cross(self):
        self.out[4] = self.row(2).astype(BF16)
        for q, to in ((0, self.up1), (1, self.down1)):
            rows = pl.ds(q * QUARTER, QUARTER)
            self.links.start(self.base + 2 + q, self.out.at[4, rows], self.quarters.at[rows], to)

    def finals(self):
        up, down = self.row(1), self.row(3)
        self.links.arrive(self.base + 2, self.quarters.at[pl.ds(0, QUARTER)])
        self.out[5, :QUARTER] = (up[:QUARTER] + self.quarters[:QUARTER].astype(F32)).astype(BF16)
        self.out[5, QUARTER:] = up[QUARTER:].astype(BF16)
        self.send(1, 0, 0, self.out.at[5], self.up1)
        self.links.arrive(self.base + 3, self.quarters.at[pl.ds(QUARTER, QUARTER)])
        self.out[6, :QUARTER] = down[:QUARTER].astype(BF16)
        self.out[6, QUARTER:] = (down[QUARTER:] + self.quarters[QUARTER:].astype(F32)).astype(BF16)
        self.send(3, 0, 1, self.out.at[6], self.down1)

    def result(self):
        return self.row(0) + self.landed(0) + self.landed(1)


def reduce_kernel(
    p_ref, kacc, vacc, wkt_ref, wvt_ref, outputs_ref, queries_ref, nodes_ref,
    low, high, to_sib, from_sib, sums, land, kland, quarters, ksums, send, recv,
):
    x, y, z, core, _ = place()
    xp, xm, yp, ym, zp, zm, sib = neighbours()
    links = Links(send, recv, sib)
    begin = enter()
    order = [2, 1, 3, 0]
    part = lambda c: pl.ds(c * D, D)
    parts = [(0, 0), (0, 1), (1, 1), (2, 0), (1, 0), (2, 1), (3, 0), (3, 1)]
    rings = [
        HalfReduce(links, 16, low, kland.at[0], quarters.at[0], ksums.at[0], (x, xp, xm), (y, yp, ym)),
        HalfReduce(links, 32, high, kland.at[1], quarters.at[1], ksums.at[1], (y, yp, ym), (x, xp, xm)),
    ]

    def block(i, c, mine):
        return p_ref[ahead(z, order[i]) * 2 + (core if mine else 1 - core), part(c)]

    def weigh(half, d):
        at = ahead(x if half else y, d)
        total = 0.0
        for found, weight in ((kacc, wkt_ref), (vacc, wvt_ref)):
            rows = found[at, :, HALF:] if half else found[:, at, :HALF]
            total += dot(rows.reshape(4 * HALF, D).astype(BF16), weight[...])
        (high if half else low)[at] = total.reshape(4, HALF, D).astype(BF16)

    for i, c in parts[:4]:
        to_sib[i, c] = block(i, c, False).astype(BF16)
    weigh(0, 2)
    begin()
    for i, c in parts[:4]:
        links.start(8 + 2 * i + c, to_sib.at[i, c], from_sib.at[i, c], sib)
    rings[0].first()
    weigh(1, 2)
    rings[1].first()
    for i, c in parts[4:]:
        to_sib[i, c] = block(i, c, False).astype(BF16)
        links.start(8 + 2 * i + c, to_sib.at[i, c], from_sib.at[i, c], sib)

    def both(i, c):
        links.arrive(8 + 2 * i + c, from_sib.at[i, c])
        return block(i, c, True) + from_sib[i, c].astype(F32)

    def put(channel, i, c, value, to):
        sums[i, c] = value.astype(BF16)
        links.start(channel, sums.at[i, c], land.at[channel], to)

    def landed(channel):
        links.arrive(channel, land.at[channel])
        return land[channel].astype(F32)

    put(0, 0, 0, both(0, 0), zp)
    put(1, 0, 1, both(0, 1), zm)
    put(2, 1, 1, both(1, 1), zp)
    put(3, 2, 0, both(2, 0), zm)
    for half, ring in enumerate(rings):
        weigh(half, 1)
        weigh(half, 3)
        ring.second()
    for ring in rings:
        ring.middle()
    weigh(0, 0)
    weigh(1, 0)
    up, down = both(1, 0), both(2, 1)
    put(4, 1, 0, up + landed(0), zp)
    put(5, 2, 1, down + landed(1), zm)
    for ring in rings:
        ring.cross()
    for ring in rings:
        ring.finals()
    outputs_ref[...] = both(3, 0) + landed(3) + landed(4)
    queries_ref[...] = ((both(3, 1) + landed(2) + landed(5)) * SCALE).astype(BF16)
    for half, ring in enumerate(rings):
        nodes_ref[half * HALF : (half + 1) * HALF] = ring.result()
    links.finish()


def reduce(parts, kacc, vacc, wkt, wvt):
    vmem = pl.BlockSpec(memory_space=VMEM)
    block = (2, D, BLOCK)
    return pl.pallas_call(
        reduce_kernel,
        out_shape=[VMEM((D, BLOCK), F32), VMEM((D, BLOCK), BF16), VMEM((BLOCK, D), F32)],
        in_specs=[vmem] * 5,
        out_specs=[vmem] * 3,
        scratch_shapes=[
            VMEM((4, 4, HALF, D), BF16),
            VMEM((4, 4, HALF, D), BF16),
            VMEM((4, *block), BF16),
            VMEM((4, *block), BF16),
            VMEM((3, *block), BF16),
            VMEM((6, D, BLOCK), BF16),
            VMEM((2, 16, HALF, D), BF16),
            VMEM((2, HALF, D), BF16),
            VMEM((2, 7, HALF, D), BF16),
            pltpu.SemaphoreType.DMA((48,)),
            pltpu.SemaphoreType.DMA((48,)),
        ],
        compiler_params=pltpu.CompilerParams(
            collective_id=2, has_side_effects=True, vmem_limit_bytes=24 * 2**20
        ),
        name="reduce",
    )(parts, kacc.reshape(4, 4, BLOCK, D), vacc.reshape(4, 4, BLOCK, D), wkt, wvt)


def finish_kernel(outputs_ref, queries_ref, nodes_ref, wq_ref, attn_ref, grad_ref):
    attn_ref[...] = outputs_ref[...].T.astype(BF16)
    grad_ref[...] = (dot(wq_ref[...], queries_ref[...]).T + nodes_ref[...]).astype(BF16)


def finish(outputs, queries, nodes, w_query):
    vmem = pl.BlockSpec(memory_space=VMEM)
    return pl.pallas_call(
        finish_kernel,
        out_shape=[jax.ShapeDtypeStruct((BLOCK, D), BF16)] * 2,
        in_specs=[vmem] * 4,
        out_specs=[vmem] * 2,
        compiler_params=pltpu.CompilerParams(vmem_limit_bytes=8 * 2**20),
        name="finish",
    )(outputs, queries, nodes, w_query)


def local(features, cotangent, w_query, w_key, w_value, tile_coords, tile_count, mask_table):
    masks = mask_table.transpose(0, 2, 1)
    coords = tile_coords.transpose(0, 3, 1, 2)
    found = gather(features, cotangent, w_query, w_key, w_value, masks, coords, tile_count)
    qt, gt, qn, gn, keys, values = (a.reshape(-1, *a.shape[2:]) for a in found[:6])
    masks, wq, wk, wv, coords, coords2, count2 = found[6:]
    partial, tiles, *kept = stats(tile_count, coords, count2, coords2, qt, gt, keys, values, masks)
    fin, acc, kacc, vacc, keys_t, values_t, wkt, wvt = merge(partial, keys, values, wk, wv, *kept[:2])
    arrays = (qt, gt, qn, gn, keys, values, keys_t, values_t, masks, fin, *kept)
    parts, kacc, vacc = grads(tiles, arrays, acc, kacc, vacc)
    return tuple(finish(*reduce(parts, kacc, vacc, wkt, wvt), wq))


def solution(mesh):
    return jax.shard_map(
        local,
        mesh=mesh,
        in_specs=(
            P(("reader", "blk"), None),
            P(("reader", "blk"), None),
            P(),
            P(),
            P(),
            P("reader", "blk", None, None),
            P("reader", "blk"),
            P(),
        ),
        out_specs=(P(("reader", "blk"), None), P(("reader", "blk"), None)),
        check_vma=False,
    )
```

```python
import functools

import jax
import jax.numpy as jnp
from jax import lax
from jax.experimental import pallas as pl
from jax.experimental.pallas import tpu as pltpu
from jax.sharding import PartitionSpec as P

HEADS = 8
HEAD_DIM = 64
D = 512
BLOCK = 128
SCALE = 0.125
FLOOR = -1e20
NEG_FILL = -1e30
MESH = pl.DeviceIdType.MESH
F32 = jnp.float32
BF16 = jnp.bfloat16
VMEM = pltpu.VMEM


def dot(a, b):
    return jnp.dot(a, b, preferred_element_type=F32)


def remote(src, dst, send, recv, device):
    return pltpu.make_async_remote_copy(
        src_ref=src, dst_ref=dst, send_sem=send, recv_sem=recv, device_id=device, device_id_type=MESH
    )


class Links:
    def __init__(self, send, recv, self_device):
        self.send, self.recv, self.anyone, self.started = send, recv, self_device, {}

    def start(self, i, src, dst, device):
        copy = remote(src, dst, self.send.at[i], self.recv.at[i], device)
        self.started[i] = copy
        copy.start()

    def arrive(self, i, dst):
        remote(dst, dst, self.send.at[i], self.recv.at[i], self.anyone).wait_recv()

    def finish(self):
        for copy in self.started.values():
            copy.wait_send()


def place():
    reader, blk = lax.axis_index("reader"), lax.axis_index("blk")
    side = lax.rem(blk // 2, 2)
    return (reader // 4) * 2 + side, lax.rem(reader, 4), blk // 4, lax.rem(blk, 2), side


def device(x, y, z, core):
    return (x // 2) * 4 + y, z * 4 + lax.rem(x, 2) * 2 + core


def ahead(i, d):
    return lax.rem(i + d, 4)


def neighbours():
    x, y, z, core, _ = place()
    return (
        device(ahead(x, 1), y, z, core),
        device(ahead(x, 3), y, z, core),
        device(x, ahead(y, 1), z, core),
        device(x, ahead(y, 3), z, core),
        device(x, y, ahead(z, 1), core),
        device(x, y, ahead(z, 3), core),
        device(x, y, z, 1 - core),
    )


def enter():
    barrier = pltpu.get_barrier_semaphore()
    for one in neighbours():
        pl.semaphore_signal(barrier, inc=1, device_id=one, device_id_type=MESH)
    return lambda: pl.semaphore_wait(barrier, 7)


HALF = BLOCK // 2
QUARTER = HALF // 2


class HalfGather:
    def __init__(self, links, base, buf, source, first, second):
        self.links, self.base, self.buf, self.source = links, base, buf, source
        self.me1, self.up1, self.down1 = first
        self.me2, self.up2, self.down2 = second

    def piece(self, d1, d2):
        return self.buf.at[ahead(self.me2, d2), ahead(self.me1, d1)]

    def quarter(self, d1, q):
        return self.buf.at[self.me2, ahead(self.me1, d1), pl.ds(q * QUARTER, QUARTER)]

    def spread(self, d1):
        ref = self.piece(d1, 0)
        self.links.start(self.base + 4 + d1, ref, ref, self.up2)
        self.links.start(self.base + 8 + d1, ref, ref, self.down2)

    def own(self):
        ref = self.piece(0, 0)
        self.links.start(self.base, self.source, ref, self.up1)
        self.links.start(self.base + 1, self.source, ref, self.down1)

    def near(self):
        self.links.arrive(self.base, self.piece(3, 0))
        self.links.start(self.base + 2, self.quarter(3, 0), self.quarter(3, 0), self.up1)
        self.links.arrive(self.base + 1, self.piece(1, 0))
        self.links.start(self.base + 3, self.quarter(1, 1), self.quarter(1, 1), self.down1)

    def far(self):
        self.links.arrive(self.base + 2, self.quarter(2, 0))
        self.links.arrive(self.base + 3, self.quarter(2, 1))
        self.spread(2)

    def relay(self, d1):
        up = d1 < 2
        ref = self.piece(d1, 3 if up else 1)
        self.links.arrive(self.base + (4 if up else 8) + d1, ref)
        self.links.start(self.base + 12 + d1, ref, ref, self.up2 if up else self.down2)

    def rest(self, up):
        for d1 in (3, 2) if up else (0, 1):
            self.links.arrive(self.base + (4 if up else 8) + d1, self.piece(d1, 3 if up else 1))

    def last(self):
        for d1 in (0, 3, 1, 2):
            self.links.arrive(self.base + 12 + d1, self.piece(d1, 2))


def gather_kernel(
    x_hbm, g_hbm, wq_hbm, wk_hbm, wv_hbm, mask_hbm, coords_hbm, count_ref,
    qt_ref, gt_ref, qn_ref, gn_ref, k_ref, v_ref, mask_ref, wq_ref, wk_ref, wv_ref, coords_own, coords_out, count_out,
    xb, low, high, count_buf, send, recv, local,
):
    x, y, z, core, side = place()
    xp, xm, yp, ym, zp, zm, sib = neighbours()
    links = Links(send, recv, sib)
    begin = enter()
    count_buf[...] = jnp.full(count_buf.shape, count_ref[0, 0], jnp.int32)
    loads = [
        pltpu.make_async_copy(src, dst, local.at[i])
        for i, (src, dst) in enumerate(
            [
                (x_hbm.at[pl.ds(0, HALF)], low.at[y, x]), (x_hbm.at[pl.ds(HALF, HALF)], high.at[x, y]),
                (x_hbm, xb.at[z, core]), (g_hbm, gn_ref.at[z, core]), (wk_hbm, wk_ref), (wv_hbm, wv_ref),
                (wq_hbm, wq_ref), (mask_hbm, mask_ref), (coords_hbm, coords_own),
            ]
        )
    ]
    for load in loads:
        load.start()
    rings = [
        HalfGather(links, 16, low, low.at[y, x], (x, xp, xm), (y, yp, ym)),
        HalfGather(links, 32, high, high.at[x, y], (y, yp, ym), (x, xp, xm)),
    ]
    for i in range(4):
        loads[i].wait()
    begin()

    for ring in rings:
        ring.own()
    for ring in rings:
        ring.spread(0)
    links.start(0, xb.at[z, core], xb.at[z, core], zp)
    links.start(2, xb.at[z, core], xb.at[z, core], zm)
    links.start(1, gn_ref.at[z, core], gn_ref.at[z, core], zp)
    links.start(3, gn_ref.at[z, core], gn_ref.at[z, core], zm)
    links.start(8, xb.at[z, core], xb.at[z, core], sib)
    links.start(9, gn_ref.at[z, core], gn_ref.at[z, core], sib)
    other = device(x + 1 - 2 * side, y, z, core)
    links.start(6, coords_hbm, coords_out, other)
    links.start(7, count_buf, count_out, other)

    def arrive(i, ref, dz, c=core):
        links.arrive(i, ref.at[ahead(z, dz), c])

    def pass_on(i, ref, dz, to):
        block = ref.at[ahead(z, dz), core]
        links.start(i, block, block, to)

    def prepare(dz):
        b = ahead(z, dz)
        rows = xb[b].reshape(2 * BLOCK, D)
        q = (dot(rows, wq_ref[...]).astype(BF16).astype(F32) * SCALE).astype(BF16)
        for c in range(2):
            one = q[c * BLOCK : (c + 1) * BLOCK]
            qn_ref[b, c] = one
            qt_ref[b, c] = one.T
            gt_ref[b, c] = gn_ref[b, c].T

    def project(half, d):
        at = ahead(x if half else y, d)
        rows = (high if half else low)[at].reshape(4 * HALF, D)
        for weight, out in ((wk_ref, k_ref), (wv_ref, v_ref)):
            found = dot(rows, weight[...]).astype(BF16).reshape(4, HALF, D)
            if half:
                out[at, :, HALF:] = found
            else:
                out[:, at, :HALF] = found

    for ring in rings:
        ring.near()
    for ring in rings:
        ring.spread(3)
        ring.spread(1)
    arrive(0, xb, 3)
    pass_on(4, xb, 3, zp)
    for ring in rings:
        ring.far()
    for ring in rings:
        ring.relay(0)
        ring.relay(3)
    for ring in rings:
        ring.relay(1)
    pass_on(10, xb, 3, sib)
    arrive(2, xb, 1)
    pass_on(12, xb, 1, sib)
    for i in range(4, 7):
        loads[i].wait()
    project(0, 0)
    project(1, 0)

    arrive(3, gn_ref, 1)
    pass_on(5, gn_ref, 1, zm)
    pass_on(13, gn_ref, 1, sib)
    arrive(1, gn_ref, 3)
    pass_on(11, gn_ref, 3, sib)
    for ring in rings:
        ring.relay(2)
    arrive(8, xb, 0, 1 - core)
    arrive(9, gn_ref, 0, 1 - core)
    prepare(0)
    for half, ring in enumerate(rings):
        ring.rest(True)
        project(half, 3)
        ring.rest(False)
        project(half, 1)
    arrive(4, xb, 2)
    pass_on(14, xb, 2, sib)
    for i, dz in ((10, 3), (12, 1)):
        arrive(i, xb, dz, 1 - core)
        arrive(i + 1, gn_ref, dz, 1 - core)
        prepare(dz)
        if i == 10:
            arrive(5, gn_ref, 2)
            pass_on(15, gn_ref, 2, sib)
    arrive(14, xb, 2, 1 - core)
    arrive(15, gn_ref, 2, 1 - core)
    prepare(2)
    for half, ring in enumerate(rings):
        ring.last()
        project(half, 2)
    links.arrive(6, coords_out)
    links.arrive(7, count_out)
    loads[7].wait()
    loads[8].wait()
    links.finish()


def gather(features, cotangent, w_query, w_key, w_value, masks, coords, count):
    hbm, vmem = pl.BlockSpec(memory_space=pltpu.HBM), pl.BlockSpec(memory_space=VMEM)
    operands = (features, cotangent, w_query, w_key, w_value, masks, coords)
    return pl.pallas_call(
        gather_kernel,
        out_shape=[
            VMEM((4, 2, D, BLOCK), BF16),
            VMEM((4, 2, D, BLOCK), BF16),
            VMEM((4, 2, BLOCK, D), BF16),
            VMEM((4, 2, BLOCK, D), BF16),
            VMEM((4, 4, BLOCK, D), BF16),
            VMEM((4, 4, BLOCK, D), BF16),
            VMEM(masks.shape, jnp.int32),
            VMEM((D, D), BF16),
            VMEM((D, D), BF16),
            VMEM((D, D), BF16),
            VMEM(coords.shape, jnp.int32),
            VMEM(coords.shape, jnp.int32),
            VMEM((8, 128), jnp.int32),
        ],
        in_specs=[hbm] * 7 + [pl.BlockSpec(memory_space=pltpu.SMEM)],
        out_specs=[vmem] * 13,
        scratch_shapes=[
            VMEM((4, 2, BLOCK, D), BF16),
            VMEM((4, 4, HALF, D), BF16),
            VMEM((4, 4, HALF, D), BF16),
            VMEM((8, 128), jnp.int32),
            pltpu.SemaphoreType.DMA((48,)),
            pltpu.SemaphoreType.DMA((48,)),
            pltpu.SemaphoreType.DMA((9,)),
        ],
        compiler_params=pltpu.CompilerParams(
            collective_id=0, has_side_effects=True, vmem_limit_bytes=16 * 2**20
        ),
        name="gather",
    )(*(pltpu.with_memory_space_constraint(a, pltpu.HBM) for a in operands), count)


def tile_bias(words, first, used):
    spread = jnp.concatenate(
        [jnp.broadcast_to(words[w : w + 1], (32, BLOCK)) for w in range(BLOCK // 32)], axis=0
    )
    key = lax.broadcasted_iota(jnp.int32, (BLOCK, BLOCK), 0)
    query = lax.broadcasted_iota(jnp.int32, (BLOCK, BLOCK), 1)
    bits = (lax.shift_right_logical(spread, key & 31) | jnp.where(key == query, first, 0)) & used
    return jnp.where(bits > 0, 0.0, NEG_FILL).astype(F32)


def pair_product(left, right):
    zero = jnp.zeros((HEAD_DIM, BLOCK), right.dtype)
    top = jnp.concatenate([right[:HEAD_DIM], zero], axis=1)
    bottom = jnp.concatenate([zero, right[HEAD_DIM:]], axis=1)
    return dot(left, jnp.concatenate([top, bottom], axis=0))


UNROLL = 4
WIDE = 8
LIST = 2 * 32 + UNROLL
KEPT = 32


def unpacked(word):
    return word & 7, lax.shift_right_logical(word, 3) & 15, lax.shift_right_logical(word, 8), lax.shift_right_logical(word, 7) & 1


def stats_kernel(
    count_ref, coords_ref, count2_ref, coords2_ref, qt_ref, gt_ref, k_ref, v_ref, mask_ref,
    out_ref, list_ref, kept_e, kept_d, peaks_ref, run,
):
    nb = run.shape[0]
    row = lax.broadcasted_iota(jnp.int32, run.shape, 1)
    run[...] = jnp.where(row < HEADS, FLOOR, 0.0).astype(F32)
    side = lax.rem(lax.axis_index("blk") // 2, 2)

    def collect(counts, coords, column, found):
        def one(i, found):
            qb, kb, p = (coords[0, c, 0, i] for c in range(3))
            key = lax.shift_right_logical(kb, 2) * 8 + column * 4 + (kb & 3)
            first = jnp.where(i + found + (column != side) == 0, 128, 0)
            list_ref[found] = lax.shift_right_logical(qb, 2) * 2 + (qb & 1) + key * 8 + first + p * 256
            return found + jnp.where((lax.shift_right_logical(qb, 1) & 1) == side, 1, 0)

        return lax.fori_loop(0, counts[0, 0], one, found)

    count = collect(count_ref, coords_ref, side, 0)
    count = collect(count2_ref, coords2_ref, 1 - side, count)
    for u in range(UNROLL):
        list_ref[count + u] = 0
    list_ref[LIST] = count

    def tile(t):
        qb, kb, p, first = unpacked(list_ref[t])
        bias = tile_bias(mask_ref[p], first, jnp.where(t < count, 1, 0))
        slot = jnp.minimum(t, KEPT)
        peaks, totals, dots = [], [], []
        for pair in range(HEADS // 2):
            two = slice(pair * 128, pair * 128 + 128)
            s2 = pair_product(k_ref[kb, :, two], qt_ref[qb, two])
            d2 = pair_product(v_ref[kb, :, two], gt_ref[qb, two])
            for half in range(2):
                h = 2 * pair + half
                lanes = slice(half * BLOCK, (half + 1) * BLOCK)
                s = s2[:, lanes] + bias
                peak = jnp.max(s, axis=0, keepdims=True)
                e = jnp.exp(s - peak)
                kept_e[slot, h] = e.astype(BF16)
                kept_d[slot, h] = d2[:, lanes].astype(BF16)
                peaks.append(peak)
                totals.append(jnp.sum(e, axis=0, keepdims=True))
                dots.append(jnp.sum(e * d2[:, lanes], axis=0, keepdims=True))
        peak, total, dot_sum = (jnp.concatenate(rows, axis=0) for rows in (peaks, totals, dots))
        peaks_ref[slot] = peak
        return qb, peak, total, dot_sum

    def add(qb, peak, total, dots):
        before = run[qb, :HEADS]
        m = jnp.maximum(before, peak)
        old, new = jnp.exp(before - m), jnp.exp(peak - m)
        run[qb, :HEADS] = m
        run[qb, HEADS : 2 * HEADS] = run[qb, HEADS : 2 * HEADS] * old + total * new
        run[qb, 2 * HEADS :] = run[qb, 2 * HEADS :] * old + dots * new

    def step(width, g, carry):
        for found in [tile(g * width + u) for u in range(width)]:
            add(*found)
        return carry

    wide = count // WIDE
    lax.fori_loop(0, wide, functools.partial(step, WIDE), 0)
    groups = (count + UNROLL - 1) // UNROLL
    lax.fori_loop(wide * (WIDE // UNROLL), groups, functools.partial(step, UNROLL), 0)
    for b in range(nb):
        total = jnp.maximum(run[b, HEADS : 2 * HEADS], 1e-30)
        out_ref[b, :HEADS] = run[b, :HEADS] + jnp.log(total)
        out_ref[b, HEADS:] = run[b, 2 * HEADS :] / total


def stats(count, coords, count2, coords2, qt, gt, keys, values, masks):
    nb = qt.shape[0]
    smem, vmem = pl.BlockSpec(memory_space=pltpu.SMEM), pl.BlockSpec(memory_space=VMEM)
    return pl.pallas_call(
        stats_kernel,
        out_shape=[
            VMEM((nb, 2 * HEADS, BLOCK), F32),
            jax.ShapeDtypeStruct((LIST + 1,), jnp.int32),
            VMEM((KEPT + 1, HEADS, BLOCK, BLOCK), BF16),
            VMEM((KEPT + 1, HEADS, BLOCK, BLOCK), BF16),
            VMEM((KEPT + 1, HEADS, BLOCK), F32),
        ],
        in_specs=[smem] * 4 + [vmem] * 5,
        out_specs=[vmem, smem, vmem, vmem, vmem],
        scratch_shapes=[VMEM((nb, 3 * HEADS, BLOCK), F32)],
        compiler_params=pltpu.CompilerParams(vmem_limit_bytes=4 * 2**20),
        name="stats",
    )(count, coords, count2, coords2, qt, gt, keys, values, masks)


def merge_kernel(
    st_ref, k_ref, v_ref, wk_ref, wv_ref, kept_e, kept_d, out_ref, acc, kacc, vacc, kt_ref, vt_ref, wkt_ref, wvt_ref,
    land, fin, send, recv, fsend, frecv,
):
    x, y, z, core, _ = place()
    nb = st_ref.shape[0]
    me = z * 2 + core
    block = lambda d: lax.rem(me + d, nb)
    peer = lambda d: device(x, y, block(d) // 2, lax.rem(block(d), 2))
    source = lambda d: lax.rem(me + nb - d, nb)
    barrier = pltpu.get_barrier_semaphore()
    for d in range(1, nb):
        pl.semaphore_signal(barrier, inc=1, device_id=peer(d), device_id_type=MESH)

    def part(d):
        return remote(st_ref.at[block(d)], land.at[d], send.at[d], recv.at[d], peer(d))

    def whole(d):
        return remote(fin.at[0], fin.at[d], fsend.at[d], frecv.at[d], peer(d))

    def turn(b, carry):
        kt_ref[b] = k_ref[b].T
        vt_ref[b] = v_ref[b].T
        return carry

    def clear(b, carry):
        kacc[b] = jnp.zeros(kacc.shape[1:], F32)
        vacc[b] = jnp.zeros(vacc.shape[1:], F32)
        return carry

    def clear_queries(b, carry):
        acc[b] = jnp.zeros(acc.shape[1:], F32)
        return carry

    wkt_ref[...] = wk_ref[...].T
    wvt_ref[...] = wv_ref[...].T
    pl.semaphore_wait(barrier, nb - 1)
    for d in (4, 3, 5, 2, 6, 1, 7):
        part(d).start()
    land[0] = st_ref[me]
    lax.fori_loop(0, 16, turn, 0)
    for d in range(1, nb):
        part(d).wait()
    m = land[0, :HEADS]
    for d in range(1, nb):
        m = jnp.maximum(m, land[d, :HEADS])
    total = jnp.zeros_like(m)
    dots = jnp.zeros_like(m)
    for d in range(nb):
        weight = jnp.exp(land[d, :HEADS] - m)
        total += weight
        dots += land[d, HEADS:] * weight
    fin[0, :HEADS] = m + jnp.log(total)
    fin[0, HEADS:] = dots / total
    for d in (4, 3, 5, 2, 6, 1, 7):
        whole(d).start()
    out_ref[me] = fin[0]
    lax.fori_loop(0, 16, clear, 0)
    lax.fori_loop(0, nb, clear_queries, 0)
    for d in range(1, nb):
        whole(d).wait()
        out_ref[source(d)] = fin[d]


def merge(partial, keys, values, wk, wv, kept_e, kept_d):
    nb, nk = partial.shape[0], keys.shape[0]
    vmem = pl.BlockSpec(memory_space=VMEM)
    return pl.pallas_call(
        merge_kernel,
        out_shape=[
            VMEM(partial.shape, F32),
            VMEM((nb, 2 * D, BLOCK), F32),
            VMEM((nk, BLOCK, D), F32),
            VMEM((nk, BLOCK, D), F32),
            VMEM((nk, D, BLOCK), BF16),
            VMEM((nk, D, BLOCK), BF16),
            VMEM((D, D), BF16),
            VMEM((D, D), BF16),
        ],
        in_specs=[vmem] * 7,
        out_specs=[vmem] * 8,
        scratch_shapes=[
            VMEM(partial.shape, F32),
            VMEM(partial.shape, F32),
            *[pltpu.SemaphoreType.DMA((nb,))] * 4,
        ],
        compiler_params=pltpu.CompilerParams(
            collective_id=1, has_side_effects=True, vmem_limit_bytes=4 * 2**20
        ),
        name="merge",
    )(partial, keys, values, wk, wv, *(pltpu.with_memory_space_constraint(a, pltpu.VMEM) for a in (kept_e, kept_d)))


def lane_split(block):
    lane = lax.broadcasted_iota(jnp.int32, block.shape, 1)
    zero = jnp.zeros_like(block)
    return jnp.concatenate(
        [jnp.where(lane < HEAD_DIM, block, zero), jnp.where(lane >= HEAD_DIM, block, zero)], axis=0
    )


def grad_kernel(
    list_ref, qt_ref, gt_ref, qn_ref, gn_ref, k_ref, v_ref, kt_ref, vt_ref, mask_ref, fin_ref,
    kept_e, kept_d, peaks_ref, acc_in, kacc_in, vacc_in, acc, kacc, vacc, probs, dscores,
):
    count = list_ref[LIST]

    def scores(t, u):
        qb, kb, p, first = unpacked(list_ref[t])
        bias = tile_bias(mask_ref[p], first, jnp.where(t < count, 1, 0))
        for pair in range(HEADS // 2):
            two = slice(pair * 128, pair * 128 + 128)
            s2 = pair_product(k_ref[kb, :, two], qt_ref[qb, two])
            d2 = pair_product(v_ref[kb, :, two], gt_ref[qb, two])
            for half in range(2):
                h = pair * 2 + half
                lanes = slice(half * BLOCK, (half + 1) * BLOCK)
                prob = jnp.exp(s2[:, lanes] + bias - fin_ref[qb, h : h + 1])
                probs[u, h] = prob.astype(BF16)
                delta = fin_ref[qb, HEADS + h : HEADS + h + 1]
                dscores[u, h] = (prob * (d2[:, lanes] - delta)).astype(BF16)

    def kept_scores(t, u):
        qb = unpacked(list_ref[t])[0]
        factor = jnp.exp(peaks_ref[t] - fin_ref[qb, :HEADS])
        for h in range(HEADS):
            prob = kept_e[t, h].astype(F32) * factor[h : h + 1]
            probs[u, h] = prob.astype(BF16)
            delta = fin_ref[qb, HEADS + h : HEADS + h + 1]
            dscores[u, h] = (prob * (kept_d[t, h].astype(F32) - delta)).astype(BF16)

    def products(t, u):
        qb, kb = unpacked(list_ref[t])[:2]
        for pair in range(HEADS // 2):
            for h in (2 * pair, 2 * pair + 1):
                head = slice(h * HEAD_DIM, (h + 1) * HEAD_DIM)
                ghead = slice(D + h * HEAD_DIM, D + (h + 1) * HEAD_DIM)
                acc[qb, head] += dot(vt_ref[kb, head], probs[u, h])
                acc[qb, ghead] += dot(kt_ref[kb, head], dscores[u, h])
            two = slice(pair * 128, pair * 128 + 128)
            low = jnp.concatenate([probs[u, 2 * pair], probs[u, 2 * pair + 1]], axis=1)
            ds = jnp.concatenate([dscores[u, 2 * pair], dscores[u, 2 * pair + 1]], axis=1)
            kacc[kb, :, two] += dot(ds, lane_split(qn_ref[qb, :, two]))
            vacc[kb, :, two] += dot(low, lane_split(gn_ref[qb, :, two]))

    def step(find, g, carry):
        for u in range(UNROLL):
            find(g * UNROLL + u, u)
        for u in range(UNROLL):
            products(g * UNROLL + u, u)
        return carry

    groups = (count + UNROLL - 1) // UNROLL
    kept = jnp.minimum(groups, KEPT // UNROLL)
    lax.fori_loop(0, kept, functools.partial(step, kept_scores), 0)
    lax.fori_loop(kept, groups, functools.partial(step, scores), 0)


def grads(tiles, arrays, acc, kacc, vacc):
    smem, vmem = pl.BlockSpec(memory_space=pltpu.SMEM), pl.BlockSpec(memory_space=VMEM)
    first = 1 + len(arrays)
    return pl.pallas_call(
        grad_kernel,
        out_shape=[
            VMEM(acc.shape, F32),
            VMEM(kacc.shape, F32),
            VMEM(vacc.shape, F32),
        ],
        in_specs=[smem] + [vmem] * (len(arrays) + 3),
        out_specs=[vmem] * 3,
        scratch_shapes=[VMEM((UNROLL, HEADS, BLOCK, BLOCK), BF16)] * 2,
        input_output_aliases={first: 0, first + 1: 1, first + 2: 2},
        compiler_params=pltpu.CompilerParams(vmem_limit_bytes=5 * 2**20),
        name="grads",
    )(tiles, *arrays, acc, kacc, vacc)


class HalfReduce:
    def __init__(self, links, base, buf, land, quarters, out, first, second):
        self.links, self.base, self.buf, self.land, self.quarters, self.out = links, base, buf, land, quarters, out
        self.me1, self.up1, self.down1 = first
        self.me2, self.up2, self.down2 = second

    def at(self, d1, d2):
        return ahead(self.me2, d2), ahead(self.me1, d1)

    def send(self, d1, d2, channel, src, to):
        self.links.start(self.base + channel, src, self.land.at[channel], to)

    def landed(self, channel):
        self.links.arrive(self.base + channel, self.land.at[channel])
        return self.land[channel].astype(F32)

    def first(self):
        for d1 in (1, 2, 0, 3):
            self.send(d1, 2, 12 + d1, self.buf.at[self.at(d1, 2)], self.up2 if d1 < 2 else self.down2)

    def direct(self, d1):
        up = d1 >= 2
        d2, channel = (1, 4 + d1) if up else (3, 8 + d1)
        self.send(d1, d2, channel, self.buf.at[self.at(d1, d2)], self.up2 if up else self.down2)

    def middle(self, d1):
        up = d1 < 2
        d2, channel = (1, 4 + d1) if up else (3, 8 + d1)
        total = self.buf[self.at(d1, d2)].astype(F32) + self.landed(12 + d1)
        self.out[d1] = total.astype(BF16)
        self.send(d1, d2, channel, self.out.at[d1], self.up2 if up else self.down2)

    def row(self, d1):
        return self.buf[self.at(d1, 0)].astype(F32) + self.landed(4 + d1) + self.landed(8 + d1)

    def cross(self):
        self.out[4] = self.row(2).astype(BF16)
        for q, to in ((0, self.up1), (1, self.down1)):
            rows = pl.ds(q * QUARTER, QUARTER)
            self.links.start(self.base + 2 + q, self.out.at[4, rows], self.quarters.at[rows], to)

    def finals(self):
        up, down = self.row(1), self.row(3)
        self.links.arrive(self.base + 2, self.quarters.at[pl.ds(0, QUARTER)])
        self.out[5, :QUARTER] = (up[:QUARTER] + self.quarters[:QUARTER].astype(F32)).astype(BF16)
        self.out[5, QUARTER:] = up[QUARTER:].astype(BF16)
        self.send(1, 0, 0, self.out.at[5], self.up1)
        self.links.arrive(self.base + 3, self.quarters.at[pl.ds(QUARTER, QUARTER)])
        self.out[6, :QUARTER] = down[:QUARTER].astype(BF16)
        self.out[6, QUARTER:] = (down[QUARTER:] + self.quarters[QUARTER:].astype(F32)).astype(BF16)
        self.send(3, 0, 1, self.out.at[6], self.down1)

    def result(self):
        return self.row(0) + self.landed(0) + self.landed(1)


def reduce_kernel(
    p_ref, kacc, vacc, wkt_ref, wvt_ref, outputs_ref, queries_ref, nodes_ref,
    low, high, to_sib, from_sib, sums, land, kland, quarters, ksums, send, recv,
):
    x, y, z, core, _ = place()
    xp, xm, yp, ym, zp, zm, sib = neighbours()
    links = Links(send, recv, sib)
    begin = enter()
    order = [2, 1, 3, 0]
    part = lambda c: pl.ds(c * D, D)
    parts = [(0, 0), (0, 1), (1, 1), (2, 0), (1, 0), (2, 1), (3, 0), (3, 1)]
    rings = [
        HalfReduce(links, 16, low, kland.at[0], quarters.at[0], ksums.at[0], (x, xp, xm), (y, yp, ym)),
        HalfReduce(links, 32, high, kland.at[1], quarters.at[1], ksums.at[1], (y, yp, ym), (x, xp, xm)),
    ]

    def block(i, c, mine):
        return p_ref[ahead(z, order[i]) * 2 + (core if mine else 1 - core), part(c)]

    def weigh(half, d):
        at = ahead(x if half else y, d)
        total = 0.0
        for found, weight in ((kacc, wkt_ref), (vacc, wvt_ref)):
            rows = found[at, :, HALF:] if half else found[:, at, :HALF]
            total += dot(rows.reshape(4 * HALF, D).astype(BF16), weight[...])
        (high if half else low)[at] = total.reshape(4, HALF, D).astype(BF16)

    for i, c in parts[:4]:
        to_sib[i, c] = block(i, c, False).astype(BF16)
    weigh(0, 2)
    begin()
    for i, c in parts[:4]:
        links.start(8 + 2 * i + c, to_sib.at[i, c], from_sib.at[i, c], sib)
    rings[0].first()
    weigh(1, 2)
    rings[1].first()
    for i, c in parts[4:]:
        to_sib[i, c] = block(i, c, False).astype(BF16)
        links.start(8 + 2 * i + c, to_sib.at[i, c], from_sib.at[i, c], sib)

    def both(i, c):
        links.arrive(8 + 2 * i + c, from_sib.at[i, c])
        return block(i, c, True) + from_sib[i, c].astype(F32)

    def put(channel, i, c, value, to):
        sums[i, c] = value.astype(BF16)
        links.start(channel, sums.at[i, c], land.at[channel], to)

    def landed(channel):
        links.arrive(channel, land.at[channel])
        return land[channel].astype(F32)

    for half, ring in enumerate(rings):
        weigh(half, 1)
        weigh(half, 3)
        ring.direct(2)
    put(0, 0, 0, both(0, 0), zp)
    put(1, 0, 1, both(0, 1), zm)
    for ring in rings:
        ring.middle(2)
        ring.direct(1)
    put(2, 1, 1, both(1, 1), zp)
    put(3, 2, 0, both(2, 0), zm)
    for ring in rings:
        ring.middle(1)
        ring.direct(3)
    for ring in rings:
        ring.middle(3)
    weigh(0, 0)
    weigh(1, 0)
    for ring in rings:
        ring.cross()
    for ring in rings:
        ring.middle(0)
        ring.direct(0)
    up, down = both(1, 0), both(2, 1)
    put(4, 1, 0, up + landed(0), zp)
    put(5, 2, 1, down + landed(1), zm)
    for ring in rings:
        ring.finals()
    outputs_ref[...] = both(3, 0) + landed(3) + landed(4)
    queries_ref[...] = ((both(3, 1) + landed(2) + landed(5)) * SCALE).astype(BF16)
    for half, ring in enumerate(rings):
        nodes_ref[half * HALF : (half + 1) * HALF] = ring.result()
    links.finish()


def reduce(parts, kacc, vacc, wkt, wvt):
    vmem = pl.BlockSpec(memory_space=VMEM)
    block = (2, D, BLOCK)
    return pl.pallas_call(
        reduce_kernel,
        out_shape=[VMEM((D, BLOCK), F32), VMEM((D, BLOCK), BF16), VMEM((BLOCK, D), F32)],
        in_specs=[vmem] * 5,
        out_specs=[vmem] * 3,
        scratch_shapes=[
            VMEM((4, 4, HALF, D), BF16),
            VMEM((4, 4, HALF, D), BF16),
            VMEM((4, *block), BF16),
            VMEM((4, *block), BF16),
            VMEM((3, *block), BF16),
            VMEM((6, D, BLOCK), BF16),
            VMEM((2, 16, HALF, D), BF16),
            VMEM((2, HALF, D), BF16),
            VMEM((2, 7, HALF, D), BF16),
            pltpu.SemaphoreType.DMA((48,)),
            pltpu.SemaphoreType.DMA((48,)),
        ],
        compiler_params=pltpu.CompilerParams(
            collective_id=2, has_side_effects=True, vmem_limit_bytes=24 * 2**20
        ),
        name="reduce",
    )(parts, kacc.reshape(4, 4, BLOCK, D), vacc.reshape(4, 4, BLOCK, D), wkt, wvt)


def finish_kernel(outputs_ref, queries_ref, nodes_ref, wq_ref, attn_ref, grad_ref):
    attn_ref[...] = outputs_ref[...].T.astype(BF16)
    grad_ref[...] = (dot(wq_ref[...], queries_ref[...]).T + nodes_ref[...]).astype(BF16)


def finish(outputs, queries, nodes, w_query):
    vmem = pl.BlockSpec(memory_space=VMEM)
    return pl.pallas_call(
        finish_kernel,
        out_shape=[jax.ShapeDtypeStruct((BLOCK, D), BF16)] * 2,
        in_specs=[vmem] * 4,
        out_specs=[vmem] * 2,
        compiler_params=pltpu.CompilerParams(vmem_limit_bytes=8 * 2**20),
        name="finish",
    )(outputs, queries, nodes, w_query)


def local(features, cotangent, w_query, w_key, w_value, tile_coords, tile_count, mask_table):
    masks = mask_table.transpose(0, 2, 1)
    coords = tile_coords.transpose(0, 3, 1, 2)
    found = gather(features, cotangent, w_query, w_key, w_value, masks, coords, tile_count)
    qt, gt, qn, gn, keys, values = (a.reshape(-1, *a.shape[2:]) for a in found[:6])
    masks, wq, wk, wv, coords, coords2, count2 = found[6:]
    partial, tiles, *kept = stats(tile_count, coords, count2, coords2, qt, gt, keys, values, masks)
    fin, acc, kacc, vacc, keys_t, values_t, wkt, wvt = merge(partial, keys, values, wk, wv, *kept[:2])
    arrays = (qt, gt, qn, gn, keys, values, keys_t, values_t, masks, fin, *kept)
    parts, kacc, vacc = grads(tiles, arrays, acc, kacc, vacc)
    return tuple(finish(*reduce(parts, kacc, vacc, wkt, wvt), wq))


def solution(mesh):
    return jax.shard_map(
        local,
        mesh=mesh,
        in_specs=(
            P(("reader", "blk"), None),
            P(("reader", "blk"), None),
            P(),
            P(),
            P(),
            P("reader", "blk", None, None),
            P("reader", "blk"),
            P(),
        ),
        out_specs=(P(("reader", "blk"), None), P(("reader", "blk"), None)),
        check_vma=False,
    )
```

```python
import functools

import jax
import jax.numpy as jnp
from jax import lax
from jax.experimental import pallas as pl
from jax.experimental.pallas import tpu as pltpu
from jax.sharding import PartitionSpec as P

HEADS = 8
HEAD_DIM = 64
D = 512
BLOCK = 128
SCALE = 0.125
FLOOR = -1e20
NEG_FILL = -1e30
MESH = pl.DeviceIdType.MESH
F32 = jnp.float32
BF16 = jnp.bfloat16
VMEM = pltpu.VMEM


def dot(a, b):
    return jnp.dot(a, b, preferred_element_type=F32)


def remote(src, dst, send, recv, device):
    return pltpu.make_async_remote_copy(
        src_ref=src, dst_ref=dst, send_sem=send, recv_sem=recv, device_id=device, device_id_type=MESH
    )


class Links:
    def __init__(self, send, recv, self_device):
        self.send, self.recv, self.anyone, self.started = send, recv, self_device, {}

    def start(self, i, src, dst, device):
        copy = remote(src, dst, self.send.at[i], self.recv.at[i], device)
        self.started[i] = copy
        copy.start()

    def arrive(self, i, dst):
        remote(dst, dst, self.send.at[i], self.recv.at[i], self.anyone).wait_recv()

    def finish(self):
        for copy in self.started.values():
            copy.wait_send()


def place():
    reader, blk = lax.axis_index("reader"), lax.axis_index("blk")
    side = lax.rem(blk // 2, 2)
    return (reader // 4) * 2 + side, lax.rem(reader, 4), blk // 4, lax.rem(blk, 2), side


def device(x, y, z, core):
    return (x // 2) * 4 + y, z * 4 + lax.rem(x, 2) * 2 + core


def ahead(i, d):
    return lax.rem(i + d, 4)


def neighbours():
    x, y, z, core, _ = place()
    return (
        device(ahead(x, 1), y, z, core),
        device(ahead(x, 3), y, z, core),
        device(x, ahead(y, 1), z, core),
        device(x, ahead(y, 3), z, core),
        device(x, y, ahead(z, 1), core),
        device(x, y, ahead(z, 3), core),
        device(x, y, z, 1 - core),
    )


def enter():
    barrier = pltpu.get_barrier_semaphore()
    for one in neighbours():
        pl.semaphore_signal(barrier, inc=1, device_id=one, device_id_type=MESH)
    return lambda: pl.semaphore_wait(barrier, 7)


HALF = BLOCK // 2
QUARTER = HALF // 2


class HalfGather:
    def __init__(self, links, base, buf, source, first, second):
        self.links, self.base, self.buf, self.source = links, base, buf, source
        self.me1, self.up1, self.down1 = first
        self.me2, self.up2, self.down2 = second

    def piece(self, d1, d2):
        return self.buf.at[ahead(self.me2, d2), ahead(self.me1, d1)]

    def quarter(self, d1, q):
        return self.buf.at[self.me2, ahead(self.me1, d1), pl.ds(q * QUARTER, QUARTER)]

    def spread(self, d1):
        ref = self.piece(d1, 0)
        self.links.start(self.base + 4 + d1, ref, ref, self.up2)
        self.links.start(self.base + 8 + d1, ref, ref, self.down2)

    def own(self):
        ref = self.piece(0, 0)
        self.links.start(self.base, self.source, ref, self.up1)
        self.links.start(self.base + 1, self.source, ref, self.down1)

    def near(self):
        self.links.arrive(self.base, self.piece(3, 0))
        self.links.start(self.base + 2, self.quarter(3, 0), self.quarter(3, 0), self.up1)
        self.links.arrive(self.base + 1, self.piece(1, 0))
        self.links.start(self.base + 3, self.quarter(1, 1), self.quarter(1, 1), self.down1)

    def far(self):
        self.links.arrive(self.base + 2, self.quarter(2, 0))
        self.links.arrive(self.base + 3, self.quarter(2, 1))
        self.spread(2)

    def relay(self, d1):
        up = d1 < 2
        ref = self.piece(d1, 3 if up else 1)
        self.links.arrive(self.base + (4 if up else 8) + d1, ref)
        self.links.start(self.base + 12 + d1, ref, ref, self.up2 if up else self.down2)

    def rest(self, up):
        for d1 in (3, 2) if up else (0, 1):
            self.links.arrive(self.base + (4 if up else 8) + d1, self.piece(d1, 3 if up else 1))

    def last(self):
        for d1 in (0, 3, 1, 2):
            self.links.arrive(self.base + 12 + d1, self.piece(d1, 2))


def gather_kernel(
    x_hbm, g_hbm, wq_hbm, wk_hbm, wv_hbm, mask_hbm, coords_hbm, count_ref,
    qt_ref, gt_ref, qn_ref, gn_ref, k_ref, v_ref, mask_ref, wq_ref, wk_ref, wv_ref, coords_own, coords_out, count_out,
    xb, low, high, count_buf, send, recv, local,
):
    x, y, z, core, side = place()
    xp, xm, yp, ym, zp, zm, sib = neighbours()
    links = Links(send, recv, sib)
    begin = enter()
    count_buf[...] = jnp.full(count_buf.shape, count_ref[0, 0], jnp.int32)
    loads = [
        pltpu.make_async_copy(src, dst, local.at[i])
        for i, (src, dst) in enumerate(
            [
                (x_hbm.at[pl.ds(0, HALF)], low.at[y, x]), (x_hbm.at[pl.ds(HALF, HALF)], high.at[x, y]),
                (x_hbm, xb.at[z, core]), (g_hbm, gn_ref.at[z, core]), (wk_hbm, wk_ref), (wv_hbm, wv_ref),
                (wq_hbm, wq_ref), (mask_hbm, mask_ref), (coords_hbm, coords_own),
            ]
        )
    ]
    for load in loads:
        load.start()
    rings = [
        HalfGather(links, 16, low, low.at[y, x], (x, xp, xm), (y, yp, ym)),
        HalfGather(links, 32, high, high.at[x, y], (y, yp, ym), (x, xp, xm)),
    ]
    for i in range(4):
        loads[i].wait()
    begin()

    for ring in rings:
        ring.own()
    for ring in rings:
        ring.spread(0)
    links.start(0, xb.at[z, core], xb.at[z, core], zp)
    links.start(2, xb.at[z, core], xb.at[z, core], zm)
    links.start(1, gn_ref.at[z, core], gn_ref.at[z, core], zp)
    links.start(3, gn_ref.at[z, core], gn_ref.at[z, core], zm)
    links.start(8, xb.at[z, core], xb.at[z, core], sib)
    links.start(9, gn_ref.at[z, core], gn_ref.at[z, core], sib)
    other = device(x + 1 - 2 * side, y, z, core)
    links.start(6, coords_hbm, coords_out, other)
    links.start(7, count_buf, count_out, other)

    def arrive(i, ref, dz, c=core):
        links.arrive(i, ref.at[ahead(z, dz), c])

    def pass_on(i, ref, dz, to):
        block = ref.at[ahead(z, dz), core]
        links.start(i, block, block, to)

    def prepare(dz):
        b = ahead(z, dz)
        rows = xb[b].reshape(2 * BLOCK, D)
        q = (dot(rows, wq_ref[...]).astype(BF16).astype(F32) * SCALE).astype(BF16)
        for c in range(2):
            one = q[c * BLOCK : (c + 1) * BLOCK]
            qn_ref[b, c] = one
            qt_ref[b, c] = one.T
            gt_ref[b, c] = gn_ref[b, c].T

    def project(half, d):
        at = ahead(x if half else y, d)
        rows = (high if half else low)[at].reshape(4 * HALF, D)
        for weight, out in ((wk_ref, k_ref), (wv_ref, v_ref)):
            found = dot(rows, weight[...]).astype(BF16).reshape(4, HALF, D)
            if half:
                out[at, :, HALF:] = found
            else:
                out[:, at, :HALF] = found

    for ring in rings:
        ring.near()
    for ring in rings:
        ring.spread(3)
        ring.spread(1)
    arrive(0, xb, 3)
    pass_on(4, xb, 3, zp)
    for ring in rings:
        ring.far()
    for ring in rings:
        ring.relay(0)
        ring.relay(3)
    for ring in rings:
        ring.relay(1)
    pass_on(10, xb, 3, sib)
    arrive(2, xb, 1)
    pass_on(12, xb, 1, sib)
    for i in range(4, 7):
        loads[i].wait()
    project(0, 0)
    project(1, 0)

    arrive(3, gn_ref, 1)
    pass_on(5, gn_ref, 1, zm)
    pass_on(13, gn_ref, 1, sib)
    arrive(1, gn_ref, 3)
    pass_on(11, gn_ref, 3, sib)
    for ring in rings:
        ring.relay(2)
    arrive(8, xb, 0, 1 - core)
    arrive(9, gn_ref, 0, 1 - core)
    prepare(0)
    for half, ring in enumerate(rings):
        ring.rest(True)
        project(half, 3)
        ring.rest(False)
        project(half, 1)
    arrive(4, xb, 2)
    pass_on(14, xb, 2, sib)
    for i, dz in ((10, 3), (12, 1)):
        arrive(i, xb, dz, 1 - core)
        arrive(i + 1, gn_ref, dz, 1 - core)
        prepare(dz)
        if i == 10:
            arrive(5, gn_ref, 2)
            pass_on(15, gn_ref, 2, sib)
    arrive(14, xb, 2, 1 - core)
    arrive(15, gn_ref, 2, 1 - core)
    prepare(2)
    for half, ring in enumerate(rings):
        ring.last()
        project(half, 2)
    links.arrive(6, coords_out)
    links.arrive(7, count_out)
    loads[7].wait()
    loads[8].wait()
    links.finish()


def gather(features, cotangent, w_query, w_key, w_value, masks, coords, count):
    hbm, vmem = pl.BlockSpec(memory_space=pltpu.HBM), pl.BlockSpec(memory_space=VMEM)
    operands = (features, cotangent, w_query, w_key, w_value, masks, coords)
    return pl.pallas_call(
        gather_kernel,
        out_shape=[
            VMEM((4, 2, D, BLOCK), BF16),
            VMEM((4, 2, D, BLOCK), BF16),
            VMEM((4, 2, BLOCK, D), BF16),
            VMEM((4, 2, BLOCK, D), BF16),
            VMEM((4, 4, BLOCK, D), BF16),
            VMEM((4, 4, BLOCK, D), BF16),
            VMEM(masks.shape, jnp.int32),
            VMEM((D, D), BF16),
            VMEM((D, D), BF16),
            VMEM((D, D), BF16),
            VMEM(coords.shape, jnp.int32),
            VMEM(coords.shape, jnp.int32),
            VMEM((8, 128), jnp.int32),
        ],
        in_specs=[hbm] * 7 + [pl.BlockSpec(memory_space=pltpu.SMEM)],
        out_specs=[vmem] * 13,
        scratch_shapes=[
            VMEM((4, 2, BLOCK, D), BF16),
            VMEM((4, 4, HALF, D), BF16),
            VMEM((4, 4, HALF, D), BF16),
            VMEM((8, 128), jnp.int32),
            pltpu.SemaphoreType.DMA((48,)),
            pltpu.SemaphoreType.DMA((48,)),
            pltpu.SemaphoreType.DMA((9,)),
        ],
        compiler_params=pltpu.CompilerParams(
            collective_id=0, has_side_effects=True, vmem_limit_bytes=16 * 2**20
        ),
        name="gather",
    )(*(pltpu.with_memory_space_constraint(a, pltpu.HBM) for a in operands), count)


def tile_bias(words, first, used):
    spread = jnp.concatenate(
        [jnp.broadcast_to(words[w : w + 1], (32, BLOCK)) for w in range(BLOCK // 32)], axis=0
    )
    key = lax.broadcasted_iota(jnp.int32, (BLOCK, BLOCK), 0)
    query = lax.broadcasted_iota(jnp.int32, (BLOCK, BLOCK), 1)
    bits = (lax.shift_right_logical(spread, key & 31) | jnp.where(key == query, first, 0)) & used
    return jnp.where(bits > 0, 0.0, NEG_FILL).astype(F32)


def pair_product(left, right):
    zero = jnp.zeros((HEAD_DIM, BLOCK), right.dtype)
    top = jnp.concatenate([right[:HEAD_DIM], zero], axis=1)
    bottom = jnp.concatenate([zero, right[HEAD_DIM:]], axis=1)
    return dot(left, jnp.concatenate([top, bottom], axis=0))


UNROLL = 4
WIDE = 8
LIST = 2 * 32 + UNROLL
KEPT = 32


def unpacked(word):
    return word & 7, lax.shift_right_logical(word, 3) & 15, lax.shift_right_logical(word, 8), lax.shift_right_logical(word, 7) & 1


def stats_kernel(
    count_ref, coords_ref, count2_ref, coords2_ref, qt_ref, gt_ref, k_ref, v_ref, mask_ref,
    out_ref, list_ref, kept_e, kept_d, peaks_ref, run,
):
    nb = run.shape[0]
    row = lax.broadcasted_iota(jnp.int32, run.shape, 1)
    run[...] = jnp.where(row < HEADS, FLOOR, 0.0).astype(F32)
    side = lax.rem(lax.axis_index("blk") // 2, 2)

    def collect(counts, coords, column, found):
        def one(i, found):
            qb, kb, p = (coords[0, c, 0, i] for c in range(3))
            key = lax.shift_right_logical(kb, 2) * 8 + column * 4 + (kb & 3)
            first = jnp.where(i + found + (column != side) == 0, 128, 0)
            list_ref[found] = lax.shift_right_logical(qb, 2) * 2 + (qb & 1) + key * 8 + first + p * 256
            return found + jnp.where((lax.shift_right_logical(qb, 1) & 1) == side, 1, 0)

        return lax.fori_loop(0, counts[0, 0], one, found)

    count = collect(count_ref, coords_ref, side, 0)
    count = collect(count2_ref, coords2_ref, 1 - side, count)
    for u in range(UNROLL):
        list_ref[count + u] = 0
    list_ref[LIST] = count

    def tile(t):
        qb, kb, p, first = unpacked(list_ref[t])
        bias = tile_bias(mask_ref[p], first, jnp.where(t < count, 1, 0))
        slot = jnp.minimum(t, KEPT)
        peaks, totals, dots = [], [], []
        for pair in range(HEADS // 2):
            two = slice(pair * 128, pair * 128 + 128)
            s2 = pair_product(k_ref[kb, :, two], qt_ref[qb, two])
            d2 = pair_product(v_ref[kb, :, two], gt_ref[qb, two])
            for half in range(2):
                h = 2 * pair + half
                lanes = slice(half * BLOCK, (half + 1) * BLOCK)
                s = s2[:, lanes] + bias
                peak = jnp.max(s, axis=0, keepdims=True)
                e = jnp.exp(s - peak)
                kept_e[slot, h] = e.astype(BF16)
                kept_d[slot, h] = d2[:, lanes].astype(BF16)
                peaks.append(peak)
                totals.append(jnp.sum(e, axis=0, keepdims=True))
                dots.append(jnp.sum(e * d2[:, lanes], axis=0, keepdims=True))
        peak, total, dot_sum = (jnp.concatenate(rows, axis=0) for rows in (peaks, totals, dots))
        peaks_ref[slot] = peak
        return qb, peak, total, dot_sum

    def add(qb, peak, total, dots):
        before = run[qb, :HEADS]
        m = jnp.maximum(before, peak)
        old, new = jnp.exp(before - m), jnp.exp(peak - m)
        run[qb, :HEADS] = m
        run[qb, HEADS : 2 * HEADS] = run[qb, HEADS : 2 * HEADS] * old + total * new
        run[qb, 2 * HEADS :] = run[qb, 2 * HEADS :] * old + dots * new

    def step(width, g, carry):
        for found in [tile(g * width + u) for u in range(width)]:
            add(*found)
        return carry

    wide = count // WIDE
    lax.fori_loop(0, wide, functools.partial(step, WIDE), 0)
    groups = (count + UNROLL - 1) // UNROLL
    lax.fori_loop(wide * (WIDE // UNROLL), groups, functools.partial(step, UNROLL), 0)
    for b in range(nb):
        total = jnp.maximum(run[b, HEADS : 2 * HEADS], 1e-30)
        out_ref[b, :HEADS] = run[b, :HEADS] + jnp.log(total)
        out_ref[b, HEADS:] = run[b, 2 * HEADS :] / total


def stats(count, coords, count2, coords2, qt, gt, keys, values, masks):
    nb = qt.shape[0]
    smem, vmem = pl.BlockSpec(memory_space=pltpu.SMEM), pl.BlockSpec(memory_space=VMEM)
    return pl.pallas_call(
        stats_kernel,
        out_shape=[
            VMEM((nb, 2 * HEADS, BLOCK), F32),
            jax.ShapeDtypeStruct((LIST + 1,), jnp.int32),
            VMEM((KEPT + 1, HEADS, BLOCK, BLOCK), BF16),
            VMEM((KEPT + 1, HEADS, BLOCK, BLOCK), BF16),
            VMEM((KEPT + 1, HEADS, BLOCK), F32),
        ],
        in_specs=[smem] * 4 + [vmem] * 5,
        out_specs=[vmem, smem, vmem, vmem, vmem],
        scratch_shapes=[VMEM((nb, 3 * HEADS, BLOCK), F32)],
        compiler_params=pltpu.CompilerParams(vmem_limit_bytes=4 * 2**20),
        name="stats",
    )(count, coords, count2, coords2, qt, gt, keys, values, masks)


def merge_kernel(
    st_ref, k_ref, v_ref, wk_ref, wv_ref, kept_e, kept_d, out_ref, acc, kacc, vacc, kt_ref, vt_ref, wkt_ref, wvt_ref,
    land, fin, send, recv, fsend, frecv,
):
    x, y, z, core, _ = place()
    nb = st_ref.shape[0]
    me = z * 2 + core
    block = lambda d: lax.rem(me + d, nb)
    peer = lambda d: device(x, y, block(d) // 2, lax.rem(block(d), 2))
    source = lambda d: lax.rem(me + nb - d, nb)
    barrier = pltpu.get_barrier_semaphore()
    for d in range(1, nb):
        pl.semaphore_signal(barrier, inc=1, device_id=peer(d), device_id_type=MESH)

    def part(d):
        return remote(st_ref.at[block(d)], land.at[d], send.at[d], recv.at[d], peer(d))

    def whole(d):
        return remote(fin.at[0], fin.at[d], fsend.at[d], frecv.at[d], peer(d))

    def turn(b, carry):
        kt_ref[b] = k_ref[b].T
        vt_ref[b] = v_ref[b].T
        return carry

    def clear(b, carry):
        kacc[b] = jnp.zeros(kacc.shape[1:], F32)
        vacc[b] = jnp.zeros(vacc.shape[1:], F32)
        return carry

    def clear_queries(b, carry):
        acc[b] = jnp.zeros(acc.shape[1:], F32)
        return carry

    wkt_ref[...] = wk_ref[...].T
    wvt_ref[...] = wv_ref[...].T
    pl.semaphore_wait(barrier, nb - 1)
    for d in (4, 3, 5, 2, 6, 1, 7):
        part(d).start()
    land[0] = st_ref[me]
    lax.fori_loop(0, 16, turn, 0)
    for d in range(1, nb):
        part(d).wait()
    m = land[0, :HEADS]
    for d in range(1, nb):
        m = jnp.maximum(m, land[d, :HEADS])
    total = jnp.zeros_like(m)
    dots = jnp.zeros_like(m)
    for d in range(nb):
        weight = jnp.exp(land[d, :HEADS] - m)
        total += weight
        dots += land[d, HEADS:] * weight
    fin[0, :HEADS] = m + jnp.log(total)
    fin[0, HEADS:] = dots / total
    for d in (4, 3, 5, 2, 6, 1, 7):
        whole(d).start()
    out_ref[me] = fin[0]
    lax.fori_loop(0, 16, clear, 0)
    lax.fori_loop(0, nb, clear_queries, 0)
    for d in range(1, nb):
        whole(d).wait()
        out_ref[source(d)] = fin[d]


def merge(partial, keys, values, wk, wv, kept_e, kept_d):
    nb, nk = partial.shape[0], keys.shape[0]
    vmem = pl.BlockSpec(memory_space=VMEM)
    return pl.pallas_call(
        merge_kernel,
        out_shape=[
            VMEM(partial.shape, F32),
            VMEM((nb, 2 * D, BLOCK), F32),
            VMEM((nk, BLOCK, D), F32),
            VMEM((nk, BLOCK, D), F32),
            VMEM((nk, D, BLOCK), BF16),
            VMEM((nk, D, BLOCK), BF16),
            VMEM((D, D), BF16),
            VMEM((D, D), BF16),
        ],
        in_specs=[vmem] * 7,
        out_specs=[vmem] * 8,
        scratch_shapes=[
            VMEM(partial.shape, F32),
            VMEM(partial.shape, F32),
            *[pltpu.SemaphoreType.DMA((nb,))] * 4,
        ],
        compiler_params=pltpu.CompilerParams(
            collective_id=1, has_side_effects=True, vmem_limit_bytes=4 * 2**20
        ),
        name="merge",
    )(partial, keys, values, wk, wv, *(pltpu.with_memory_space_constraint(a, pltpu.VMEM) for a in (kept_e, kept_d)))


def lane_split(block):
    lane = lax.broadcasted_iota(jnp.int32, block.shape, 1)
    zero = jnp.zeros_like(block)
    return jnp.concatenate(
        [jnp.where(lane < HEAD_DIM, block, zero), jnp.where(lane >= HEAD_DIM, block, zero)], axis=0
    )


def grad_kernel(
    list_ref, qt_ref, gt_ref, qn_ref, gn_ref, k_ref, v_ref, kt_ref, vt_ref, mask_ref, fin_ref,
    kept_e, kept_d, peaks_ref, acc_in, kacc_in, vacc_in, acc, kacc, vacc, probs, dscores,
):
    count = list_ref[LIST]

    def scores(t, u):
        qb, kb, p, first = unpacked(list_ref[t])
        bias = tile_bias(mask_ref[p], first, jnp.where(t < count, 1, 0))
        for pair in range(HEADS // 2):
            two = slice(pair * 128, pair * 128 + 128)
            s2 = pair_product(k_ref[kb, :, two], qt_ref[qb, two])
            d2 = pair_product(v_ref[kb, :, two], gt_ref[qb, two])
            for half in range(2):
                h = pair * 2 + half
                lanes = slice(half * BLOCK, (half + 1) * BLOCK)
                prob = jnp.exp(s2[:, lanes] + bias - fin_ref[qb, h : h + 1])
                probs[u, h] = prob.astype(BF16)
                delta = fin_ref[qb, HEADS + h : HEADS + h + 1]
                dscores[u, h] = (prob * (d2[:, lanes] - delta)).astype(BF16)

    def kept_scores(t, u):
        qb = unpacked(list_ref[t])[0]
        factor = jnp.exp(peaks_ref[t] - fin_ref[qb, :HEADS])
        for h in range(HEADS):
            prob = kept_e[t, h].astype(F32) * factor[h : h + 1]
            probs[u, h] = prob.astype(BF16)
            delta = fin_ref[qb, HEADS + h : HEADS + h + 1]
            dscores[u, h] = (prob * (kept_d[t, h].astype(F32) - delta)).astype(BF16)

    def products(t, u):
        qb, kb = unpacked(list_ref[t])[:2]
        for pair in range(HEADS // 2):
            for h in (2 * pair, 2 * pair + 1):
                head = slice(h * HEAD_DIM, (h + 1) * HEAD_DIM)
                ghead = slice(D + h * HEAD_DIM, D + (h + 1) * HEAD_DIM)
                acc[qb, head] += dot(vt_ref[kb, head], probs[u, h])
                acc[qb, ghead] += dot(kt_ref[kb, head], dscores[u, h])
            two = slice(pair * 128, pair * 128 + 128)
            low = jnp.concatenate([probs[u, 2 * pair], probs[u, 2 * pair + 1]], axis=1)
            ds = jnp.concatenate([dscores[u, 2 * pair], dscores[u, 2 * pair + 1]], axis=1)
            kacc[kb, :, two] += dot(ds, lane_split(qn_ref[qb, :, two]))
            vacc[kb, :, two] += dot(low, lane_split(gn_ref[qb, :, two]))

    def step(find, g, carry):
        for u in range(UNROLL):
            find(g * UNROLL + u, u)
        for u in range(UNROLL):
            products(g * UNROLL + u, u)
        return carry

    groups = (count + UNROLL - 1) // UNROLL
    kept = jnp.minimum(groups, KEPT // UNROLL)
    lax.fori_loop(0, kept, functools.partial(step, kept_scores), 0)
    lax.fori_loop(kept, groups, functools.partial(step, scores), 0)


def grads(tiles, arrays, acc, kacc, vacc):
    smem, vmem = pl.BlockSpec(memory_space=pltpu.SMEM), pl.BlockSpec(memory_space=VMEM)
    first = 1 + len(arrays)
    return pl.pallas_call(
        grad_kernel,
        out_shape=[
            VMEM(acc.shape, F32),
            VMEM(kacc.shape, F32),
            VMEM(vacc.shape, F32),
        ],
        in_specs=[smem] + [vmem] * (len(arrays) + 3),
        out_specs=[vmem] * 3,
        scratch_shapes=[VMEM((UNROLL, HEADS, BLOCK, BLOCK), BF16)] * 2,
        input_output_aliases={first: 0, first + 1: 1, first + 2: 2},
        compiler_params=pltpu.CompilerParams(vmem_limit_bytes=5 * 2**20),
        name="grads",
    )(tiles, *arrays, acc, kacc, vacc)


class HalfReduce:
    def __init__(self, links, base, buf, land, quarters, out, first, second):
        self.links, self.base, self.buf, self.land, self.quarters, self.out = links, base, buf, land, quarters, out
        self.me1, self.up1, self.down1 = first
        self.me2, self.up2, self.down2 = second

    def at(self, d1, d2):
        return ahead(self.me2, d2), ahead(self.me1, d1)

    def send(self, d1, d2, channel, src, to):
        self.links.start(self.base + channel, src, self.land.at[channel], to)

    def landed(self, channel):
        self.links.arrive(self.base + channel, self.land.at[channel])
        return self.land[channel].astype(F32)

    def first(self):
        for d1 in (1, 2, 0, 3):
            self.send(d1, 2, 12 + d1, self.buf.at[self.at(d1, 2)], self.up2 if d1 < 2 else self.down2)

    def direct(self, d1):
        up = d1 >= 2
        d2, channel = (1, 4 + d1) if up else (3, 8 + d1)
        self.send(d1, d2, channel, self.buf.at[self.at(d1, d2)], self.up2 if up else self.down2)

    def middle(self, d1):
        up = d1 < 2
        d2, channel = (1, 4 + d1) if up else (3, 8 + d1)
        total = self.buf[self.at(d1, d2)].astype(F32) + self.landed(12 + d1)
        self.out[d1] = total.astype(BF16)
        self.send(d1, d2, channel, self.out.at[d1], self.up2 if up else self.down2)

    def row(self, d1):
        return self.buf[self.at(d1, 0)].astype(F32) + self.landed(4 + d1) + self.landed(8 + d1)

    def cross(self):
        self.out[4] = self.row(2).astype(BF16)
        for q, to in ((0, self.up1), (1, self.down1)):
            rows = pl.ds(q * QUARTER, QUARTER)
            self.links.start(self.base + 2 + q, self.out.at[4, rows], self.quarters.at[rows], to)

    def final_up(self):
        up = self.row(1)
        self.links.arrive(self.base + 2, self.quarters.at[pl.ds(0, QUARTER)])
        self.out[5, :QUARTER] = (up[:QUARTER] + self.quarters[:QUARTER].astype(F32)).astype(BF16)
        self.out[5, QUARTER:] = up[QUARTER:].astype(BF16)
        self.send(1, 0, 0, self.out.at[5], self.up1)

    def final_down(self):
        down = self.row(3)
        self.links.arrive(self.base + 3, self.quarters.at[pl.ds(QUARTER, QUARTER)])
        self.out[6, :QUARTER] = down[:QUARTER].astype(BF16)
        self.out[6, QUARTER:] = (down[QUARTER:] + self.quarters[QUARTER:].astype(F32)).astype(BF16)
        self.send(3, 0, 1, self.out.at[6], self.down1)

    def result(self):
        return self.row(0) + self.landed(0) + self.landed(1)


def reduce_kernel(
    p_ref, kacc, vacc, wq_ref, wkt_ref, wvt_ref, attn_ref, grad_ref,
    low, high, to_sib, from_sib, sums, land, kland, quarters, ksums, send, recv,
):
    x, y, z, core, _ = place()
    xp, xm, yp, ym, zp, zm, sib = neighbours()
    links = Links(send, recv, sib)
    begin = enter()
    order = [2, 1, 3, 0]
    part = lambda c: pl.ds(c * D, D)
    parts = [(0, 0), (0, 1), (1, 1), (2, 0), (1, 0), (2, 1), (3, 0), (3, 1)]
    rings = [
        HalfReduce(links, 16, low, kland.at[0], quarters.at[0], ksums.at[0], (x, xp, xm), (y, yp, ym)),
        HalfReduce(links, 32, high, kland.at[1], quarters.at[1], ksums.at[1], (y, yp, ym), (x, xp, xm)),
    ]

    def block(i, c, mine):
        return p_ref[ahead(z, order[i]) * 2 + (core if mine else 1 - core), part(c)]

    def weigh(half, d):
        at = ahead(x if half else y, d)
        total = 0.0
        for found, weight in ((kacc, wkt_ref), (vacc, wvt_ref)):
            rows = found[at, :, HALF:] if half else found[:, at, :HALF]
            total += dot(rows.reshape(4 * HALF, D).astype(BF16), weight[...])
        (high if half else low)[at] = total.reshape(4, HALF, D).astype(BF16)

    for i, c in parts[:4]:
        to_sib[i, c] = block(i, c, False).astype(BF16)
    weigh(0, 2)
    begin()
    for i, c in parts[:4]:
        links.start(8 + 2 * i + c, to_sib.at[i, c], from_sib.at[i, c], sib)
    rings[0].first()
    weigh(1, 2)
    rings[1].first()
    for i, c in parts[4:]:
        to_sib[i, c] = block(i, c, False).astype(BF16)
        links.start(8 + 2 * i + c, to_sib.at[i, c], from_sib.at[i, c], sib)

    def both(i, c):
        links.arrive(8 + 2 * i + c, from_sib.at[i, c])
        return block(i, c, True) + from_sib[i, c].astype(F32)

    def put(channel, i, c, value, to):
        sums[i, c] = value.astype(BF16)
        links.start(channel, sums.at[i, c], land.at[channel], to)

    def landed(channel):
        links.arrive(channel, land.at[channel])
        return land[channel].astype(F32)

    for half, ring in enumerate(rings):
        weigh(half, 1)
        weigh(half, 3)
        ring.direct(2)
    put(0, 0, 0, both(0, 0), zp)
    put(1, 0, 1, both(0, 1), zm)
    for ring in rings:
        ring.middle(2)
        ring.direct(1)
    put(2, 1, 1, both(1, 1), zp)
    put(3, 2, 0, both(2, 0), zm)
    for ring in rings:
        ring.middle(1)
        ring.direct(3)
    for ring in rings:
        ring.middle(3)
    weigh(0, 0)
    weigh(1, 0)
    for ring in rings:
        ring.cross()
    for ring in rings:
        ring.middle(0)
        ring.direct(0)
    up, down = both(1, 0), both(2, 1)
    put(4, 1, 0, up + landed(0), zp)
    put(5, 2, 1, down + landed(1), zm)
    for ring in rings:
        ring.final_up()
    for ring in rings:
        ring.final_down()
    attn_ref[...] = (both(3, 0) + landed(3) + landed(4)).T.astype(BF16)
    queries = ((both(3, 1) + landed(2) + landed(5)) * SCALE).astype(BF16)
    nodes = dot(wq_ref[...], queries).T
    for half, ring in enumerate(rings):
        rows = slice(half * HALF, (half + 1) * HALF)
        grad_ref[rows] = (nodes[rows] + ring.result()).astype(BF16)
    links.finish()


def reduce(parts, kacc, vacc, wq, wkt, wvt):
    vmem = pl.BlockSpec(memory_space=VMEM)
    block = (2, D, BLOCK)
    return pl.pallas_call(
        reduce_kernel,
        out_shape=[VMEM((BLOCK, D), BF16)] * 2,
        in_specs=[vmem] * 6,
        out_specs=[vmem] * 2,
        scratch_shapes=[
            VMEM((4, 4, HALF, D), BF16),
            VMEM((4, 4, HALF, D), BF16),
            VMEM((4, *block), BF16),
            VMEM((4, *block), BF16),
            VMEM((3, *block), BF16),
            VMEM((6, D, BLOCK), BF16),
            VMEM((2, 16, HALF, D), BF16),
            VMEM((2, HALF, D), BF16),
            VMEM((2, 7, HALF, D), BF16),
            pltpu.SemaphoreType.DMA((48,)),
            pltpu.SemaphoreType.DMA((48,)),
        ],
        compiler_params=pltpu.CompilerParams(
            collective_id=2, has_side_effects=True, vmem_limit_bytes=24 * 2**20
        ),
        name="reduce",
    )(parts, kacc.reshape(4, 4, BLOCK, D), vacc.reshape(4, 4, BLOCK, D), wq, wkt, wvt)


def finish_kernel(attn_ref, grad_ref, attn_out, grad_out, sems):
    copies = [
        pltpu.make_async_copy(attn_ref, attn_out, sems.at[0]),
        pltpu.make_async_copy(grad_ref, grad_out, sems.at[1]),
    ]
    for copy in copies:
        copy.start()
    for copy in copies:
        copy.wait()


def finish(attn, grad):
    vmem, hbm = pl.BlockSpec(memory_space=VMEM), pl.BlockSpec(memory_space=pltpu.HBM)
    return pl.pallas_call(
        finish_kernel,
        out_shape=[jax.ShapeDtypeStruct((BLOCK, D), BF16)] * 2,
        in_specs=[vmem] * 2,
        out_specs=[hbm] * 2,
        scratch_shapes=[pltpu.SemaphoreType.DMA((2,))],
        compiler_params=pltpu.CompilerParams(vmem_limit_bytes=4 * 2**20),
        name="finish",
    )(attn, grad)


def local(features, cotangent, w_query, w_key, w_value, tile_coords, tile_count, mask_table):
    masks = mask_table.transpose(0, 2, 1)
    coords = tile_coords.transpose(0, 3, 1, 2)
    found = gather(features, cotangent, w_query, w_key, w_value, masks, coords, tile_count)
    qt, gt, qn, gn, keys, values = (a.reshape(-1, *a.shape[2:]) for a in found[:6])
    masks, wq, wk, wv, coords, coords2, count2 = found[6:]
    partial, tiles, *kept = stats(tile_count, coords, count2, coords2, qt, gt, keys, values, masks)
    fin, acc, kacc, vacc, keys_t, values_t, wkt, wvt = merge(partial, keys, values, wk, wv, *kept[:2])
    arrays = (qt, gt, qn, gn, keys, values, keys_t, values_t, masks, fin, *kept)
    parts, kacc, vacc = grads(tiles, arrays, acc, kacc, vacc)
    return tuple(finish(*reduce(parts, kacc, vacc, wq, wkt, wvt)))


def solution(mesh):
    return jax.shard_map(
        local,
        mesh=mesh,
        in_specs=(
            P(("reader", "blk"), None),
            P(("reader", "blk"), None),
            P(),
            P(),
            P(),
            P("reader", "blk", None, None),
            P("reader", "blk"),
            P(),
        ),
        out_specs=(P(("reader", "blk"), None), P(("reader", "blk"), None)),
        check_vma=False,
    )
```

```python
import functools

import jax
import jax.numpy as jnp
from jax import lax
from jax.experimental import pallas as pl
from jax.experimental.pallas import tpu as pltpu
from jax.sharding import PartitionSpec as P

HEADS = 8
HEAD_DIM = 64
D = 512
BLOCK = 128
SCALE = 0.125
FLOOR = -1e20
NEG_FILL = -1e30
MESH = pl.DeviceIdType.MESH
F32 = jnp.float32
BF16 = jnp.bfloat16
VMEM = pltpu.VMEM


def dot(a, b):
    return jnp.dot(a, b, preferred_element_type=F32)


def remote(src, dst, send, recv, device):
    return pltpu.make_async_remote_copy(
        src_ref=src, dst_ref=dst, send_sem=send, recv_sem=recv, device_id=device, device_id_type=MESH
    )


class Links:
    def __init__(self, send, recv, self_device):
        self.send, self.recv, self.anyone, self.started = send, recv, self_device, {}

    def start(self, i, src, dst, device):
        copy = remote(src, dst, self.send.at[i], self.recv.at[i], device)
        self.started[i] = copy
        copy.start()

    def arrive(self, i, dst):
        remote(dst, dst, self.send.at[i], self.recv.at[i], self.anyone).wait_recv()

    def finish(self):
        for copy in self.started.values():
            copy.wait_send()


def place():
    reader, blk = lax.axis_index("reader"), lax.axis_index("blk")
    side = lax.rem(blk // 2, 2)
    return (reader // 4) * 2 + side, lax.rem(reader, 4), blk // 4, lax.rem(blk, 2), side


def device(x, y, z, core):
    return (x // 2) * 4 + y, z * 4 + lax.rem(x, 2) * 2 + core


def ahead(i, d):
    return lax.rem(i + d, 4)


def neighbours():
    x, y, z, core, _ = place()
    return (
        device(ahead(x, 1), y, z, core),
        device(ahead(x, 3), y, z, core),
        device(x, ahead(y, 1), z, core),
        device(x, ahead(y, 3), z, core),
        device(x, y, ahead(z, 1), core),
        device(x, y, ahead(z, 3), core),
        device(x, y, z, 1 - core),
    )


def enter():
    barrier = pltpu.get_barrier_semaphore()
    for one in neighbours():
        pl.semaphore_signal(barrier, inc=1, device_id=one, device_id_type=MESH)
    return lambda: pl.semaphore_wait(barrier, 7)


HALF = BLOCK // 2
QUARTER = HALF // 2


class HalfGather:
    def __init__(self, links, base, buf, source, first, second):
        self.links, self.base, self.buf, self.source = links, base, buf, source
        self.me1, self.up1, self.down1 = first
        self.me2, self.up2, self.down2 = second

    def piece(self, d1, d2):
        return self.buf.at[ahead(self.me2, d2), ahead(self.me1, d1)]

    def quarter(self, d1, q):
        return self.buf.at[self.me2, ahead(self.me1, d1), pl.ds(q * QUARTER, QUARTER)]

    def spread(self, d1):
        ref = self.piece(d1, 0)
        self.links.start(self.base + 4 + d1, ref, ref, self.up2)
        self.links.start(self.base + 8 + d1, ref, ref, self.down2)

    def own(self):
        ref = self.piece(0, 0)
        self.links.start(self.base, self.source, ref, self.up1)
        self.links.start(self.base + 1, self.source, ref, self.down1)

    def near(self):
        self.links.arrive(self.base, self.piece(3, 0))
        self.links.start(self.base + 2, self.quarter(3, 0), self.quarter(3, 0), self.up1)
        self.links.arrive(self.base + 1, self.piece(1, 0))
        self.links.start(self.base + 3, self.quarter(1, 1), self.quarter(1, 1), self.down1)

    def far(self):
        self.links.arrive(self.base + 2, self.quarter(2, 0))
        self.links.arrive(self.base + 3, self.quarter(2, 1))
        self.spread(2)

    def relay(self, d1):
        up = d1 < 2
        ref = self.piece(d1, 3 if up else 1)
        self.links.arrive(self.base + (4 if up else 8) + d1, ref)
        self.links.start(self.base + 12 + d1, ref, ref, self.up2 if up else self.down2)

    def rest(self, up):
        for d1 in (3, 2) if up else (0, 1):
            self.links.arrive(self.base + (4 if up else 8) + d1, self.piece(d1, 3 if up else 1))

    def last(self):
        for d1 in (0, 3, 1, 2):
            self.links.arrive(self.base + 12 + d1, self.piece(d1, 2))


def gather_kernel(
    x_hbm, g_hbm, wq_hbm, wk_hbm, wv_hbm, mask_hbm, coords_hbm, count_ref,
    qt_ref, gt_ref, qn_ref, gn_ref, k_ref, v_ref, mask_ref, wq_ref, wk_ref, wv_ref, coords_own, coords_out, count_out,
    xb, low, high, count_buf, send, recv, local,
):
    x, y, z, core, side = place()
    xp, xm, yp, ym, zp, zm, sib = neighbours()
    links = Links(send, recv, sib)
    begin = enter()
    count_buf[...] = jnp.full(count_buf.shape, count_ref[0, 0], jnp.int32)
    loads = [
        pltpu.make_async_copy(src, dst, local.at[i])
        for i, (src, dst) in enumerate(
            [
                (x_hbm.at[pl.ds(0, HALF)], low.at[y, x]), (x_hbm.at[pl.ds(HALF, HALF)], high.at[x, y]),
                (x_hbm, xb.at[z, core]), (g_hbm, gn_ref.at[z, core]), (wk_hbm, wk_ref), (wv_hbm, wv_ref),
                (wq_hbm, wq_ref), (mask_hbm, mask_ref), (coords_hbm, coords_own),
            ]
        )
    ]
    for load in loads:
        load.start()
    rings = [
        HalfGather(links, 16, low, low.at[y, x], (x, xp, xm), (y, yp, ym)),
        HalfGather(links, 32, high, high.at[x, y], (y, yp, ym), (x, xp, xm)),
    ]
    for i in range(4):
        loads[i].wait()
    begin()

    for ring in rings:
        ring.own()
    for ring in rings:
        ring.spread(0)
    links.start(0, xb.at[z, core], xb.at[z, core], zp)
    links.start(2, xb.at[z, core], xb.at[z, core], zm)
    links.start(1, gn_ref.at[z, core], gn_ref.at[z, core], zp)
    links.start(3, gn_ref.at[z, core], gn_ref.at[z, core], zm)
    links.start(8, xb.at[z, core], xb.at[z, core], sib)
    links.start(9, gn_ref.at[z, core], gn_ref.at[z, core], sib)
    other = device(x + 1 - 2 * side, y, z, core)
    links.start(6, coords_hbm, coords_out, other)
    links.start(7, count_buf, count_out, other)

    def arrive(i, ref, dz, c=core):
        links.arrive(i, ref.at[ahead(z, dz), c])

    def pass_on(i, ref, dz, to):
        block = ref.at[ahead(z, dz), core]
        links.start(i, block, block, to)

    def prepare(dz):
        b = ahead(z, dz)
        rows = xb[b].reshape(2 * BLOCK, D)
        q = (dot(rows, wq_ref[...]).astype(BF16).astype(F32) * SCALE).astype(BF16)
        for c in range(2):
            one = q[c * BLOCK : (c + 1) * BLOCK]
            qn_ref[b, c] = one
            qt_ref[b, c] = one.T
            gt_ref[b, c] = gn_ref[b, c].T

    def project(half, d):
        at = ahead(x if half else y, d)
        rows = (high if half else low)[at].reshape(4 * HALF, D)
        for weight, out in ((wk_ref, k_ref), (wv_ref, v_ref)):
            found = dot(rows, weight[...]).astype(BF16).reshape(4, HALF, D)
            if half:
                out[at, :, HALF:] = found
            else:
                out[:, at, :HALF] = found

    for ring in rings:
        ring.near()
    for ring in rings:
        ring.spread(3)
        ring.spread(1)
    arrive(0, xb, 3)
    pass_on(4, xb, 3, zp)
    for ring in rings:
        ring.far()
    for ring in rings:
        ring.relay(0)
        ring.relay(3)
    for ring in rings:
        ring.relay(1)
    pass_on(10, xb, 3, sib)
    arrive(2, xb, 1)
    pass_on(12, xb, 1, sib)
    for i in range(4, 7):
        loads[i].wait()
    project(0, 0)
    project(1, 0)

    arrive(3, gn_ref, 1)
    pass_on(5, gn_ref, 1, zm)
    pass_on(13, gn_ref, 1, sib)
    arrive(1, gn_ref, 3)
    pass_on(11, gn_ref, 3, sib)
    for ring in rings:
        ring.relay(2)
    arrive(8, xb, 0, 1 - core)
    arrive(9, gn_ref, 0, 1 - core)
    prepare(0)
    for half, ring in enumerate(rings):
        ring.rest(True)
        project(half, 3)
        ring.rest(False)
        project(half, 1)
    arrive(4, xb, 2)
    pass_on(14, xb, 2, sib)
    for i, dz in ((10, 3), (12, 1)):
        arrive(i, xb, dz, 1 - core)
        arrive(i + 1, gn_ref, dz, 1 - core)
        prepare(dz)
        if i == 10:
            arrive(5, gn_ref, 2)
            pass_on(15, gn_ref, 2, sib)
    arrive(14, xb, 2, 1 - core)
    arrive(15, gn_ref, 2, 1 - core)
    prepare(2)
    for half, ring in enumerate(rings):
        ring.last()
        project(half, 2)
    links.arrive(6, coords_out)
    links.arrive(7, count_out)
    loads[7].wait()
    loads[8].wait()
    links.finish()


def gather(features, cotangent, w_query, w_key, w_value, masks, coords, count):
    hbm, vmem = pl.BlockSpec(memory_space=pltpu.HBM), pl.BlockSpec(memory_space=VMEM)
    operands = (features, cotangent, w_query, w_key, w_value, masks, coords)
    return pl.pallas_call(
        gather_kernel,
        out_shape=[
            VMEM((4, 2, D, BLOCK), BF16),
            VMEM((4, 2, D, BLOCK), BF16),
            VMEM((4, 2, BLOCK, D), BF16),
            VMEM((4, 2, BLOCK, D), BF16),
            VMEM((4, 4, BLOCK, D), BF16),
            VMEM((4, 4, BLOCK, D), BF16),
            VMEM(masks.shape, jnp.int32),
            VMEM((D, D), BF16),
            VMEM((D, D), BF16),
            VMEM((D, D), BF16),
            VMEM(coords.shape, jnp.int32),
            VMEM(coords.shape, jnp.int32),
            VMEM((8, 128), jnp.int32),
        ],
        in_specs=[hbm] * 7 + [pl.BlockSpec(memory_space=pltpu.SMEM)],
        out_specs=[vmem] * 13,
        scratch_shapes=[
            VMEM((4, 2, BLOCK, D), BF16),
            VMEM((4, 4, HALF, D), BF16),
            VMEM((4, 4, HALF, D), BF16),
            VMEM((8, 128), jnp.int32),
            pltpu.SemaphoreType.DMA((48,)),
            pltpu.SemaphoreType.DMA((48,)),
            pltpu.SemaphoreType.DMA((9,)),
        ],
        compiler_params=pltpu.CompilerParams(
            collective_id=0, has_side_effects=True, vmem_limit_bytes=16 * 2**20
        ),
        name="gather",
    )(*(pltpu.with_memory_space_constraint(a, pltpu.HBM) for a in operands), count)


def tile_bias(words, first, used):
    spread = jnp.concatenate(
        [jnp.broadcast_to(words[w : w + 1], (32, BLOCK)) for w in range(BLOCK // 32)], axis=0
    )
    key = lax.broadcasted_iota(jnp.int32, (BLOCK, BLOCK), 0)
    query = lax.broadcasted_iota(jnp.int32, (BLOCK, BLOCK), 1)
    bits = (lax.shift_right_logical(spread, key & 31) | jnp.where(key == query, first, 0)) & used
    return jnp.where(bits > 0, 0.0, NEG_FILL).astype(F32)


def pair_product(left, right):
    zero = jnp.zeros((HEAD_DIM, BLOCK), right.dtype)
    top = jnp.concatenate([right[:HEAD_DIM], zero], axis=1)
    bottom = jnp.concatenate([zero, right[HEAD_DIM:]], axis=1)
    return dot(left, jnp.concatenate([top, bottom], axis=0))


UNROLL = 4
WIDE = 8
LIST = 2 * 32 + UNROLL
KEPT = 32


def unpacked(word):
    return word & 7, lax.shift_right_logical(word, 3) & 15, lax.shift_right_logical(word, 8), lax.shift_right_logical(word, 7) & 1


def stats_kernel(
    count_ref, coords_ref, count2_ref, coords2_ref, qt_ref, gt_ref, k_ref, v_ref, mask_ref,
    out_ref, list_ref, kept_e, kept_d, peaks_ref, run,
):
    nb = run.shape[0]
    row = lax.broadcasted_iota(jnp.int32, run.shape, 1)
    run[...] = jnp.where(row < HEADS, FLOOR, 0.0).astype(F32)
    side = lax.rem(lax.axis_index("blk") // 2, 2)

    def collect(counts, coords, column, found):
        def one(i, found):
            qb, kb, p = (coords[0, c, 0, i] for c in range(3))
            key = lax.shift_right_logical(kb, 2) * 8 + column * 4 + (kb & 3)
            first = jnp.where(i + found + (column != side) == 0, 128, 0)
            list_ref[found] = lax.shift_right_logical(qb, 2) * 2 + (qb & 1) + key * 8 + first + p * 256
            return found + jnp.where((lax.shift_right_logical(qb, 1) & 1) == side, 1, 0)

        return lax.fori_loop(0, counts[0, 0], one, found)

    count = collect(count_ref, coords_ref, side, 0)
    count = collect(count2_ref, coords2_ref, 1 - side, count)
    for u in range(UNROLL):
        list_ref[count + u] = 0
    list_ref[LIST] = count

    def tile(t):
        qb, kb, p, first = unpacked(list_ref[t])
        bias = tile_bias(mask_ref[p], first, jnp.where(t < count, 1, 0))
        slot = jnp.minimum(t, KEPT)
        peaks, totals, dots = [], [], []
        for pair in range(HEADS // 2):
            two = slice(pair * 128, pair * 128 + 128)
            s2 = pair_product(k_ref[kb, :, two], qt_ref[qb, two])
            d2 = pair_product(v_ref[kb, :, two], gt_ref[qb, two])
            for half in range(2):
                h = 2 * pair + half
                lanes = slice(half * BLOCK, (half + 1) * BLOCK)
                s = s2[:, lanes] + bias
                peak = jnp.max(s, axis=0, keepdims=True)
                e = jnp.exp(s - peak)
                kept_e[slot, h] = e.astype(BF16)
                kept_d[slot, h] = d2[:, lanes].astype(BF16)
                peaks.append(peak)
                totals.append(jnp.sum(e, axis=0, keepdims=True))
                dots.append(jnp.sum(e * d2[:, lanes], axis=0, keepdims=True))
        peak, total, dot_sum = (jnp.concatenate(rows, axis=0) for rows in (peaks, totals, dots))
        peaks_ref[slot] = peak
        return qb, peak, total, dot_sum

    def add(qb, peak, total, dots):
        before = run[qb, :HEADS]
        m = jnp.maximum(before, peak)
        old, new = jnp.exp(before - m), jnp.exp(peak - m)
        run[qb, :HEADS] = m
        run[qb, HEADS : 2 * HEADS] = run[qb, HEADS : 2 * HEADS] * old + total * new
        run[qb, 2 * HEADS :] = run[qb, 2 * HEADS :] * old + dots * new

    def step(width, g, carry):
        for found in [tile(g * width + u) for u in range(width)]:
            add(*found)
        return carry

    wide = count // WIDE
    lax.fori_loop(0, wide, functools.partial(step, WIDE), 0)
    groups = (count + UNROLL - 1) // UNROLL
    lax.fori_loop(wide * (WIDE // UNROLL), groups, functools.partial(step, UNROLL), 0)
    for b in range(nb):
        total = jnp.maximum(run[b, HEADS : 2 * HEADS], 1e-30)
        out_ref[b, :HEADS] = run[b, :HEADS] + jnp.log(total)
        out_ref[b, HEADS:] = run[b, 2 * HEADS :] / total


def stats(count, coords, count2, coords2, qt, gt, keys, values, masks):
    nb = qt.shape[0]
    smem, vmem = pl.BlockSpec(memory_space=pltpu.SMEM), pl.BlockSpec(memory_space=VMEM)
    return pl.pallas_call(
        stats_kernel,
        out_shape=[
            VMEM((nb, 2 * HEADS, BLOCK), F32),
            jax.ShapeDtypeStruct((LIST + 1,), jnp.int32),
            VMEM((KEPT + 1, HEADS, BLOCK, BLOCK), BF16),
            VMEM((KEPT + 1, HEADS, BLOCK, BLOCK), BF16),
            VMEM((KEPT + 1, HEADS, BLOCK), F32),
        ],
        in_specs=[smem] * 4 + [vmem] * 5,
        out_specs=[vmem, smem, vmem, vmem, vmem],
        scratch_shapes=[VMEM((nb, 3 * HEADS, BLOCK), F32)],
        compiler_params=pltpu.CompilerParams(vmem_limit_bytes=4 * 2**20),
        name="stats",
    )(count, coords, count2, coords2, qt, gt, keys, values, masks)


def merge_kernel(
    st_ref, k_ref, v_ref, wk_ref, wv_ref, kept_e, kept_d, out_ref, acc, kacc, vacc, kt_ref, vt_ref, wkt_ref, wvt_ref,
    land, fin, send, recv, fsend, frecv,
):
    x, y, z, core, _ = place()
    nb = st_ref.shape[0]
    me = z * 2 + core
    block = lambda d: lax.rem(me + d, nb)
    peer = lambda d: device(x, y, block(d) // 2, lax.rem(block(d), 2))
    source = lambda d: lax.rem(me + nb - d, nb)
    barrier = pltpu.get_barrier_semaphore()
    for d in range(1, nb):
        pl.semaphore_signal(barrier, inc=1, device_id=peer(d), device_id_type=MESH)

    def part(d):
        return remote(st_ref.at[block(d)], land.at[d], send.at[d], recv.at[d], peer(d))

    def whole(d):
        return remote(fin.at[0], fin.at[d], fsend.at[d], frecv.at[d], peer(d))

    def turn(b, carry):
        kt_ref[b] = k_ref[b].T
        vt_ref[b] = v_ref[b].T
        return carry

    def clear(b, carry):
        kacc[b] = jnp.zeros(kacc.shape[1:], F32)
        vacc[b] = jnp.zeros(vacc.shape[1:], F32)
        return carry

    def clear_queries(b, carry):
        acc[b] = jnp.zeros(acc.shape[1:], F32)
        return carry

    wkt_ref[...] = wk_ref[...].T
    wvt_ref[...] = wv_ref[...].T
    pl.semaphore_wait(barrier, nb - 1)
    for d in (4, 3, 5, 2, 6, 1, 7):
        part(d).start()
    land[0] = st_ref[me]
    lax.fori_loop(0, 16, turn, 0)
    for d in range(1, nb):
        part(d).wait()
    m = land[0, :HEADS]
    for d in range(1, nb):
        m = jnp.maximum(m, land[d, :HEADS])
    total = jnp.zeros_like(m)
    dots = jnp.zeros_like(m)
    for d in range(nb):
        weight = jnp.exp(land[d, :HEADS] - m)
        total += weight
        dots += land[d, HEADS:] * weight
    fin[0, :HEADS] = m + jnp.log(total)
    fin[0, HEADS:] = dots / total
    for d in (4, 3, 5, 2, 6, 1, 7):
        whole(d).start()
    out_ref[me] = fin[0]
    lax.fori_loop(0, 16, clear, 0)
    lax.fori_loop(0, nb, clear_queries, 0)
    for d in range(1, nb):
        whole(d).wait()
        out_ref[source(d)] = fin[d]


def merge(partial, keys, values, wk, wv, kept_e, kept_d):
    nb, nk = partial.shape[0], keys.shape[0]
    vmem = pl.BlockSpec(memory_space=VMEM)
    return pl.pallas_call(
        merge_kernel,
        out_shape=[
            VMEM(partial.shape, F32),
            VMEM((nb, 2 * D, BLOCK), F32),
            VMEM((nk, BLOCK, D), F32),
            VMEM((nk, BLOCK, D), F32),
            VMEM((nk, D, BLOCK), BF16),
            VMEM((nk, D, BLOCK), BF16),
            VMEM((D, D), BF16),
            VMEM((D, D), BF16),
        ],
        in_specs=[vmem] * 7,
        out_specs=[vmem] * 8,
        scratch_shapes=[
            VMEM(partial.shape, F32),
            VMEM(partial.shape, F32),
            *[pltpu.SemaphoreType.DMA((nb,))] * 4,
        ],
        compiler_params=pltpu.CompilerParams(
            collective_id=1, has_side_effects=True, vmem_limit_bytes=4 * 2**20
        ),
        name="merge",
    )(partial, keys, values, wk, wv, *(pltpu.with_memory_space_constraint(a, pltpu.VMEM) for a in (kept_e, kept_d)))


def lane_split(block):
    lane = lax.broadcasted_iota(jnp.int32, block.shape, 1)
    zero = jnp.zeros_like(block)
    return jnp.concatenate(
        [jnp.where(lane < HEAD_DIM, block, zero), jnp.where(lane >= HEAD_DIM, block, zero)], axis=0
    )


def grad_kernel(
    list_ref, qt_ref, gt_ref, qn_ref, gn_ref, k_ref, v_ref, kt_ref, vt_ref, mask_ref, fin_ref,
    kept_e, kept_d, peaks_ref, acc_in, kacc_in, vacc_in, acc, kacc, vacc, probs, dscores,
):
    count = list_ref[LIST]

    def scores(t, u):
        qb, kb, p, first = unpacked(list_ref[t])
        bias = tile_bias(mask_ref[p], first, jnp.where(t < count, 1, 0))
        for pair in range(HEADS // 2):
            two = slice(pair * 128, pair * 128 + 128)
            s2 = pair_product(k_ref[kb, :, two], qt_ref[qb, two])
            d2 = pair_product(v_ref[kb, :, two], gt_ref[qb, two])
            for half in range(2):
                h = pair * 2 + half
                lanes = slice(half * BLOCK, (half + 1) * BLOCK)
                prob = jnp.exp(s2[:, lanes] + bias - fin_ref[qb, h : h + 1])
                probs[u, h] = prob.astype(BF16)
                delta = fin_ref[qb, HEADS + h : HEADS + h + 1]
                dscores[u, h] = (prob * (d2[:, lanes] - delta)).astype(BF16)

    def kept_scores(t, u):
        qb = unpacked(list_ref[t])[0]
        factor = jnp.exp(peaks_ref[t] - fin_ref[qb, :HEADS])
        for h in range(HEADS):
            prob = kept_e[t, h].astype(F32) * factor[h : h + 1]
            probs[u, h] = prob.astype(BF16)
            delta = fin_ref[qb, HEADS + h : HEADS + h + 1]
            dscores[u, h] = (prob * (kept_d[t, h].astype(F32) - delta)).astype(BF16)

    def products(t, u):
        qb, kb = unpacked(list_ref[t])[:2]
        for pair in range(HEADS // 2):
            for h in (2 * pair, 2 * pair + 1):
                head = slice(h * HEAD_DIM, (h + 1) * HEAD_DIM)
                ghead = slice(D + h * HEAD_DIM, D + (h + 1) * HEAD_DIM)
                acc[qb, head] += dot(vt_ref[kb, head], probs[u, h])
                acc[qb, ghead] += dot(kt_ref[kb, head], dscores[u, h])
            two = slice(pair * 128, pair * 128 + 128)
            low = jnp.concatenate([probs[u, 2 * pair], probs[u, 2 * pair + 1]], axis=1)
            ds = jnp.concatenate([dscores[u, 2 * pair], dscores[u, 2 * pair + 1]], axis=1)
            kacc[kb, :, two] += dot(ds, lane_split(qn_ref[qb, :, two]))
            vacc[kb, :, two] += dot(low, lane_split(gn_ref[qb, :, two]))

    def step(find, g, carry):
        for u in range(UNROLL):
            find(g * UNROLL + u, u)
        for u in range(UNROLL):
            products(g * UNROLL + u, u)
        return carry

    groups = (count + UNROLL - 1) // UNROLL
    kept = jnp.minimum(groups, KEPT // UNROLL)
    lax.fori_loop(0, kept, functools.partial(step, kept_scores), 0)
    lax.fori_loop(kept, groups, functools.partial(step, scores), 0)


def grads(tiles, arrays, acc, kacc, vacc):
    smem, vmem = pl.BlockSpec(memory_space=pltpu.SMEM), pl.BlockSpec(memory_space=VMEM)
    first = 1 + len(arrays)
    return pl.pallas_call(
        grad_kernel,
        out_shape=[
            VMEM(acc.shape, F32),
            VMEM(kacc.shape, F32),
            VMEM(vacc.shape, F32),
        ],
        in_specs=[smem] + [vmem] * (len(arrays) + 3),
        out_specs=[vmem] * 3,
        scratch_shapes=[VMEM((UNROLL, HEADS, BLOCK, BLOCK), BF16)] * 2,
        input_output_aliases={first: 0, first + 1: 1, first + 2: 2},
        compiler_params=pltpu.CompilerParams(vmem_limit_bytes=5 * 2**20),
        name="grads",
    )(tiles, *arrays, acc, kacc, vacc)


class HalfReduce:
    def __init__(self, links, base, buf, land, quarters, out, first, second):
        self.links, self.base, self.buf, self.land, self.quarters, self.out = links, base, buf, land, quarters, out
        self.me1, self.up1, self.down1 = first
        self.me2, self.up2, self.down2 = second

    def at(self, d1, d2):
        return ahead(self.me2, d2), ahead(self.me1, d1)

    def send(self, d1, d2, channel, src, to):
        self.links.start(self.base + channel, src, self.land.at[channel], to)

    def landed(self, channel):
        self.links.arrive(self.base + channel, self.land.at[channel])
        return self.land[channel].astype(F32)

    def first(self):
        for d1 in (1, 2, 0, 3):
            self.send(d1, 2, 12 + d1, self.buf.at[self.at(d1, 2)], self.up2 if d1 < 2 else self.down2)

    def direct(self, d1):
        up = d1 >= 2
        d2, channel = (1, 4 + d1) if up else (3, 8 + d1)
        self.send(d1, d2, channel, self.buf.at[self.at(d1, d2)], self.up2 if up else self.down2)

    def middle(self, d1):
        up = d1 < 2
        d2, channel = (1, 4 + d1) if up else (3, 8 + d1)
        total = self.buf[self.at(d1, d2)].astype(F32) + self.landed(12 + d1)
        self.out[d1] = total.astype(BF16)
        self.send(d1, d2, channel, self.out.at[d1], self.up2 if up else self.down2)

    def row(self, d1):
        return self.buf[self.at(d1, 0)].astype(F32) + self.landed(4 + d1) + self.landed(8 + d1)

    def cross(self):
        self.out[4] = self.row(2).astype(BF16)
        for q, to in ((0, self.up1), (1, self.down1)):
            rows = pl.ds(q * QUARTER, QUARTER)
            self.links.start(self.base + 2 + q, self.out.at[4, rows], self.quarters.at[rows], to)

    def final_up(self):
        up = self.row(1)
        self.links.arrive(self.base + 2, self.quarters.at[pl.ds(0, QUARTER)])
        self.out[5, :QUARTER] = (up[:QUARTER] + self.quarters[:QUARTER].astype(F32)).astype(BF16)
        self.out[5, QUARTER:] = up[QUARTER:].astype(BF16)
        self.send(1, 0, 0, self.out.at[5], self.up1)

    def final_down(self):
        down = self.row(3)
        self.links.arrive(self.base + 3, self.quarters.at[pl.ds(QUARTER, QUARTER)])
        self.out[6, :QUARTER] = down[:QUARTER].astype(BF16)
        self.out[6, QUARTER:] = (down[QUARTER:] + self.quarters[QUARTER:].astype(F32)).astype(BF16)
        self.send(3, 0, 1, self.out.at[6], self.down1)

    def result(self):
        return self.row(0) + self.landed(0) + self.landed(1)


def reduce_kernel(
    p_ref, kacc, vacc, wq_ref, wkt_ref, wvt_ref, attn_ref, grad_ref,
    low, high, to_sib, from_sib, sums, land, kland, quarters, ksums, send, recv,
):
    x, y, z, core, _ = place()
    xp, xm, yp, ym, zp, zm, sib = neighbours()
    links = Links(send, recv, sib)
    begin = enter()
    order = [2, 1, 3, 0]
    part = lambda c: pl.ds(c * D, D)
    parts = [(0, 0), (0, 1), (1, 1), (2, 0), (1, 0), (2, 1), (3, 0), (3, 1)]
    rings = [
        HalfReduce(links, 16, low, kland.at[0], quarters.at[0], ksums.at[0], (x, xp, xm), (y, yp, ym)),
        HalfReduce(links, 32, high, kland.at[1], quarters.at[1], ksums.at[1], (y, yp, ym), (x, xp, xm)),
    ]

    def block(i, c, mine):
        return p_ref[ahead(z, order[i]) * 2 + (core if mine else 1 - core), part(c)]

    def weigh(half, d):
        at = ahead(x if half else y, d)
        total = 0.0
        for found, weight in ((kacc, wkt_ref), (vacc, wvt_ref)):
            rows = found[at, :, HALF:] if half else found[:, at, :HALF]
            total += dot(rows.reshape(4 * HALF, D).astype(BF16), weight[...])
        (high if half else low)[at] = total.reshape(4, HALF, D).astype(BF16)

    for i, c in parts[:4]:
        to_sib[i, c] = block(i, c, False).astype(BF16)
    weigh(0, 2)
    begin()
    for i, c in parts[:4]:
        links.start(8 + 2 * i + c, to_sib.at[i, c], from_sib.at[i, c], sib)
    rings[0].first()
    weigh(1, 2)
    rings[1].first()
    for i, c in parts[4:]:
        to_sib[i, c] = block(i, c, False).astype(BF16)
        links.start(8 + 2 * i + c, to_sib.at[i, c], from_sib.at[i, c], sib)

    def both(i, c):
        links.arrive(8 + 2 * i + c, from_sib.at[i, c])
        return block(i, c, True) + from_sib[i, c].astype(F32)

    def put(channel, i, c, value, to):
        sums[i, c] = value.astype(BF16)
        links.start(channel, sums.at[i, c], land.at[channel], to)

    def landed(channel):
        links.arrive(channel, land.at[channel])
        return land[channel].astype(F32)

    for half, ring in enumerate(rings):
        weigh(half, 1)
        weigh(half, 3)
        ring.direct(2)
    put(0, 0, 0, both(0, 0), zp)
    put(1, 0, 1, both(0, 1), zm)
    for ring in rings:
        ring.middle(2)
        ring.direct(1)
    put(2, 1, 1, both(1, 1), zp)
    put(3, 2, 0, both(2, 0), zm)
    for ring in rings:
        ring.middle(1)
        ring.direct(3)
    weigh(0, 0)
    weigh(1, 0)
    for ring in rings:
        ring.cross()
    for ring in rings:
        ring.middle(3)
    for ring in rings:
        ring.middle(0)
        ring.direct(0)
    up, down = both(1, 0), both(2, 1)
    put(4, 1, 0, up + landed(0), zp)
    put(5, 2, 1, down + landed(1), zm)
    for ring in rings:
        ring.final_up()
    for ring in rings:
        ring.final_down()
    attn_ref[...] = (both(3, 0) + landed(3) + landed(4)).T.astype(BF16)
    queries = ((both(3, 1) + landed(2) + landed(5)) * SCALE).astype(BF16)
    nodes = dot(wq_ref[...], queries).T
    for half, ring in enumerate(rings):
        rows = slice(half * HALF, (half + 1) * HALF)
        grad_ref[rows] = (nodes[rows] + ring.result()).astype(BF16)
    links.finish()


def reduce(parts, kacc, vacc, wq, wkt, wvt):
    vmem = pl.BlockSpec(memory_space=VMEM)
    block = (2, D, BLOCK)
    return pl.pallas_call(
        reduce_kernel,
        out_shape=[VMEM((BLOCK, D), BF16)] * 2,
        in_specs=[vmem] * 6,
        out_specs=[vmem] * 2,
        scratch_shapes=[
            VMEM((4, 4, HALF, D), BF16),
            VMEM((4, 4, HALF, D), BF16),
            VMEM((4, *block), BF16),
            VMEM((4, *block), BF16),
            VMEM((3, *block), BF16),
            VMEM((6, D, BLOCK), BF16),
            VMEM((2, 16, HALF, D), BF16),
            VMEM((2, HALF, D), BF16),
            VMEM((2, 7, HALF, D), BF16),
            pltpu.SemaphoreType.DMA((48,)),
            pltpu.SemaphoreType.DMA((48,)),
        ],
        compiler_params=pltpu.CompilerParams(
            collective_id=2, has_side_effects=True, vmem_limit_bytes=24 * 2**20
        ),
        name="reduce",
    )(parts, kacc.reshape(4, 4, BLOCK, D), vacc.reshape(4, 4, BLOCK, D), wq, wkt, wvt)


def finish_kernel(attn_ref, grad_ref, attn_out, grad_out, sems):
    copies = [
        pltpu.make_async_copy(attn_ref, attn_out, sems.at[0]),
        pltpu.make_async_copy(grad_ref, grad_out, sems.at[1]),
    ]
    for copy in copies:
        copy.start()
    for copy in copies:
        copy.wait()


def finish(attn, grad):
    vmem, hbm = pl.BlockSpec(memory_space=VMEM), pl.BlockSpec(memory_space=pltpu.HBM)
    return pl.pallas_call(
        finish_kernel,
        out_shape=[jax.ShapeDtypeStruct((BLOCK, D), BF16)] * 2,
        in_specs=[vmem] * 2,
        out_specs=[hbm] * 2,
        scratch_shapes=[pltpu.SemaphoreType.DMA((2,))],
        compiler_params=pltpu.CompilerParams(vmem_limit_bytes=4 * 2**20),
        name="finish",
    )(attn, grad)


def local(features, cotangent, w_query, w_key, w_value, tile_coords, tile_count, mask_table):
    masks = mask_table.transpose(0, 2, 1)
    coords = tile_coords.transpose(0, 3, 1, 2)
    found = gather(features, cotangent, w_query, w_key, w_value, masks, coords, tile_count)
    qt, gt, qn, gn, keys, values = (a.reshape(-1, *a.shape[2:]) for a in found[:6])
    masks, wq, wk, wv, coords, coords2, count2 = found[6:]
    partial, tiles, *kept = stats(tile_count, coords, count2, coords2, qt, gt, keys, values, masks)
    fin, acc, kacc, vacc, keys_t, values_t, wkt, wvt = merge(partial, keys, values, wk, wv, *kept[:2])
    arrays = (qt, gt, qn, gn, keys, values, keys_t, values_t, masks, fin, *kept)
    parts, kacc, vacc = grads(tiles, arrays, acc, kacc, vacc)
    return tuple(finish(*reduce(parts, kacc, vacc, wq, wkt, wvt)))


def solution(mesh):
    return jax.shard_map(
        local,
        mesh=mesh,
        in_specs=(
            P(("reader", "blk"), None),
            P(("reader", "blk"), None),
            P(),
            P(),
            P(),
            P("reader", "blk", None, None),
            P("reader", "blk"),
            P(),
        ),
        out_specs=(P(("reader", "blk"), None), P(("reader", "blk"), None)),
        check_vma=False,
    )
```
